32 devices in a mesh: grp: 2 (over x), tp: 8 (over z, y), section: 2 (over core).
Axes of the slice: x: 2, y: 2, z: 4, core: 2. Of those that a mesh axis runs over, the one named last changes fastest.
Arguments:
- hidden_in: bfloat16 [128, 4096], P(('grp', 'section')), parts along dimension 0, may hold values from -6 to 6
- temporal_gain: float32 [4096], replicated, may hold values from 0.5 to 1.5
- temporal_qkv: bfloat16 [3, 4096, 4096], P(None, None, 'tp'), may hold values from -0.09375 to 0.09375
- temporal_out_weight: bfloat16 [4096, 4096], P('tp'), may hold values from -0.125 to 0.125
- cache_keys: bfloat16 [128, 64, 4096], P(('grp', 'section'), None, 'tp'), parts along dimension 0, may hold values from -240 to 240
- cache_values: bfloat16 [128, 64, 4096], P(('grp', 'section'), None, 'tp'), parts along dimension 0, may hold values from -6 to 6
- lengths: int32 [128], P(('grp', 'section')), parts along dimension 0, may hold values from 1 to 64, as said below
- depth_in: bfloat16 [8, 4096, 1024], P('section', 'tp'), may hold values from -0.09375 to 0.09375
- depth_embed: bfloat16 [8, 2048, 1024], P('section', 'tp'), may hold values from -6 to 6
- depth_gain: float32 [1024], replicated, may hold values from 0.5 to 1.5
- depth_qkv: bfloat16 [8, 3, 1024, 1024], P('section', None, None, 'tp'), may hold values from -0.1875 to 0.1875
- depth_out_weight: bfloat16 [8, 1024, 1024], P('section', 'tp'), may hold values from -0.1875 to 0.1875
- head_gain: float32 [1024], replicated, may hold values from 0.5 to 1.5
- head_weight: bfloat16 [8, 1024, 2048], P('section', 'tp'), may hold values from -0.25 to 0.25
- tokens: int32 [128, 8], P('grp', 'section'), parts along dimension 0, may hold values from 0 to 2047
Outputs:
- temporal_out: bfloat16 [128, 4096], P(('grp', 'section'), 'tp'), parts along dimension 0
- logits: float32 [128, 8, 2048], P('grp', 'section', 'tp'), parts along dimension 0
The draws below stay inside these ranges and needn't reach their ends.
There are 2 independent parts, one for each index of `grp`. The reference program is written for one: setup_inputs(seed, part) draws one part's arguments, and reference() takes and returns one part's arrays. A program takes and returns all parts, laid end to end along the dimension named above; an argument that names none is the same for every part. Nothing has to cross between parts.
Inputs may be any that keep to these rules, and one draw needn't show every extreme that they name: Cached positions 0 to lengths - 1 of a stream are live and the new token stands at position lengths; some stream of every group holds 64 live positions.
All inputs are finite; a program needn't handle non-finite values.
Results may differ from the reference program's by a relative error of at most 0.009.
Values may be sent and summed in bfloat16 or wider, within the bound.
No kernel may reach another device: no remote copies, remote signals or barrier semaphores. Data moves between devices by JAX's collectives and lax.ppermute only.
A program may use at most 64 MiB of HBM per device.

```python
import math
import jax
import jax.numpy as jnp
from jax import lax

D = 4096
HEADS = 32
HEAD_DIM = 128
DEPTH_D = 1024
DEPTH_HEADS = 16
DEPTH_HDIM = 64
VOCAB = 2048
CODEBOOKS = 8
STREAMS = 64
CACHE = 64


def draw_cache_keys(key, part):
    sample = jnp.clip(jax.random.normal(key, (STREAMS, CACHE, D), jnp.float32), -6.0, 6.0)
    return sample.astype(jnp.bfloat16)


def draw_lengths(key, part):
    drawn = jax.random.randint(key, (STREAMS,), 1, CACHE + 1, dtype=jnp.int32)
    where_full = jax.random.randint(jax.random.fold_in(key, 5), (), 0, STREAMS, dtype=jnp.int32)
    return drawn.at[where_full].set(CACHE)


def plant(entries, own_key, low, largest):
    dims = entries.shape
    spot = [jax.random.randint(jax.random.fold_in(own_key, axis), (), 0, dims[axis]) for axis in range(len(dims))]
    entries = entries.at[tuple(spot)].set(low)
    longest = dims.index(max(dims))
    spot[longest] = (spot[longest] + 1) % dims[longest]
    return entries.at[tuple(spot)].set(largest)


def raised(entries, key, source, target, parts, factor):
    owner, partner = [(jnp.arange(entries.shape[dim]) // (entries.shape[dim] // parts)).reshape([-1 if axis == dim else 1 for axis in range(entries.ndim)]) for dim in (source, target)]
    chosen = jax.random.permutation(key, parts)[partner]
    strong = (owner == chosen) | (owner == (partner + parts // 2) % parts)
    return jnp.where(strong, factor * entries, entries)


def steps_of(stream_key, shape, split, low, high):
    factor_of = 1.0
    for axis_at, blocks in split:
        heights = jax.random.uniform(jax.random.fold_in(jax.random.fold_in(stream_key, 6), axis_at), (blocks,), jnp.float32, low / len(split), high / len(split))
        factor_of = factor_of * jnp.repeat(jnp.exp(heights), shape[axis_at] // blocks).reshape((-1,) + (1,) * (len(shape) - 1 - axis_at))
    return factor_of


def normal_values(key, extent, scale, most, split=(), held_as=jnp.bfloat16):
    result = scale * jax.random.normal(key, extent, jnp.float32)
    if split:
        result = result * steps_of(key, extent, split, -0.22, 0.18)
    return jnp.clip(result, -most, most).astype(held_as)


def bell_draw_with(own_key, dims, width, reach, split, heavy, kind=jnp.bfloat16):
    result = width * jax.random.normal(own_key, dims, jnp.float32)
    if split:
        result = result * steps_of(own_key, dims, split, -0.22, 0.18)
    return jnp.clip(raised(result, jax.random.fold_in(own_key, 3), *heavy), -reach, reach).astype(kind)


def setup_inputs(seed: int = 0, part: int = 0) -> dict:
    streams_of = jax.random.split(jax.random.key(seed), 16)
    part_keys = jax.random.split(jax.random.fold_in(streams_of[15], part), 16)
    return {
        "hidden_in": normal_values(part_keys[0], (STREAMS, D), 1.0, 6.0, ((0, 2),)),
        "temporal_gain": jnp.clip(1.0 + 0.1 * jax.random.normal(streams_of[1], (D,), jnp.float32), 0.5, 1.5),
        "temporal_qkv": normal_values(streams_of[2], (3, D, D), D ** -0.5, 0.09375, ((2, 8),)),
        "temporal_out_weight": bell_draw_with(streams_of[3], (D, D), D ** -0.5, 0.125, ((0, 8),), (0, 1, 8, 2.0)),
        "cache_keys": draw_cache_keys(jax.random.fold_in(jax.random.fold_in(streams_of[15], part), 71), part),
        "cache_values": normal_values(part_keys[5], (STREAMS, CACHE, D), 1.0, 6.0, ((0, 2), (2, 8))),
        "lengths": draw_lengths(jax.random.fold_in(jax.random.fold_in(streams_of[15], part), 71), part),
        "depth_in": normal_values(streams_of[7], (CODEBOOKS, D, DEPTH_D), D ** -0.5, 0.09375, ((0, 2), (1, 8))),
        "depth_embed": normal_values(streams_of[8], (CODEBOOKS, VOCAB, DEPTH_D), 1.0, 6.0, ((0, 2), (1, 8))),
        "depth_gain": jnp.clip(1.0 + 0.1 * jax.random.normal(streams_of[9], (DEPTH_D,), jnp.float32), 0.5, 1.5),
        "depth_qkv": normal_values(streams_of[10], (CODEBOOKS, 3, DEPTH_D, DEPTH_D), DEPTH_D ** -0.5, 0.1875, ((0, 2), (3, 8))),
        "depth_out_weight": normal_values(streams_of[11], (CODEBOOKS, DEPTH_D, DEPTH_D), DEPTH_D ** -0.5, 0.1875, ((0, 2), (1, 8))),
        "head_gain": jnp.clip(1.0 + 0.1 * jax.random.normal(streams_of[12], (DEPTH_D,), jnp.float32), 0.5, 1.5),
        "head_weight": bell_draw_with(streams_of[13], (CODEBOOKS, DEPTH_D, VOCAB), DEPTH_D ** -0.5, 0.25, ((0, 2), (1, 8)), (1, 2, 8, 2.0)),
        "tokens": plant(jax.random.randint(part_keys[14], (STREAMS, CODEBOOKS), 0, VOCAB), jax.random.fold_in(part_keys[14], 1), 0, VOCAB - 1).astype(jnp.int32),
    }


EPSILON = 1e-05

def rms_norm(values, scale):
    wide = values.astype(jnp.float32)
    return wide * lax.rsqrt(lax.optimization_barrier(jnp.mean(wide * wide, axis=-1, keepdims=True)) + EPSILON) * scale.astype(jnp.float32)

def rotate(vectors, positions):
    halfdim = vectors.shape[-1] // 2
    spacing = jnp.arange(halfdim, dtype=jnp.float32) / halfdim
    inverse = jnp.exp(-math.log(10000.0) * spacing)
    angles = positions.astype(jnp.float32)[:, None, None] * inverse[None, None, :]
    cosine = jnp.cos(angles)
    sine = jnp.sin(angles)
    first = vectors[..., :halfdim]
    second = vectors[..., halfdim:]
    return jnp.concatenate([first * cosine - second * sine, first * sine + second * cosine], axis=-1)

def reference(hidden_in, temporal_gain, temporal_qkv, temporal_out_weight, cache_keys, cache_values, lengths, depth_in, depth_embed, depth_gain, depth_qkv, depth_out_weight, head_gain, head_weight, tokens):
    streams = hidden_in.shape[0]
    normed = rms_norm(hidden_in, temporal_gain).astype(jnp.bfloat16)
    projected = [jnp.dot(normed, temporal_qkv[number], preferred_element_type=jnp.float32) for number in range(3)]
    layout = (streams, HEADS, HEAD_DIM)
    queries = rotate(projected[0].reshape(layout), lengths).astype(jnp.bfloat16)
    keys_new = rotate(projected[1].reshape(layout), lengths).astype(jnp.bfloat16)
    values_new = projected[2].reshape(layout).astype(jnp.bfloat16)
    cached_keys = cache_keys.reshape(streams, CACHE, HEADS, HEAD_DIM).astype(jnp.float32)
    cached_values = cache_values.reshape(streams, CACHE, HEADS, HEAD_DIM).astype(jnp.float32)
    factor = 1.0 / math.sqrt(HEAD_DIM)
    scores = jnp.einsum('shd,sphd->shp', queries.astype(jnp.float32), cached_keys) * factor
    own_score = lax.optimization_barrier(jnp.sum(queries.astype(jnp.float32) * keys_new.astype(jnp.float32), axis=-1)) * factor
    valid = jnp.arange(CACHE, dtype=jnp.int32)[None, None, :] < lengths[:, None, None]
    scores = jnp.where(valid, scores, -jnp.inf)
    highest = jnp.maximum(lax.optimization_barrier(jnp.max(scores, axis=-1)), own_score)
    expo = jnp.exp(scores - highest[..., None])
    own_expo = jnp.exp(own_score - highest)
    totals = lax.optimization_barrier(jnp.sum(expo, axis=-1)) + own_expo
    weights = (expo / totals[..., None]).astype(jnp.bfloat16)
    own_weight = (own_expo / totals).astype(jnp.bfloat16)
    mixed = jnp.einsum('shp,sphd->shd', weights.astype(jnp.float32), cached_values)
    mixed = mixed + own_weight.astype(jnp.float32)[..., None] * values_new.astype(jnp.float32)
    mixed = mixed.astype(jnp.bfloat16).reshape(streams, D)
    temporal = (hidden_in.astype(jnp.float32) + jnp.dot(mixed, temporal_out_weight, preferred_element_type=jnp.float32)).astype(jnp.bfloat16)
    codes = depth_in.shape[0]
    entry = jnp.einsum('sd,cde->sce', temporal.astype(jnp.float32), depth_in.astype(jnp.float32))
    embedded = depth_embed[jnp.arange(codes, dtype=jnp.int32)[None, :], tokens]
    entry = entry + embedded.astype(jnp.float32)
    depth_normed = rms_norm(entry, depth_gain).astype(jnp.bfloat16)
    dproj = [jnp.einsum('sce,cef->scf', depth_normed.astype(jnp.float32), depth_qkv[:, number].astype(jnp.float32)).astype(jnp.bfloat16) for number in range(3)]
    shaped = [item.reshape(streams, codes, DEPTH_HEADS, DEPTH_HDIM).astype(jnp.float32) for item in dproj]
    depth_scores = jnp.einsum('sqhd,skhd->shqk', shaped[0], shaped[1]) * (1.0 / math.sqrt(DEPTH_HDIM))
    causal = jnp.arange(codes)[None, :] <= jnp.arange(codes)[:, None]
    depth_scores = jnp.where(causal[None, None], depth_scores, -jnp.inf)
    depth_top = lax.optimization_barrier(jnp.max(depth_scores, axis=-1, keepdims=True))
    depth_expo = jnp.exp(depth_scores - depth_top)
    depth_weights = (depth_expo / lax.optimization_barrier(jnp.sum(depth_expo, axis=-1, keepdims=True))).astype(jnp.bfloat16)
    depth_mixed = jnp.einsum('shqk,skhd->sqhd', depth_weights.astype(jnp.float32), shaped[2]).astype(jnp.bfloat16)
    depth_mixed = depth_mixed.reshape(streams, codes, DEPTH_D)
    resid = entry + jnp.einsum('scf,cfe->sce', depth_mixed.astype(jnp.float32), depth_out_weight.astype(jnp.float32))
    head_normed = rms_norm(resid, head_gain).astype(jnp.bfloat16)
    logits = jnp.einsum('sce,cev->scv', head_normed.astype(jnp.float32), head_weight.astype(jnp.float32))
    return (temporal, logits)
```

```python
import math

import jax
import jax.numpy as jnp
from jax import lax
from jax.sharding import PartitionSpec as P

HEAD_DIM = 128
DEPTH_HDIM = 64


EPSILON = 1e-05


def passed_along(block, axis, distance):
    devices = range(lax.axis_size(axis))
    route = [(i - distance, i) for i in devices if i - distance in devices]
    return lax.ppermute(block, axis, route)


def from_partner(shard, axis, distance):
    return lax.ppermute(shard, axis, [(i, i ^ 1 << distance) for i in range(lax.axis_size(axis))])


def rms_norm(values, scale):
    wide = values.astype(jnp.float32)
    return wide * lax.rsqrt(jnp.mean(wide * wide, axis=-1, keepdims=True) + EPSILON) * scale


def rotate(vectors, positions):
    halfdim = vectors.shape[-1] // 2
    spacing = jnp.arange(halfdim, dtype=jnp.float32) / halfdim
    inverse = jnp.exp(-math.log(10000.0) * spacing)
    angles = positions.astype(jnp.float32)[:, None, None] * inverse[None, None, :]
    cosine = jnp.cos(angles)
    sine = jnp.sin(angles)
    first = vectors[..., :halfdim]
    second = vectors[..., halfdim:]
    return jnp.concatenate(
        [first * cosine - second * sine, first * sine + second * cosine], axis=-1
    )


def scattered_sum(parts):
    moved = lax.all_to_all(parts.astype(jnp.bfloat16), "tp", 0, 0)
    return jnp.sum(moved.astype(jnp.float32), axis=0)


def gathered(block):
    size = lax.axis_size("tp")
    return lax.all_to_all(jnp.broadcast_to(block[None], (size,) + block.shape), "tp", 0, 0)


def per_device(
    hidden_in,
    temporal_gain,
    temporal_qkv,
    temporal_out_weight,
    cache_keys,
    cache_values,
    lengths,
    depth_in,
    depth_embed,
    depth_gain,
    depth_qkv,
    depth_out_weight,
    head_gain,
    head_weight,
    tokens,
):
    tp = lax.axis_size("tp")
    local_streams = hidden_in.shape[0]
    local_cols = temporal_qkv.shape[2]
    local_heads = local_cols // HEAD_DIM
    cache_len = cache_keys.shape[1]
    normed = rms_norm(hidden_in, temporal_gain).astype(jnp.bfloat16)
    projected = jnp.einsum("sd,tdf->tsf", normed, temporal_qkv, preferred_element_type=jnp.float32)
    layout = (local_streams, local_heads, HEAD_DIM)
    queries = rotate(projected[0].reshape(layout), lengths).astype(jnp.bfloat16)
    keys_new = rotate(projected[1].reshape(layout), lengths).astype(jnp.bfloat16)
    values_new = projected[2].reshape(layout).astype(jnp.bfloat16)
    cached_keys = cache_keys.reshape(local_streams, cache_len, local_heads, HEAD_DIM)
    cached_values = cache_values.reshape(local_streams, cache_len, local_heads, HEAD_DIM)
    factor = 1.0 / math.sqrt(HEAD_DIM)
    scores = (
        jnp.einsum("shd,sphd->shp", queries, cached_keys, preferred_element_type=jnp.float32)
        * factor
    )
    own_score = (
        jnp.sum(queries.astype(jnp.float32) * keys_new.astype(jnp.float32), axis=-1) * factor
    )
    valid = jnp.arange(cache_len, dtype=jnp.int32)[None, None, :] < lengths[:, None, None]
    scores = jnp.where(valid, scores, -jnp.inf)
    highest = jnp.maximum(jnp.max(scores, axis=-1), own_score)
    expo = jnp.exp(scores - highest[..., None])
    own_expo = jnp.exp(own_score - highest)
    totals = jnp.sum(expo, axis=-1) + own_expo
    weights = (expo / totals[..., None]).astype(jnp.bfloat16)
    own_weight = (own_expo / totals).astype(jnp.bfloat16)
    mixed = jnp.einsum("shp,sphd->shd", weights, cached_values, preferred_element_type=jnp.float32)
    mixed = mixed + own_weight.astype(jnp.float32)[..., None] * values_new.astype(jnp.float32)
    mixed = mixed.astype(jnp.bfloat16).reshape(local_streams, local_cols)
    partial_rows = jnp.dot(mixed, temporal_out_weight, preferred_element_type=jnp.float32)
    slice_width = partial_rows.shape[1] // tp
    by_slice = partial_rows.reshape(local_streams, tp, slice_width).transpose(1, 0, 2)
    summed = scattered_sum(by_slice)
    tp_place = lax.axis_index("tp")
    resid_in = lax.dynamic_slice_in_dim(hidden_in, tp_place * slice_width, slice_width, 1)
    temporal = (resid_in.astype(jnp.float32) + summed).astype(jnp.bfloat16)
    all_rows = lax.all_gather(temporal, "section", axis=0, tiled=True)
    streams = all_rows.shape[0]
    codes = depth_in.shape[0]
    width = depth_in.shape[2]
    vocab_local = depth_embed.shape[1]
    first_id = tp_place * vocab_local
    onehot = (
        tokens[:, :, None] == first_id + jnp.arange(vocab_local, dtype=jnp.int32)[None, None, :]
    ).astype(jnp.bfloat16)
    embedded = jnp.einsum("scv,cve->cse", onehot, depth_embed, preferred_element_type=jnp.float32)
    entry_terms = embedded + jnp.einsum(
        "sd,cde->cse", all_rows, depth_in, preferred_element_type=jnp.float32
    )
    hidden_rows = head_weight.shape[1]
    hidden_start = tp_place * hidden_rows
    entry = scattered_sum(entry_terms.reshape(codes, streams, tp, hidden_rows).transpose(2, 0, 1, 3))
    own_gain = lax.dynamic_slice_in_dim(depth_gain, hidden_start, hidden_rows, 0)
    scaled = (entry * own_gain).astype(jnp.bfloat16)
    rows = gathered(scaled)
    plain = rows.astype(jnp.float32) / depth_gain.reshape(tp, 1, 1, hidden_rows)
    inv_rms = lax.rsqrt(jnp.sum(plain * plain, axis=(0, 3)) / width + EPSILON)
    dproj = jnp.einsum(
        "tcse,cntef->ncsf",
        rows,
        depth_qkv.reshape(codes, 3, tp, hidden_rows, -1),
        preferred_element_type=jnp.float32,
    )
    dproj = (dproj * inv_rms[None, :, :, None]).astype(jnp.bfloat16)
    prior = passed_along(dproj[1:], "section", 1)
    depth_cols = dproj.shape[3]
    head_part = min(depth_cols, DEPTH_HDIM)
    local_parts = depth_cols // head_part
    sharers = DEPTH_HDIM // head_part
    both = jnp.concatenate([prior, dproj[1:]], axis=1)
    all_keys = both[0].reshape(2 * codes, streams, local_parts, head_part)
    all_values = both[1].reshape(2 * codes, streams, local_parts, head_part)
    depth_queries = dproj[0].reshape(codes, streams, local_parts, head_part)
    depth_scores = jnp.sum(
        depth_queries[:, None].astype(jnp.float32) * all_keys[None].astype(jnp.float32), axis=-1
    )
    for level in range(sharers.bit_length() - 1):
        depth_scores = depth_scores + from_partner(depth_scores, "tp", level)
    depth_scores = depth_scores * (1.0 / math.sqrt(DEPTH_HDIM))
    section_place = lax.axis_index("section")
    query_pos = jnp.arange(codes, dtype=jnp.int32)[:, None]
    key_pos = jnp.arange(2 * codes, dtype=jnp.int32)[None, :]
    allowed = jnp.where(key_pos < codes, section_place > 0, key_pos - codes <= query_pos)
    depth_scores = jnp.where(allowed[:, :, None, None], depth_scores, -jnp.inf)
    depth_top = jnp.max(depth_scores, axis=1, keepdims=True)
    depth_expo = jnp.exp(depth_scores - depth_top)
    depth_weights = (depth_expo / jnp.sum(depth_expo, axis=1, keepdims=True)).astype(jnp.bfloat16)
    depth_mixed = jnp.sum(
        depth_weights[..., None].astype(jnp.float32) * all_values[None].astype(jnp.float32), axis=1
    ).astype(jnp.bfloat16)
    depth_mixed = depth_mixed.reshape(codes, streams, depth_cols)
    depth_terms = jnp.einsum(
        "csf,cfe->cse", depth_mixed, depth_out_weight, preferred_element_type=jnp.float32
    )
    added = scattered_sum(depth_terms.reshape(codes, streams, tp, hidden_rows).transpose(2, 0, 1, 3))
    resid = entry + added
    own_head_gain = lax.dynamic_slice_in_dim(head_gain, hidden_start, hidden_rows, 0)
    own_hidden = (resid * own_head_gain).astype(jnp.bfloat16)
    squares = jnp.sum(resid * resid, axis=2)
    high = squares.astype(jnp.bfloat16)
    low = (squares - high.astype(jnp.float32)).astype(jnp.bfloat16)
    partial_logits = jnp.einsum(
        "cse,cev->csv", own_hidden, head_weight, preferred_element_type=jnp.float32
    )
    vocab_slice = partial_logits.shape[2] // tp
    outgoing = partial_logits.reshape(codes, streams, tp, vocab_slice).transpose(2, 0, 1, 3)
    outgoing = outgoing.astype(jnp.bfloat16).reshape(tp, codes * streams, vocab_slice)
    extra = jnp.stack([high.reshape(-1), low.reshape(-1)])
    extra = jnp.pad(extra, ((0, 14), (0, 0))).reshape(-1, vocab_slice)
    packed = jnp.concatenate(
        [outgoing, jnp.broadcast_to(extra[None], (tp,) + extra.shape)], axis=1
    )
    moved = lax.all_to_all(packed, "tp", 0, 0).astype(jnp.float32)
    rows_total = jnp.sum(moved, axis=0)
    stats = rows_total[codes * streams :].reshape(16, codes, streams)
    head_inv = lax.rsqrt((stats[0] + stats[1]) / width + EPSILON)
    logits = rows_total[: codes * streams].reshape(codes, streams, vocab_slice) * head_inv[..., None]
    return (temporal, logits.transpose(1, 0, 2))


def solution(mesh):
    return jax.shard_map(
        per_device,
        mesh=mesh,
        in_specs=(
            P(("grp", "section"), None),
            P(),
            P(None, None, "tp"),
            P("tp", None),
            P(("grp", "section"), None, "tp"),
            P(("grp", "section"), None, "tp"),
            P(("grp", "section")),
            P("section", "tp", None),
            P("section", "tp", None),
            P(),
            P("section", None, None, "tp"),
            P("section", "tp", None),
            P(),
            P("section", "tp", None),
            P("grp", "section"),
        ),
        out_specs=(P(("grp", "section"), "tp"), P("grp", "section", "tp")),
        check_vma=False,
    )
```

```python
import functools
import math

import jax
import jax.numpy as jnp
from jax import lax
from jax.experimental import pallas as pl
from jax.experimental.pallas import tpu as pltpu
from jax.sharding import PartitionSpec as P

HEAD_DIM = 128
DEPTH_HDIM = 64


EPSILON = 1e-05


def passed_along(block, axis, distance):
    devices = range(lax.axis_size(axis))
    route = [(i - distance, i) for i in devices if i - distance in devices]
    return lax.ppermute(block, axis, route)


def from_partner(shard, axis, distance):
    return lax.ppermute(shard, axis, [(i, i ^ 1 << distance) for i in range(lax.axis_size(axis))])


def rms_norm(values, scale):
    wide = values.astype(jnp.float32)
    return wide * lax.rsqrt(jnp.mean(wide * wide, axis=-1, keepdims=True) + EPSILON) * scale


def rotate(vectors, positions):
    halfdim = vectors.shape[-1] // 2
    spacing = jnp.arange(halfdim, dtype=jnp.float32) / halfdim
    inverse = jnp.exp(-math.log(10000.0) * spacing)
    angles = positions.astype(jnp.float32)[:, None, None] * inverse[None, None, :]
    cosine = jnp.cos(angles)
    sine = jnp.sin(angles)
    first = vectors[..., :halfdim]
    second = vectors[..., halfdim:]
    return jnp.concatenate(
        [first * cosine - second * sine, first * sine + second * cosine], axis=-1
    )


def scattered_sum(parts):
    moved = lax.all_to_all(parts.astype(jnp.bfloat16), "tp", 0, 0)
    return jnp.sum(moved.astype(jnp.float32), axis=0)


def gathered(block):
    size = lax.axis_size("tp")
    return lax.all_to_all(jnp.broadcast_to(block[None], (size,) + block.shape), "tp", 0, 0)


def general_device(
    hidden_in,
    temporal_gain,
    temporal_qkv,
    temporal_out_weight,
    cache_keys,
    cache_values,
    lengths,
    depth_in,
    depth_embed,
    depth_gain,
    depth_qkv,
    depth_out_weight,
    head_gain,
    head_weight,
    tokens,
):
    tp = lax.axis_size("tp")
    local_streams = hidden_in.shape[0]
    local_cols = temporal_qkv.shape[2]
    local_heads = local_cols // HEAD_DIM
    cache_len = cache_keys.shape[1]
    normed = rms_norm(hidden_in, temporal_gain).astype(jnp.bfloat16)
    projected = jnp.einsum("sd,tdf->tsf", normed, temporal_qkv, preferred_element_type=jnp.float32)
    layout = (local_streams, local_heads, HEAD_DIM)
    queries = rotate(projected[0].reshape(layout), lengths).astype(jnp.bfloat16)
    keys_new = rotate(projected[1].reshape(layout), lengths).astype(jnp.bfloat16)
    values_new = projected[2].reshape(layout).astype(jnp.bfloat16)
    cached_keys = cache_keys.reshape(local_streams, cache_len, local_heads, HEAD_DIM)
    cached_values = cache_values.reshape(local_streams, cache_len, local_heads, HEAD_DIM)
    factor = 1.0 / math.sqrt(HEAD_DIM)
    scores = (
        jnp.einsum("shd,sphd->shp", queries, cached_keys, preferred_element_type=jnp.float32)
        * factor
    )
    own_score = (
        jnp.sum(queries.astype(jnp.float32) * keys_new.astype(jnp.float32), axis=-1) * factor
    )
    valid = jnp.arange(cache_len, dtype=jnp.int32)[None, None, :] < lengths[:, None, None]
    scores = jnp.where(valid, scores, -jnp.inf)
    highest = jnp.maximum(jnp.max(scores, axis=-1), own_score)
    expo = jnp.exp(scores - highest[..., None])
    own_expo = jnp.exp(own_score - highest)
    totals = jnp.sum(expo, axis=-1) + own_expo
    weights = (expo / totals[..., None]).astype(jnp.bfloat16)
    own_weight = (own_expo / totals).astype(jnp.bfloat16)
    mixed = jnp.einsum("shp,sphd->shd", weights, cached_values, preferred_element_type=jnp.float32)
    mixed = mixed + own_weight.astype(jnp.float32)[..., None] * values_new.astype(jnp.float32)
    mixed = mixed.astype(jnp.bfloat16).reshape(local_streams, local_cols)
    partial_rows = jnp.dot(mixed, temporal_out_weight, preferred_element_type=jnp.float32)
    slice_width = partial_rows.shape[1] // tp
    by_slice = partial_rows.reshape(local_streams, tp, slice_width).transpose(1, 0, 2)
    summed = scattered_sum(by_slice)
    tp_place = lax.axis_index("tp")
    resid_in = lax.dynamic_slice_in_dim(hidden_in, tp_place * slice_width, slice_width, 1)
    temporal = (resid_in.astype(jnp.float32) + summed).astype(jnp.bfloat16)
    all_rows = lax.all_gather(temporal, "section", axis=0, tiled=True)
    streams = all_rows.shape[0]
    codes = depth_in.shape[0]
    width = depth_in.shape[2]
    vocab_local = depth_embed.shape[1]
    first_id = tp_place * vocab_local
    onehot = (
        tokens[:, :, None] == first_id + jnp.arange(vocab_local, dtype=jnp.int32)[None, None, :]
    ).astype(jnp.bfloat16)
    embedded = jnp.einsum("scv,cve->cse", onehot, depth_embed, preferred_element_type=jnp.float32)
    entry_terms = embedded + jnp.einsum(
        "sd,cde->cse", all_rows, depth_in, preferred_element_type=jnp.float32
    )
    hidden_rows = head_weight.shape[1]
    hidden_start = tp_place * hidden_rows
    entry = scattered_sum(entry_terms.reshape(codes, streams, tp, hidden_rows).transpose(2, 0, 1, 3))
    own_gain = lax.dynamic_slice_in_dim(depth_gain, hidden_start, hidden_rows, 0)
    scaled = (entry * own_gain).astype(jnp.bfloat16)
    rows = gathered(scaled)
    plain = rows.astype(jnp.float32) / depth_gain.reshape(tp, 1, 1, hidden_rows)
    inv_rms = lax.rsqrt(jnp.sum(plain * plain, axis=(0, 3)) / width + EPSILON)
    dproj = jnp.einsum(
        "tcse,cntef->ncsf",
        rows,
        depth_qkv.reshape(codes, 3, tp, hidden_rows, -1),
        preferred_element_type=jnp.float32,
    )
    dproj = (dproj * inv_rms[None, :, :, None]).astype(jnp.bfloat16)
    prior = passed_along(dproj[1:], "section", 1)
    depth_cols = dproj.shape[3]
    head_part = min(depth_cols, DEPTH_HDIM)
    local_parts = depth_cols // head_part
    sharers = DEPTH_HDIM // head_part
    both = jnp.concatenate([prior, dproj[1:]], axis=1)
    all_keys = both[0].reshape(2 * codes, streams, local_parts, head_part)
    all_values = both[1].reshape(2 * codes, streams, local_parts, head_part)
    depth_queries = dproj[0].reshape(codes, streams, local_parts, head_part)
    depth_scores = jnp.sum(
        depth_queries[:, None].astype(jnp.float32) * all_keys[None].astype(jnp.float32), axis=-1
    )
    for level in range(sharers.bit_length() - 1):
        depth_scores = depth_scores + from_partner(depth_scores, "tp", level)
    depth_scores = depth_scores * (1.0 / math.sqrt(DEPTH_HDIM))
    section_place = lax.axis_index("section")
    query_pos = jnp.arange(codes, dtype=jnp.int32)[:, None]
    key_pos = jnp.arange(2 * codes, dtype=jnp.int32)[None, :]
    allowed = jnp.where(key_pos < codes, section_place > 0, key_pos - codes <= query_pos)
    depth_scores = jnp.where(allowed[:, :, None, None], depth_scores, -jnp.inf)
    depth_top = jnp.max(depth_scores, axis=1, keepdims=True)
    depth_expo = jnp.exp(depth_scores - depth_top)
    depth_weights = (depth_expo / jnp.sum(depth_expo, axis=1, keepdims=True)).astype(jnp.bfloat16)
    depth_mixed = jnp.sum(
        depth_weights[..., None].astype(jnp.float32) * all_values[None].astype(jnp.float32), axis=1
    ).astype(jnp.bfloat16)
    depth_mixed = depth_mixed.reshape(codes, streams, depth_cols)
    depth_terms = jnp.einsum(
        "csf,cfe->cse", depth_mixed, depth_out_weight, preferred_element_type=jnp.float32
    )
    added = scattered_sum(depth_terms.reshape(codes, streams, tp, hidden_rows).transpose(2, 0, 1, 3))
    resid = entry + added
    own_head_gain = lax.dynamic_slice_in_dim(head_gain, hidden_start, hidden_rows, 0)
    own_hidden = (resid * own_head_gain).astype(jnp.bfloat16)
    squares = jnp.sum(resid * resid, axis=2)
    high = squares.astype(jnp.bfloat16)
    low = (squares - high.astype(jnp.float32)).astype(jnp.bfloat16)
    partial_logits = jnp.einsum(
        "cse,cev->csv", own_hidden, head_weight, preferred_element_type=jnp.float32
    )
    vocab_slice = partial_logits.shape[2] // tp
    outgoing = partial_logits.reshape(codes, streams, tp, vocab_slice).transpose(2, 0, 1, 3)
    outgoing = outgoing.astype(jnp.bfloat16).reshape(tp, codes * streams, vocab_slice)
    extra = jnp.stack([high.reshape(-1), low.reshape(-1)])
    extra = jnp.pad(extra, ((0, 14), (0, 0))).reshape(-1, vocab_slice)
    packed = jnp.concatenate(
        [outgoing, jnp.broadcast_to(extra[None], (tp,) + extra.shape)], axis=1
    )
    moved = lax.all_to_all(packed, "tp", 0, 0).astype(jnp.float32)
    rows_total = jnp.sum(moved, axis=0)
    stats = rows_total[codes * streams :].reshape(16, codes, streams)
    head_inv = lax.rsqrt((stats[0] + stats[1]) / width + EPSILON)
    logits = rows_total[: codes * streams].reshape(codes, streams, vocab_slice) * head_inv[..., None]
    return (temporal, logits.transpose(1, 0, 2))


HBM = pl.BlockSpec(memory_space=pltpu.HBM)
VMEM = pl.BlockSpec(memory_space=pltpu.VMEM)
SMEM = pl.BlockSpec(memory_space=pltpu.SMEM)


def params(mebibytes):
    return pltpu.CompilerParams(vmem_limit_bytes=mebibytes * 1024 * 1024)


def in_hbm(array):
    return pltpu.with_memory_space_constraint(array, pltpu.HBM)


def shape(dims, dtype):
    return jax.ShapeDtypeStruct(dims, dtype)


def product(left, right):
    return jnp.dot(left, right, preferred_element_type=jnp.float32)


def product_t(left, right):
    return lax.dot_general(left, right, (((1,), (1,)), ((), ())), preferred_element_type=jnp.float32)


def column_of(row):
    size = row.shape[1]
    first = lax.broadcasted_iota(jnp.int32, (size, size), 0)
    second = lax.broadcasted_iota(jnp.int32, (size, size), 1)
    return jnp.sum(jnp.where(first == second, row, 0.0), axis=1, keepdims=True)


def temporal_kernel(
    hidden_hbm, gain_hbm, lengths_ref, qkv_hbm, out_hbm, keys_hbm, values_hbm, parts_ref,
    hidden_buf, gain_buf, qkv_buf, out_buf, keys_buf, values_buf, small_sems, qkv_sems, out_sems, cache_sems,
):
    streams, depth = hidden_buf.shape
    cols = qkv_buf.shape[2]
    heads = cols // HEAD_DIM
    cache_len = keys_buf.shape[1]
    steps = qkv_sems.shape[1]
    chunk = depth // steps
    places = parts_ref.shape[0]
    width = parts_ref.shape[2]
    small = [
        pltpu.make_async_copy(hidden_hbm, hidden_buf, small_sems.at[0]),
        pltpu.make_async_copy(gain_hbm, gain_buf, small_sems.at[1]),
    ]
    weight = [
        [
            pltpu.make_async_copy(
                qkv_hbm.at[n, pl.ds(i * chunk, chunk)],
                qkv_buf.at[n, pl.ds(i * chunk, chunk)],
                qkv_sems.at[n, i],
            )
            for i in range(steps)
        ]
        for n in range(3)
    ]
    caches = [
        pltpu.make_async_copy(keys_hbm, keys_buf, cache_sems.at[0]),
        pltpu.make_async_copy(values_hbm, values_buf, cache_sems.at[1]),
    ]
    outs = [
        pltpu.make_async_copy(
            out_hbm.at[:, pl.ds(t * width, width)], out_buf.at[:, pl.ds(t * width, width)], out_sems.at[t]
        )
        for t in range(places)
    ]
    for copy in small + weight[0] + weight[1] + caches[:1] + weight[2] + caches[1:] + outs:
        copy.start()

    for copy in small:
        copy.wait()
    wide = hidden_buf[...].astype(jnp.float32)
    inv = lax.rsqrt(jnp.mean(wide * wide, axis=1, keepdims=True) + EPSILON)
    normed = (wide * inv * gain_buf[...]).astype(jnp.bfloat16)

    def projected(n):
        total = None
        for i in range(steps):
            weight[n][i].wait()
            part = product(normed[:, i * chunk : (i + 1) * chunk], qkv_buf[n, pl.ds(i * chunk, chunk), :])
            total = part if total is None else total + part
        return total

    lengths_row = lengths_ref[...].astype(jnp.float32)
    lengths_col = column_of(lengths_row)
    half = HEAD_DIM // 2
    lane = lax.broadcasted_iota(jnp.int32, (streams, HEAD_DIM), 1)
    spacing = (lane & (half - 1)).astype(jnp.float32) / half
    angles = lengths_col * jnp.exp(-math.log(10000.0) * spacing)
    cosine = jnp.cos(angles)
    sine = jnp.where(lane < half, -1.0, 1.0) * jnp.sin(angles)

    def rotated(block):
        pieces = []
        for h in range(heads):
            piece = block[:, h * HEAD_DIM : (h + 1) * HEAD_DIM]
            pieces.append(piece * cosine + pltpu.roll(piece, half, 1) * sine)
        return jnp.concatenate(pieces, axis=1)

    queries = rotated(projected(0))
    keys_new = rotated(projected(1)).astype(jnp.bfloat16)
    head_lane = lax.broadcasted_iota(jnp.int32, (streams, cols), 1) // HEAD_DIM
    spread = jnp.concatenate(
        [jnp.where(head_lane == h, queries, 0.0) for h in range(heads)], axis=0
    ).astype(jnp.bfloat16)
    pairs = heads * streams
    factor = 1.0 / math.sqrt(HEAD_DIM)
    pair = lax.broadcasted_iota(jnp.int32, (1, pairs), 1)
    pair_stream = pair % streams
    own = product_t(keys_new, spread) * factor
    stream_row = lax.broadcasted_iota(jnp.int32, (streams, pairs), 0)
    own_score = jnp.sum(jnp.where(stream_row == pair_stream, own, 0.0), axis=0, keepdims=True)
    tiled = jnp.sum(jnp.where(stream_row == pair_stream, lengths_col, 0.0), axis=0, keepdims=True)
    first_row = pair_stream * cache_len
    last_row = first_row + tiled.astype(jnp.int32)
    caches[0].wait()
    rows = streams * cache_len
    scores = product_t(keys_buf[...].reshape(rows, cols), spread) * factor
    row = lax.broadcasted_iota(jnp.int32, (rows, pairs), 0)
    scores = jnp.where((row >= first_row) & (row < last_row), scores, -jnp.inf)
    highest = jnp.maximum(jnp.max(scores, axis=0, keepdims=True), own_score)
    expo = jnp.exp(scores - highest)
    own_expo = jnp.exp(own_score - highest)
    inverse = 1.0 / (jnp.sum(expo, axis=0, keepdims=True) + own_expo)
    weights = (expo * inverse).astype(jnp.bfloat16)
    own_weight = (own_expo * inverse).astype(jnp.bfloat16).astype(jnp.float32)
    values_new = projected(2).astype(jnp.bfloat16).astype(jnp.float32)
    caches[1].wait()
    mixed_all = lax.dot_general(
        weights,
        values_buf[...].reshape(rows, cols),
        (((0,), (0,)), ((), ())),
        preferred_element_type=jnp.float32,
    )
    pair_lane = lax.broadcasted_iota(jnp.int32, (streams, pairs), 1)
    pair_row = lax.broadcasted_iota(jnp.int32, (streams, pairs), 0)
    mixed = []
    for h in range(heads):
        own_col = jnp.sum(
            jnp.where(pair_lane == pair_row + h * streams, own_weight, 0.0), axis=1, keepdims=True
        )
        lanes = slice(h * HEAD_DIM, (h + 1) * HEAD_DIM)
        mixed.append(
            mixed_all[h * streams : (h + 1) * streams, lanes] + own_col * values_new[:, lanes]
        )
    mixed = jnp.concatenate(mixed, axis=1).astype(jnp.bfloat16)
    for t in range(places):
        outs[t].wait()
        parts_ref[t] = product(mixed, out_buf[:, pl.ds(t * width, width)]).astype(jnp.bfloat16)


def temporal_parts(hidden_in, gain, lengths, qkv, out_weight, keys, values, places):
    streams, depth = hidden_in.shape
    cols = qkv.shape[2]
    steps = 4
    bf16 = jnp.bfloat16
    return pl.pallas_call(
        temporal_kernel,
        in_specs=[HBM, HBM, VMEM, HBM, HBM, HBM, HBM],
        out_specs=VMEM,
        out_shape=shape((places, streams, out_weight.shape[1] // places), bf16),
        scratch_shapes=[
            pltpu.VMEM(hidden_in.shape, bf16),
            pltpu.VMEM((1, depth), jnp.float32),
            pltpu.VMEM(qkv.shape, bf16),
            pltpu.VMEM(out_weight.shape, bf16),
            pltpu.VMEM(keys.shape, bf16),
            pltpu.VMEM(values.shape, bf16),
            pltpu.SemaphoreType.DMA((2,)),
            pltpu.SemaphoreType.DMA((3, steps)),
            pltpu.SemaphoreType.DMA((places,)),
            pltpu.SemaphoreType.DMA((2,)),
        ],
        compiler_params=params(30),
        name="temporal",
    )(
        in_hbm(hidden_in),
        in_hbm(gain.reshape(1, depth)),
        lengths.reshape(1, streams),
        in_hbm(qkv),
        in_hbm(out_weight),
        in_hbm(keys),
        in_hbm(values),
    )


def entry_kernel(rows_ref, tokens_ref, weight_hbm, embed_hbm, parts_ref, weight_buf, embed_buf, sems):
    codes, depth, width = weight_buf.shape
    vocab = embed_buf.shape[1]
    places = parts_ref.shape[0]
    part = width // places
    streams = rows_ref.shape[0]
    weight = [pltpu.make_async_copy(weight_hbm.at[c], weight_buf.at[c], sems.at[0, c]) for c in range(codes)]
    embed = [pltpu.make_async_copy(embed_hbm.at[c], embed_buf.at[c], sems.at[1, c]) for c in range(codes)]
    for c in range(codes):
        embed[c].start()
        weight[c].start()
    vocab_lane = lax.broadcasted_iota(jnp.int32, (streams, vocab), 1)
    for c in range(codes):
        hit = tokens_ref[:, c : c + 1] == vocab_lane
        onehot = jnp.where(hit, 1.0, 0.0).astype(jnp.bfloat16)
        embed[c].wait()
        total = product(onehot, embed_buf[c])
        weight[c].wait()
        total = (total + product(rows_ref[...], weight_buf[c])).astype(jnp.bfloat16)
        for t in range(places):
            parts_ref[t, c] = total[:, t * part : (t + 1) * part]


def entry_parts(rows, local_tokens, weight, embed, places):
    codes, depth, width = weight.shape
    streams = rows.shape[0]
    return pl.pallas_call(
        entry_kernel,
        in_specs=[VMEM, VMEM, HBM, HBM],
        out_specs=VMEM,
        out_shape=shape((places, codes, streams, width // places), jnp.bfloat16),
        scratch_shapes=[
            pltpu.VMEM(weight.shape, jnp.bfloat16),
            pltpu.VMEM(embed.shape, jnp.bfloat16),
            pltpu.SemaphoreType.DMA((2, codes)),
        ],
        compiler_params=params(24),
        name="entry",
    )(rows, local_tokens, weight, embed)


def qkv_kernel(rows_ref, gain_ref, weight_hbm, queries_ref, pair_ref, weight_buf, sems):
    codes, _, width, cols = weight_buf.shape
    places = rows_ref.shape[0]
    copies = [pltpu.make_async_copy(weight_hbm.at[c], weight_buf.at[c], sems.at[c]) for c in range(codes)]
    for copy in copies:
        copy.start()
    inverse_gain = 1.0 / gain_ref[...]
    for c in range(codes):
        row = jnp.concatenate([rows_ref[t, c] for t in range(places)], axis=1)
        plain = row.astype(jnp.float32) * inverse_gain
        inv = lax.rsqrt(jnp.sum(plain * plain, axis=1, keepdims=True) / width + EPSILON)
        copies[c].wait()
        for n in range(3):
            value = (product(row, weight_buf[c, n]) * inv).astype(jnp.bfloat16)
            if n == 0:
                queries_ref[c] = value
            else:
                pair_ref[n - 1, c] = value


def depth_projections(rows, gain, weight):
    codes, _, width, cols = weight.shape
    streams = rows.shape[2]
    bf16 = jnp.bfloat16
    return pl.pallas_call(
        qkv_kernel,
        in_specs=[VMEM, VMEM, HBM],
        out_specs=[VMEM, VMEM],
        out_shape=[shape((codes, streams, cols), bf16), shape((2, codes, streams, cols), bf16)],
        scratch_shapes=[pltpu.VMEM(weight.shape, bf16), pltpu.SemaphoreType.DMA((codes,))],
        compiler_params=params(16),
        name="depth_qkv",
    )(rows, gain.reshape(1, width), weight)


def mix_kernel(place_ref, queries_ref, own_ref, prior_ref, weight_hbm, kept_ref, *rest):
    sends, (total_buf, weight_buf, sems) = rest[:-3], rest[-3:]
    codes, streams, cols = queries_ref.shape
    span = kept_ref.shape[2]
    copy = pltpu.make_async_copy(weight_hbm, weight_buf, sems)
    copy.start()
    has_prior = place_ref[1] > 0
    first = lax.broadcasted_iota(jnp.int32, (2 * cols, cols), 0) % cols
    second = lax.broadcasted_iota(jnp.int32, (2 * cols, cols), 1)
    same = jnp.where(first // DEPTH_HDIM == second // DEPTH_HDIM, 1.0, 0.0).astype(jnp.bfloat16)
    keys = [prior_ref[0, j].astype(jnp.float32) for j in range(codes)]
    keys += [own_ref[0, j].astype(jnp.float32) for j in range(codes)]
    values = [prior_ref[1, j].astype(jnp.float32) for j in range(codes)]
    values += [own_ref[1, j].astype(jnp.float32) for j in range(codes)]
    factor = 1.0 / math.sqrt(DEPTH_HDIM)
    mixed = []
    for q in range(codes):
        query = queries_ref[q].astype(jnp.float32)
        reach = codes + q + 1
        pieces = []
        for j in range(reach):
            exact = query * keys[j]
            high = exact.astype(jnp.bfloat16)
            low = (exact - high.astype(jnp.float32)).astype(jnp.bfloat16)
            pieces.append(jnp.concatenate([high, low], axis=1))
        scores = product(jnp.concatenate(pieces, axis=0), same) * factor
        score = [scores[j * streams : (j + 1) * streams] for j in range(reach)]
        score = [jnp.where(has_prior, s, -jnp.inf) if j < codes else s for j, s in enumerate(score)]
        top = score[0]
        for s in score[1:]:
            top = jnp.maximum(top, s)
        expo = [jnp.exp(s - top) for s in score]
        inverse = 1.0 / sum(expo)
        total = jnp.zeros_like(query)
        for j in range(reach):
            total = total + (expo[j] * inverse).astype(jnp.bfloat16).astype(jnp.float32) * values[j]
        mixed.append(total.astype(jnp.bfloat16))
    copy.wait()
    for q in range(codes):
        total_buf[q] = product(mixed[q], weight_buf[q])
    place = place_ref[0] // 2
    for k in range(len(sends) + 1):
        start = pl.multiple_of((place ^ k) * span, span)
        block = total_buf[:, :, pl.ds(start, span)]
        if k == 0:
            kept_ref[...] = block
        else:
            sends[k - 1][...] = block.astype(jnp.bfloat16)


def mixed_parts(place, queries, own, prior, weight, far):
    codes, streams, cols = queries.shape
    width = weight.shape[2]
    block = (codes, streams, width // (far + 1))
    return pl.pallas_call(
        mix_kernel,
        in_specs=[SMEM, VMEM, VMEM, VMEM, HBM],
        out_specs=[VMEM] * (far + 1),
        out_shape=[shape(block, jnp.float32)] + [shape(block, jnp.bfloat16)] * far,
        scratch_shapes=[
            pltpu.VMEM((codes, streams, width), jnp.float32),
            pltpu.VMEM(weight.shape, jnp.bfloat16),
            pltpu.SemaphoreType.DMA(()),
        ],
        compiler_params=params(16),
        name="depth_mix",
    )(place, queries, own, prior, weight)


def pair_sum_kernel(place_ref, entry_ref, kept_ref, *rest):
    arrived, (total_ref, sent_ref) = rest[:-2], rest[-2:]
    total = kept_ref[...]
    for block in arrived:
        total = total + block[...].astype(jnp.float32)
    entry = entry_ref[...]
    none = jnp.zeros_like(entry)
    odd = place_ref[0] % 2 == 1
    total = total + jnp.concatenate([jnp.where(odd, none, entry), jnp.where(odd, entry, none)], axis=2)
    total_ref[...] = total
    sent_ref[...] = total.astype(jnp.bfloat16)


def pair_sums(place, entry, kept, arrived):
    return pl.pallas_call(
        pair_sum_kernel,
        in_specs=[SMEM] + [VMEM] * (2 + len(arrived)),
        out_specs=[VMEM, VMEM],
        out_shape=[shape(kept.shape, jnp.float32), shape(kept.shape, jnp.bfloat16)],
        compiler_params=params(16),
        name="pair_sum",
    )(place, entry, kept, *arrived)


def swap_kernel(place_ref, weight_hbm, *rest):
    halves, sems = rest[:-1], rest[-1]
    count, codes, _, part = halves[0].shape
    other = 1 - place_ref[0] % 2
    copies = [
        pltpu.make_async_copy(
            weight_hbm.at[pl.ds(n * codes, codes), :, pl.ds(pl.multiple_of((2 * k + other) * part, part), part)],
            half.at[k],
            sems.at[n, k],
        )
        for n, half in enumerate(halves)
        for k in range(count)
    ]
    for copy in copies:
        copy.start()
    for copy in copies:
        copy.wait()


def partner_columns(place, weight, places):
    codes, depth, vocab = weight.shape
    half = shape((places // 2, codes // 2, depth, vocab // places), jnp.bfloat16)
    return pl.pallas_call(
        swap_kernel,
        in_specs=[SMEM, HBM],
        out_specs=[VMEM, VMEM],
        out_shape=[half, half],
        scratch_shapes=[pltpu.SemaphoreType.DMA((2, places // 2))],
        name="partner_columns",
    )(place, in_hbm(weight))


STAT_ROWS = 16


def head_kernel(place_ref, gain_ref, total_ref, arrived_ref, own_hbm, early_ref, late_ref, kept_ref, stat_ref, *rest):
    sends, (weight_buf, sems) = rest[:-2], rest[-2:]
    codes, streams, span = total_ref.shape
    count, _, depth, part = weight_buf.shape
    odd = place_ref[0] % 2
    place = place_ref[0] // 2
    copies = [
        pltpu.make_async_copy(
            own_hbm.at[:, :, pl.ds(pl.multiple_of((2 * (place ^ k) + odd) * part, part), part)],
            weight_buf.at[k],
            sems.at[k],
        )
        for k in range(count)
    ]
    for copy in copies:
        copy.start()
    resid = total_ref[...] + arrived_ref[...].astype(jnp.float32)
    flat = resid.reshape(codes * streams, span)
    squares = flat * flat
    stat = product_t(jnp.ones((STAT_ROWS // 2, span), jnp.float32), squares)[:1]
    stat_ref[...] = stat
    high = stat.astype(jnp.bfloat16).astype(jnp.float32)
    stat_row = lax.broadcasted_iota(jnp.int32, (STAT_ROWS, codes * streams), 0)
    stat_block = jnp.where(stat_row == 0, high, jnp.where(stat_row == 1, stat - high, 0.0))
    stat_block = stat_block.astype(jnp.bfloat16)
    scaled = resid * gain_ref[...]
    low_half, high_half = scaled[:, :, :depth], scaled[:, :, depth:]
    ordered = jnp.concatenate(
        [jnp.where(odd == 1, high_half, low_half), jnp.where(odd == 1, low_half, high_half)], axis=2
    ).astype(jnp.bfloat16)
    rows = codes * streams
    for k in range(count):
        copies[k].wait()
        blocks = []
        for c in range(codes):
            partner = early_ref[place ^ k, c] if c < codes // 2 else late_ref[place ^ k, c - codes // 2]
            blocks.append(product(ordered[c], jnp.concatenate([weight_buf[k, c], partner], axis=0)))
        block = jnp.concatenate(blocks, axis=0)
        if k == 0:
            kept_ref[...] = block
        else:
            sends[k - 1][pl.ds(0, rows), :] = block.astype(jnp.bfloat16)
            sends[k - 1][pl.ds(rows, STAT_ROWS), :] = stat_block


def head_parts(place, gain, total, arrived, weight, early, late):
    codes, streams, span = total.shape
    count, _, depth, part = early.shape
    rows = codes * streams
    return pl.pallas_call(
        head_kernel,
        in_specs=[SMEM, VMEM, VMEM, VMEM, HBM, VMEM, VMEM],
        out_specs=[VMEM] * (count + 1),
        out_shape=[shape((rows, part), jnp.float32), shape((1, rows), jnp.float32)]
        + [shape((rows + STAT_ROWS, part), jnp.bfloat16)] * (count - 1),
        scratch_shapes=[
            pltpu.VMEM((count, codes, depth, part), jnp.bfloat16),
            pltpu.SemaphoreType.DMA((count,)),
        ],
        compiler_params=params(16),
        name="head",
    )(place, gain, total, arrived, in_hbm(weight), early, late)


def logits_kernel(width, kept_ref, stat_ref, *rest):
    arrived, out_ref = rest[:-1], rest[-1]
    streams, codes, part = out_ref.shape
    rows = codes * streams
    total = kept_ref[...]
    stat = stat_ref[...]
    for block in arrived:
        wide = block[...].astype(jnp.float32)
        total = total + wide[:rows]
        stat = stat + wide[rows : rows + 1] + wide[rows + 1 : rows + 2]
    total = total * column_of(lax.rsqrt(stat / width + EPSILON))
    for c in range(codes):
        out_ref[:, c, :] = total[c * streams : (c + 1) * streams]


def finished_logits(kept, stat, arrived, codes, width):
    rows, part = kept.shape
    return pl.pallas_call(
        functools.partial(logits_kernel, width),
        in_specs=[VMEM] * (2 + len(arrived)),
        out_specs=VMEM,
        out_shape=shape((rows // codes, codes, part), jnp.float32),
        compiler_params=params(16),
        name="logits",
    )(kept, stat, *arrived)


def paired_device(
    hidden_in,
    temporal_gain,
    temporal_qkv,
    temporal_out_weight,
    cache_keys,
    cache_values,
    lengths,
    depth_in,
    depth_embed,
    depth_gain,
    depth_qkv,
    depth_out_weight,
    head_gain,
    head_weight,
    tokens,
):
    tp = lax.axis_size("tp")
    tp_place = lax.axis_index("tp")
    place = jnp.stack([tp_place, lax.axis_index("section")])
    far = tp // 2 - 1

    def to_pairs(blocks):
        return [
            lax.ppermute(block, "tp", [(i, i ^ 2 * (k + 1)) for i in range(tp)])
            for k, block in enumerate(blocks)
        ]

    def to_neighbour(block):
        return lax.ppermute(block, "tp", [(i, i ^ 1) for i in range(tp)])

    early_half, late_half = partner_columns(place, head_weight, tp)
    early = to_neighbour(early_half)
    parts = temporal_parts(
        hidden_in, temporal_gain, lengths, temporal_qkv, temporal_out_weight, cache_keys, cache_values, tp
    )
    slice_width = parts.shape[2]
    parts, early = lax.optimization_barrier((parts, early))
    summed = scattered_sum(parts)
    resid_in = lax.dynamic_slice_in_dim(hidden_in, tp_place * slice_width, slice_width, 1)
    temporal = (resid_in.astype(jnp.float32) + summed).astype(jnp.bfloat16)
    all_rows = lax.all_gather(temporal, "section", axis=0, tiled=True)
    codes = depth_in.shape[0]
    width = depth_in.shape[2]
    hidden_rows = head_weight.shape[1]
    local_tokens = tokens - tp_place * depth_embed.shape[1]
    entry = scattered_sum(entry_parts(all_rows, local_tokens, depth_in, depth_embed, tp))
    own_gain = lax.dynamic_slice_in_dim(depth_gain, tp_place * hidden_rows, hidden_rows, 0)
    rows = gathered((entry * own_gain).astype(jnp.bfloat16))
    queries, own_pair = depth_projections(rows, depth_gain, depth_qkv)
    prior_pair = passed_along(own_pair, "section", 1)
    kept, *blocks = mixed_parts(place, queries, own_pair, prior_pair, depth_out_weight, far)
    late_half, kept = lax.optimization_barrier((late_half, kept))
    late = to_neighbour(late_half)
    total, sent = pair_sums(place, entry, kept, to_pairs(blocks))
    pair_gain = lax.dynamic_slice_in_dim(head_gain, tp_place // 2 * 2 * hidden_rows, 2 * hidden_rows, 0)
    kept, stat, *blocks = head_parts(
        place, pair_gain.reshape(1, 1, -1), total, to_neighbour(sent), head_weight, early, late
    )
    logits = finished_logits(kept, stat, to_pairs(blocks), codes, width)
    return (temporal, logits)


def per_device(*arrays):
    hidden_in, temporal_qkv, depth_qkv, head_weight = arrays[0], arrays[2], arrays[10], arrays[13]
    tp = lax.axis_size("tp")
    pairs = hidden_in.shape[0] * (temporal_qkv.shape[2] // HEAD_DIM)
    whole_tiles = (
        pairs % 128 == 0
        and temporal_qkv.shape[2] % HEAD_DIM == 0
        and head_weight.shape[1] % 128 == 0
        and head_weight.shape[2] // tp % 128 == 0
        and depth_qkv.shape[3] % 128 == 0
        and tp >= 4
        and tp & (tp - 1) == 0
    )
    return (paired_device if whole_tiles else general_device)(*arrays)


def solution(mesh):
    return jax.shard_map(
        per_device,
        mesh=mesh,
        in_specs=(
            P(("grp", "section"), None),
            P(),
            P(None, None, "tp"),
            P("tp", None),
            P(("grp", "section"), None, "tp"),
            P(("grp", "section"), None, "tp"),
            P(("grp", "section")),
            P("section", "tp", None),
            P("section", "tp", None),
            P(),
            P("section", None, None, "tp"),
            P("section", "tp", None),
            P(),
            P("section", "tp", None),
            P("grp", "section"),
        ),
        out_specs=(P(("grp", "section"), "tp"), P("grp", "section", "tp")),
        check_vma=False,
    )
```

```python
import functools
import math

import jax
import jax.numpy as jnp
from jax import lax
from jax.experimental import pallas as pl
from jax.experimental.pallas import tpu as pltpu
from jax.sharding import PartitionSpec as P

HEAD_DIM = 128
DEPTH_HDIM = 64


EPSILON = 1e-05


def passed_along(block, axis, distance):
    devices = range(lax.axis_size(axis))
    route = [(i - distance, i) for i in devices if i - distance in devices]
    return lax.ppermute(block, axis, route)


def from_partner(shard, axis, distance):
    return lax.ppermute(shard, axis, [(i, i ^ 1 << distance) for i in range(lax.axis_size(axis))])


def rms_norm(values, scale):
    wide = values.astype(jnp.float32)
    return wide * lax.rsqrt(jnp.mean(wide * wide, axis=-1, keepdims=True) + EPSILON) * scale


def rotate(vectors, positions):
    halfdim = vectors.shape[-1] // 2
    spacing = jnp.arange(halfdim, dtype=jnp.float32) / halfdim
    inverse = jnp.exp(-math.log(10000.0) * spacing)
    angles = positions.astype(jnp.float32)[:, None, None] * inverse[None, None, :]
    cosine = jnp.cos(angles)
    sine = jnp.sin(angles)
    first = vectors[..., :halfdim]
    second = vectors[..., halfdim:]
    return jnp.concatenate(
        [first * cosine - second * sine, first * sine + second * cosine], axis=-1
    )


def scattered_sum(parts):
    moved = lax.all_to_all(parts.astype(jnp.bfloat16), "tp", 0, 0)
    return jnp.sum(moved.astype(jnp.float32), axis=0)


def gathered(block):
    size = lax.axis_size("tp")
    return lax.all_to_all(jnp.broadcast_to(block[None], (size,) + block.shape), "tp", 0, 0)


def general_device(
    hidden_in,
    temporal_gain,
    temporal_qkv,
    temporal_out_weight,
    cache_keys,
    cache_values,
    lengths,
    depth_in,
    depth_embed,
    depth_gain,
    depth_qkv,
    depth_out_weight,
    head_gain,
    head_weight,
    tokens,
):
    tp = lax.axis_size("tp")
    local_streams = hidden_in.shape[0]
    local_cols = temporal_qkv.shape[2]
    local_heads = local_cols // HEAD_DIM
    cache_len = cache_keys.shape[1]
    normed = rms_norm(hidden_in, temporal_gain).astype(jnp.bfloat16)
    projected = jnp.einsum("sd,tdf->tsf", normed, temporal_qkv, preferred_element_type=jnp.float32)
    layout = (local_streams, local_heads, HEAD_DIM)
    queries = rotate(projected[0].reshape(layout), lengths).astype(jnp.bfloat16)
    keys_new = rotate(projected[1].reshape(layout), lengths).astype(jnp.bfloat16)
    values_new = projected[2].reshape(layout).astype(jnp.bfloat16)
    cached_keys = cache_keys.reshape(local_streams, cache_len, local_heads, HEAD_DIM)
    cached_values = cache_values.reshape(local_streams, cache_len, local_heads, HEAD_DIM)
    factor = 1.0 / math.sqrt(HEAD_DIM)
    scores = (
        jnp.einsum("shd,sphd->shp", queries, cached_keys, preferred_element_type=jnp.float32)
        * factor
    )
    own_score = (
        jnp.sum(queries.astype(jnp.float32) * keys_new.astype(jnp.float32), axis=-1) * factor
    )
    valid = jnp.arange(cache_len, dtype=jnp.int32)[None, None, :] < lengths[:, None, None]
    scores = jnp.where(valid, scores, -jnp.inf)
    highest = jnp.maximum(jnp.max(scores, axis=-1), own_score)
    expo = jnp.exp(scores - highest[..., None])
    own_expo = jnp.exp(own_score - highest)
    totals = jnp.sum(expo, axis=-1) + own_expo
    weights = (expo / totals[..., None]).astype(jnp.bfloat16)
    own_weight = (own_expo / totals).astype(jnp.bfloat16)
    mixed = jnp.einsum("shp,sphd->shd", weights, cached_values, preferred_element_type=jnp.float32)
    mixed = mixed + own_weight.astype(jnp.float32)[..., None] * values_new.astype(jnp.float32)
    mixed = mixed.astype(jnp.bfloat16).reshape(local_streams, local_cols)
    partial_rows = jnp.dot(mixed, temporal_out_weight, preferred_element_type=jnp.float32)
    slice_width = partial_rows.shape[1] // tp
    by_slice = partial_rows.reshape(local_streams, tp, slice_width).transpose(1, 0, 2)
    summed = scattered_sum(by_slice)
    tp_place = lax.axis_index("tp")
    resid_in = lax.dynamic_slice_in_dim(hidden_in, tp_place * slice_width, slice_width, 1)
    temporal = (resid_in.astype(jnp.float32) + summed).astype(jnp.bfloat16)
    all_rows = lax.all_gather(temporal, "section", axis=0, tiled=True)
    streams = all_rows.shape[0]
    codes = depth_in.shape[0]
    width = depth_in.shape[2]
    vocab_local = depth_embed.shape[1]
    first_id = tp_place * vocab_local
    onehot = (
        tokens[:, :, None] == first_id + jnp.arange(vocab_local, dtype=jnp.int32)[None, None, :]
    ).astype(jnp.bfloat16)
    embedded = jnp.einsum("scv,cve->cse", onehot, depth_embed, preferred_element_type=jnp.float32)
    entry_terms = embedded + jnp.einsum(
        "sd,cde->cse", all_rows, depth_in, preferred_element_type=jnp.float32
    )
    hidden_rows = head_weight.shape[1]
    hidden_start = tp_place * hidden_rows
    entry = scattered_sum(entry_terms.reshape(codes, streams, tp, hidden_rows).transpose(2, 0, 1, 3))
    own_gain = lax.dynamic_slice_in_dim(depth_gain, hidden_start, hidden_rows, 0)
    scaled = (entry * own_gain).astype(jnp.bfloat16)
    rows = gathered(scaled)
    plain = rows.astype(jnp.float32) / depth_gain.reshape(tp, 1, 1, hidden_rows)
    inv_rms = lax.rsqrt(jnp.sum(plain * plain, axis=(0, 3)) / width + EPSILON)
    dproj = jnp.einsum(
        "tcse,cntef->ncsf",
        rows,
        depth_qkv.reshape(codes, 3, tp, hidden_rows, -1),
        preferred_element_type=jnp.float32,
    )
    dproj = (dproj * inv_rms[None, :, :, None]).astype(jnp.bfloat16)
    prior = passed_along(dproj[1:], "section", 1)
    depth_cols = dproj.shape[3]
    head_part = min(depth_cols, DEPTH_HDIM)
    local_parts = depth_cols // head_part
    sharers = DEPTH_HDIM // head_part
    both = jnp.concatenate([prior, dproj[1:]], axis=1)
    all_keys = both[0].reshape(2 * codes, streams, local_parts, head_part)
    all_values = both[1].reshape(2 * codes, streams, local_parts, head_part)
    depth_queries = dproj[0].reshape(codes, streams, local_parts, head_part)
    depth_scores = jnp.sum(
        depth_queries[:, None].astype(jnp.float32) * all_keys[None].astype(jnp.float32), axis=-1
    )
    for level in range(sharers.bit_length() - 1):
        depth_scores = depth_scores + from_partner(depth_scores, "tp", level)
    depth_scores = depth_scores * (1.0 / math.sqrt(DEPTH_HDIM))
    section_place = lax.axis_index("section")
    query_pos = jnp.arange(codes, dtype=jnp.int32)[:, None]
    key_pos = jnp.arange(2 * codes, dtype=jnp.int32)[None, :]
    allowed = jnp.where(key_pos < codes, section_place > 0, key_pos - codes <= query_pos)
    depth_scores = jnp.where(allowed[:, :, None, None], depth_scores, -jnp.inf)
    depth_top = jnp.max(depth_scores, axis=1, keepdims=True)
    depth_expo = jnp.exp(depth_scores - depth_top)
    depth_weights = (depth_expo / jnp.sum(depth_expo, axis=1, keepdims=True)).astype(jnp.bfloat16)
    depth_mixed = jnp.sum(
        depth_weights[..., None].astype(jnp.float32) * all_values[None].astype(jnp.float32), axis=1
    ).astype(jnp.bfloat16)
    depth_mixed = depth_mixed.reshape(codes, streams, depth_cols)
    depth_terms = jnp.einsum(
        "csf,cfe->cse", depth_mixed, depth_out_weight, preferred_element_type=jnp.float32
    )
    added = scattered_sum(depth_terms.reshape(codes, streams, tp, hidden_rows).transpose(2, 0, 1, 3))
    resid = entry + added
    own_head_gain = lax.dynamic_slice_in_dim(head_gain, hidden_start, hidden_rows, 0)
    own_hidden = (resid * own_head_gain).astype(jnp.bfloat16)
    squares = jnp.sum(resid * resid, axis=2)
    high = squares.astype(jnp.bfloat16)
    low = (squares - high.astype(jnp.float32)).astype(jnp.bfloat16)
    partial_logits = jnp.einsum(
        "cse,cev->csv", own_hidden, head_weight, preferred_element_type=jnp.float32
    )
    vocab_slice = partial_logits.shape[2] // tp
    outgoing = partial_logits.reshape(codes, streams, tp, vocab_slice).transpose(2, 0, 1, 3)
    outgoing = outgoing.astype(jnp.bfloat16).reshape(tp, codes * streams, vocab_slice)
    extra = jnp.stack([high.reshape(-1), low.reshape(-1)])
    extra = jnp.pad(extra, ((0, 14), (0, 0))).reshape(-1, vocab_slice)
    packed = jnp.concatenate(
        [outgoing, jnp.broadcast_to(extra[None], (tp,) + extra.shape)], axis=1
    )
    moved = lax.all_to_all(packed, "tp", 0, 0).astype(jnp.float32)
    rows_total = jnp.sum(moved, axis=0)
    stats = rows_total[codes * streams :].reshape(16, codes, streams)
    head_inv = lax.rsqrt((stats[0] + stats[1]) / width + EPSILON)
    logits = rows_total[: codes * streams].reshape(codes, streams, vocab_slice) * head_inv[..., None]
    return (temporal, logits.transpose(1, 0, 2))


HBM = pl.BlockSpec(memory_space=pltpu.HBM)
VMEM = pl.BlockSpec(memory_space=pltpu.VMEM)
SMEM = pl.BlockSpec(memory_space=pltpu.SMEM)


def params(mebibytes):
    return pltpu.CompilerParams(vmem_limit_bytes=mebibytes * 1024 * 1024)


def in_hbm(array):
    return pltpu.with_memory_space_constraint(array, pltpu.HBM)


def shape(dims, dtype):
    return jax.ShapeDtypeStruct(dims, dtype)


def vmem(dims, dtype):
    return pltpu.VMEM(dims, dtype)


def product(left, right):
    return jnp.dot(left, right, preferred_element_type=jnp.float32)


def product_t(left, right):
    return lax.dot_general(left, right, (((1,), (1,)), ((), ())), preferred_element_type=jnp.float32)


def column_of(row):
    size = row.shape[1]
    first = lax.broadcasted_iota(jnp.int32, (size, size), 0)
    second = lax.broadcasted_iota(jnp.int32, (size, size), 1)
    return jnp.sum(jnp.where(first == second, row, 0.0), axis=1, keepdims=True)


IN_FLIGHT = 6


class Stream:
    def __init__(self, copies):
        self.copies = copies
        self.done = 0
        for copy in copies[:IN_FLIGHT]:
            copy.start()

    def arrived(self, upto):
        while self.done <= upto:
            self.copies[self.done].wait()
            if self.done + IN_FLIGHT < len(self.copies):
                self.copies[self.done + IN_FLIGHT].start()
            self.done += 1


def temporal_kernel(
    place_ref, hidden_hbm, gain_hbm, lengths_hbm, qkv_hbm, out_hbm, keys_hbm, values_hbm, kept_ref, sent_ref,
    hidden_buf, gain_buf, lengths_buf, qkv_buf, out_buf, keys_buf, values_buf, small_sems, sems,
):
    streams, depth = hidden_buf.shape
    cols = qkv_buf.shape[2]
    heads = cols // HEAD_DIM
    cache_len = keys_buf.shape[1]
    steps, halves = QKV_STEPS, CACHE_STEPS
    chunk = depth // steps
    batch = streams // halves
    count, _, width = kept_ref.shape
    odd = place_ref[0] % 2
    place = place_ref[0] // 2
    small = [
        pltpu.make_async_copy(hidden_hbm, hidden_buf, small_sems.at[0]),
        pltpu.make_async_copy(gain_hbm, gain_buf, small_sems.at[1]),
        pltpu.make_async_copy(lengths_hbm, lengths_buf, small_sems.at[2]),
    ]
    for copy in small:
        copy.start()
    pairs = []
    for n in (0, 1):
        pairs += [(qkv_hbm.at[n, pl.ds(i * chunk, chunk)], qkv_buf.at[n, pl.ds(i * chunk, chunk)]) for i in range(steps)]
    pairs += [(keys_hbm.at[pl.ds(i * batch, batch)], keys_buf.at[pl.ds(i * batch, batch)]) for i in range(halves)]
    pairs += [(qkv_hbm.at[2, pl.ds(i * chunk, chunk)], qkv_buf.at[2, pl.ds(i * chunk, chunk)]) for i in range(steps)]
    pairs += [(values_hbm.at[pl.ds(i * batch, batch)], values_buf.at[pl.ds(i * batch, batch)]) for i in range(halves)]
    pairs += [
        (out_hbm.at[:, pl.ds(pl.multiple_of((place ^ k) * 2 * width, 2 * width), 2 * width)], out_buf.at[k])
        for k in range(count)
    ]
    stream = Stream([pltpu.make_async_copy(src, dst, sems.at[i]) for i, (src, dst) in enumerate(pairs)])
    first_of = (0, steps, 2 * steps + halves)
    keys_end = 2 * steps + halves - 1
    values_end = 3 * steps + 2 * halves - 1

    for copy in small:
        copy.wait()
    wide = hidden_buf[...].astype(jnp.float32)
    inv = lax.rsqrt(jnp.mean(wide * wide, axis=1, keepdims=True) + EPSILON)
    normed = (wide * inv * gain_buf[...]).astype(jnp.bfloat16)

    def projected(n):
        total = None
        for i in range(steps):
            stream.arrived(first_of[n] + i)
            part = product(normed[:, i * chunk : (i + 1) * chunk], qkv_buf[n, pl.ds(i * chunk, chunk), :])
            total = part if total is None else total + part
        return total

    lengths_row = lengths_buf[...].astype(jnp.float32)
    lengths_col = column_of(lengths_row)
    half = HEAD_DIM // 2
    lane = lax.broadcasted_iota(jnp.int32, (streams, HEAD_DIM), 1)
    spacing = (lane & (half - 1)).astype(jnp.float32) / half
    angles = lengths_col * jnp.exp(-math.log(10000.0) * spacing)
    cosine = jnp.cos(angles)
    sine = jnp.where(lane < half, -1.0, 1.0) * jnp.sin(angles)

    def rotated(block):
        pieces = []
        for h in range(heads):
            piece = block[:, h * HEAD_DIM : (h + 1) * HEAD_DIM]
            pieces.append(piece * cosine + pltpu.roll(piece, half, 1) * sine)
        return jnp.concatenate(pieces, axis=1)

    queries = rotated(projected(0))
    keys_new = rotated(projected(1)).astype(jnp.bfloat16)
    head_lane = lax.broadcasted_iota(jnp.int32, (streams, cols), 1) // HEAD_DIM
    spread = jnp.concatenate(
        [jnp.where(head_lane == h, queries, 0.0) for h in range(heads)], axis=0
    ).astype(jnp.bfloat16)
    pairs = heads * streams
    factor = 1.0 / math.sqrt(HEAD_DIM)
    pair = lax.broadcasted_iota(jnp.int32, (1, pairs), 1)
    pair_stream = pair % streams
    own = product_t(keys_new, spread) * factor
    stream_row = lax.broadcasted_iota(jnp.int32, (streams, pairs), 0)
    own_score = jnp.sum(jnp.where(stream_row == pair_stream, own, 0.0), axis=0, keepdims=True)
    tiled = jnp.sum(jnp.where(stream_row == pair_stream, lengths_col, 0.0), axis=0, keepdims=True)
    first_row = pair_stream * cache_len
    last_row = first_row + tiled.astype(jnp.int32)
    stream.arrived(keys_end)
    rows = streams * cache_len
    scores = product_t(keys_buf[...].reshape(rows, cols), spread) * factor
    row = lax.broadcasted_iota(jnp.int32, (rows, pairs), 0)
    scores = jnp.where((row >= first_row) & (row < last_row), scores, -jnp.inf)
    highest = jnp.maximum(jnp.max(scores, axis=0, keepdims=True), own_score)
    expo = jnp.exp(scores - highest)
    own_expo = jnp.exp(own_score - highest)
    inverse = 1.0 / (jnp.sum(expo, axis=0, keepdims=True) + own_expo)
    weights = (expo * inverse).astype(jnp.bfloat16)
    own_weight = (own_expo * inverse).astype(jnp.bfloat16).astype(jnp.float32)
    values_new = projected(2).astype(jnp.bfloat16).astype(jnp.float32)
    stream.arrived(values_end)
    mixed_all = lax.dot_general(
        weights,
        values_buf[...].reshape(rows, cols),
        (((0,), (0,)), ((), ())),
        preferred_element_type=jnp.float32,
    )
    pair_lane = lax.broadcasted_iota(jnp.int32, (streams, pairs), 1)
    pair_row = lax.broadcasted_iota(jnp.int32, (streams, pairs), 0)
    mixed = []
    for h in range(heads):
        own_col = jnp.sum(
            jnp.where(pair_lane == pair_row + h * streams, own_weight, 0.0), axis=1, keepdims=True
        )
        lanes = slice(h * HEAD_DIM, (h + 1) * HEAD_DIM)
        mixed.append(
            mixed_all[h * streams : (h + 1) * streams, lanes] + own_col * values_new[:, lanes]
        )
    mixed = jnp.concatenate(mixed, axis=1).astype(jnp.bfloat16)
    for k in range(count):
        stream.arrived(values_end + 1 + k)
        block = product(mixed, out_buf[k])
        even_side, odd_side = block[:, :width], block[:, width:]
        kept_ref[k] = jnp.where(odd == 1, odd_side, even_side)
        sent_ref[k] = jnp.where(odd == 1, even_side, odd_side).astype(jnp.bfloat16)


QKV_STEPS = 4
CACHE_STEPS = 2


def temporal_parts(place, hidden_in, gain, lengths, qkv, out_weight, keys, values, places):
    streams, depth = hidden_in.shape
    bf16 = jnp.bfloat16
    count, width = places // 2, out_weight.shape[1] // places
    block = (count, streams, width)
    return pl.pallas_call(
        temporal_kernel,
        in_specs=[SMEM] + [HBM] * 7,
        out_specs=[VMEM, VMEM],
        out_shape=[vmem(block, jnp.float32), vmem(block, bf16)],
        scratch_shapes=[
            pltpu.VMEM(hidden_in.shape, bf16),
            pltpu.VMEM((1, depth), jnp.float32),
            pltpu.VMEM((1, streams), jnp.int32),
            pltpu.VMEM(qkv.shape, bf16),
            pltpu.VMEM((count, out_weight.shape[0], 2 * width), bf16),
            pltpu.VMEM(keys.shape, bf16),
            pltpu.VMEM(values.shape, bf16),
            pltpu.SemaphoreType.DMA((3,)),
            pltpu.SemaphoreType.DMA((3 * QKV_STEPS + 2 * CACHE_STEPS + count,)),
        ],
        compiler_params=params(30),
        name="temporal",
    )(
        place,
        in_hbm(hidden_in),
        in_hbm(gain.reshape(1, depth)),
        in_hbm(lengths.reshape(1, streams)),
        in_hbm(qkv),
        in_hbm(out_weight),
        in_hbm(keys),
        in_hbm(values),
    )


def prepare_kernel(
    place_ref, tokens_ref, hidden_hbm, embed_hbm, weight_hbm, resid_ref, embedded_ref, weight_ref, embed_buf, sem, sems
):
    codes, vocab, _ = embed_buf.shape
    streams = tokens_ref.shape[0]
    part = resid_ref.shape[1]
    start = pl.multiple_of(place_ref[0] * part, part)
    resid = pltpu.make_async_copy(hidden_hbm.at[:, pl.ds(start, part)], resid_ref, sem)
    resid.start()
    embed = [pltpu.make_async_copy(embed_hbm.at[c], embed_buf.at[c], sems.at[0, c]) for c in range(codes)]
    weight = [pltpu.make_async_copy(weight_hbm.at[c], weight_ref.at[c], sems.at[1, c]) for c in range(codes)]
    for copy in embed + weight:
        copy.start()
    vocab_lane = lax.broadcasted_iota(jnp.int32, (streams, vocab), 1) + place_ref[0] * vocab
    for c in range(codes):
        hit = tokens_ref[:, c : c + 1] == vocab_lane
        onehot = jnp.where(hit, 1.0, 0.0).astype(jnp.bfloat16)
        embed[c].wait()
        embedded_ref[c] = product(onehot, embed_buf[c])
    for copy in weight:
        copy.wait()
    resid.wait()


def prepared_entry(place, tokens, hidden_in, embed, weight, places):
    codes, _, width = weight.shape
    streams = tokens.shape[0]
    resid_shape = (hidden_in.shape[0], hidden_in.shape[1] // places)
    return pl.pallas_call(
        prepare_kernel,
        in_specs=[SMEM, VMEM, HBM, HBM, HBM],
        out_specs=[VMEM] * 3,
        out_shape=[
            vmem(resid_shape, jnp.bfloat16),
            vmem((codes, streams, width), jnp.float32),
            vmem(weight.shape, jnp.bfloat16),
        ],
        scratch_shapes=[
            pltpu.VMEM(embed.shape, jnp.bfloat16),
            pltpu.SemaphoreType.DMA(()),
            pltpu.SemaphoreType.DMA((2, codes)),
        ],
        compiler_params=params(16),
        name="entry_prepare",
    )(place, tokens, in_hbm(hidden_in), in_hbm(embed), in_hbm(weight))


def near_kernel(
    place_ref, gain_ref, qkv_hbm, out_hbm, head_hbm, own_ref, qkv_ref, out_ref, near_cols_ref, far_cols_ref, sems, col_sems
):
    copies = [
        pltpu.make_async_copy(source.at[c], target.at[c], sems.at[i, c])
        for i, (source, target) in enumerate(((qkv_hbm, qkv_ref), (out_hbm, out_ref)))
        for c in range(source.shape[0])
    ]
    count, _, _, vocab_part = near_cols_ref.shape
    odd = place_ref[0] % 2
    place = place_ref[0] // 2
    for n, (half, side) in enumerate(((far_cols_ref, 1 - odd), (near_cols_ref, odd))):
        for k in range(count):
            start = pl.multiple_of(((place ^ k) * 2 + side) * vocab_part, vocab_part)
            copies.append(
                pltpu.make_async_copy(head_hbm.at[:, :, pl.ds(start, vocab_part)], half.at[k], col_sems.at[n, k])
            )
    for copy in copies:
        copy.start()
    part = own_ref.shape[1]
    own_ref[...] = gain_ref[:, pl.ds(pl.multiple_of(place_ref[0] * part, part), part)]
    for copy in copies:
        copy.wait()


def brought_near(place, gain, qkv, out_weight, head_weight, places):
    width = gain.shape[0]
    codes, depth, vocab = head_weight.shape
    half = vmem((places // 2, codes, depth, vocab // places), jnp.bfloat16)
    return pl.pallas_call(
        near_kernel,
        in_specs=[SMEM, VMEM, HBM, HBM, HBM],
        out_specs=[VMEM] * 5,
        out_shape=[
            vmem((1, width // places), jnp.float32),
            vmem(qkv.shape, jnp.bfloat16),
            vmem(out_weight.shape, jnp.bfloat16),
            half,
            half,
        ],
        scratch_shapes=[pltpu.SemaphoreType.DMA((2, codes)), pltpu.SemaphoreType.DMA((2, places // 2))],
        compiler_params=params(16),
        name="brought_near",
    )(place, gain.reshape(1, width), in_hbm(qkv), in_hbm(out_weight), in_hbm(head_weight))


def entry_kernel(place_ref, own_ref, other_ref, embedded_ref, weight_ref, kept_ref, sent_ref, total_buf):
    codes = weight_ref.shape[0]
    count, _, _, part = kept_ref.shape
    odd = place_ref[0] % 2
    place = place_ref[0] // 2
    first_section = place_ref[1] == 0
    own, other = own_ref[...], other_ref[...]
    rows = jnp.concatenate(
        [jnp.where(first_section, own, other), jnp.where(first_section, other, own)], axis=0
    )
    for c in range(codes):
        total_buf[...] = embedded_ref[c] + product(rows, weight_ref[c])
        for k in range(count):
            pair = (place ^ k) * 2
            kept_ref[k, c] = total_buf[:, pl.ds(pl.multiple_of((pair + odd) * part, part), part)]
            sent = total_buf[:, pl.ds(pl.multiple_of((pair + 1 - odd) * part, part), part)]
            sent_ref[k, c] = sent.astype(jnp.bfloat16)


def entry_parts(place, own, other, embedded, weight, places):
    codes, _, width = weight.shape
    streams = 2 * own.shape[0]
    block = (places // 2, codes, streams, width // places)
    return pl.pallas_call(
        entry_kernel,
        in_specs=[SMEM] + [VMEM] * 4,
        out_specs=[VMEM, VMEM],
        out_shape=[shape(block, jnp.float32), shape(block, jnp.bfloat16)],
        scratch_shapes=[pltpu.VMEM((streams, width), jnp.float32)],
        compiler_params=params(16),
        name="entry",
    )(place, own, other, embedded, weight)


def qkv_kernel(
    place_ref, near_ref, far_ref, gain_ref, weight_ref, columns_ref, queries_ref, pair_ref, passed_ref, sem
):
    passed = pltpu.make_async_copy(columns_ref, passed_ref, sem)
    passed.start()
    codes, _, width, cols = weight_ref.shape
    count, _, _, part = near_ref.shape
    odd = place_ref[0] % 2
    place = place_ref[0] // 2
    starts = [
        pl.multiple_of(((place ^ k) * 2 + side) * part, part) for side in (odd, 1 - odd) for k in range(count)
    ]
    inverse_gain = 1.0 / jnp.concatenate([gain_ref[:, pl.ds(start, part)] for start in starts], axis=1)
    for c in range(codes):
        row = jnp.concatenate([ref[k, c] for ref in (near_ref, far_ref) for k in range(count)], axis=1)
        plain = row.astype(jnp.float32) * inverse_gain
        inv = lax.rsqrt(jnp.sum(plain * plain, axis=1, keepdims=True) / width + EPSILON)
        for n in range(3):
            weight = jnp.concatenate([weight_ref[c, n, pl.ds(start, part), :] for start in starts], axis=0)
            value = (product(row, weight) * inv).astype(jnp.bfloat16)
            if n == 0:
                queries_ref[c] = value
            else:
                pair_ref[n - 1, c] = value
    passed.wait()


def depth_projections(place, near, far, gain, weight, columns):
    codes, _, width, cols = weight.shape
    streams = near.shape[2]
    bf16 = jnp.bfloat16
    return pl.pallas_call(
        qkv_kernel,
        in_specs=[SMEM] + [VMEM] * 5,
        out_specs=[VMEM] * 3,
        out_shape=[
            shape((codes, streams, cols), bf16),
            shape((2, codes, streams, cols), bf16),
            vmem(columns.shape, bf16),
        ],
        scratch_shapes=[pltpu.SemaphoreType.DMA(())],
        compiler_params=params(16),
        name="depth_qkv",
    )(place, near, far, gain.reshape(1, width), weight, columns)


def mix_kernel(place_ref, queries_ref, own_ref, prior_ref, weight_ref, kept_ref, *rest):
    sends, total_buf = rest[:-1], rest[-1]
    codes, streams, cols = queries_ref.shape
    span = kept_ref.shape[2]
    has_prior = place_ref[1] > 0
    first = lax.broadcasted_iota(jnp.int32, (2 * cols, cols), 0) % cols
    second = lax.broadcasted_iota(jnp.int32, (2 * cols, cols), 1)
    same = jnp.where(first // DEPTH_HDIM == second // DEPTH_HDIM, 1.0, 0.0).astype(jnp.bfloat16)
    keys = [prior_ref[0, j].astype(jnp.float32) for j in range(codes)]
    keys += [own_ref[0, j].astype(jnp.float32) for j in range(codes)]
    values = [prior_ref[1, j].astype(jnp.float32) for j in range(codes)]
    values += [own_ref[1, j].astype(jnp.float32) for j in range(codes)]
    factor = 1.0 / math.sqrt(DEPTH_HDIM)
    mixed = []
    for q in range(codes):
        query = queries_ref[q].astype(jnp.float32)
        reach = codes + q + 1
        pieces = []
        for j in range(reach):
            exact = query * keys[j]
            high = exact.astype(jnp.bfloat16)
            low = (exact - high.astype(jnp.float32)).astype(jnp.bfloat16)
            pieces.append(jnp.concatenate([high, low], axis=1))
        scores = product(jnp.concatenate(pieces, axis=0), same) * factor
        score = [scores[j * streams : (j + 1) * streams] for j in range(reach)]
        score = [jnp.where(has_prior, s, -jnp.inf) if j < codes else s for j, s in enumerate(score)]
        top = score[0]
        for s in score[1:]:
            top = jnp.maximum(top, s)
        expo = [jnp.exp(s - top) for s in score]
        inverse = 1.0 / sum(expo)
        total = jnp.zeros_like(query)
        for j in range(reach):
            total = total + (expo[j] * inverse).astype(jnp.bfloat16).astype(jnp.float32) * values[j]
        mixed.append(total.astype(jnp.bfloat16))
    for q in range(codes):
        total_buf[q] = product(mixed[q], weight_ref[q])
    place = place_ref[0] // 2
    for k in range(len(sends) + 1):
        start = pl.multiple_of((place ^ k) * span, span)
        block = total_buf[:, :, pl.ds(start, span)]
        if k == 0:
            kept_ref[...] = block
        else:
            sends[k - 1][...] = block.astype(jnp.bfloat16)


def mixed_parts(place, queries, own, prior, weight, far):
    codes, streams, cols = queries.shape
    width = weight.shape[2]
    block = (codes, streams, width // (far + 1))
    return pl.pallas_call(
        mix_kernel,
        in_specs=[SMEM] + [VMEM] * 4,
        out_specs=[VMEM] * (far + 1),
        out_shape=[shape(block, jnp.float32)] + [shape(block, jnp.bfloat16)] * far,
        scratch_shapes=[pltpu.VMEM((codes, streams, width), jnp.float32)],
        compiler_params=params(16),
        name="depth_mix",
    )(place, queries, own, prior, weight)


STAT_ROWS = 16


def head_kernel(place_ref, gain_ref, total_ref, arrived_ref, weight_ref, partner_ref, kept_ref, stat_ref, *sends):
    codes, streams, span = total_ref.shape
    count, _, depth, part = weight_ref.shape
    odd = place_ref[0] % 2
    resid = total_ref[...] + arrived_ref[...].astype(jnp.float32)
    flat = resid.reshape(codes * streams, span)
    squares = flat * flat
    stat = product_t(jnp.ones((STAT_ROWS // 2, span), jnp.float32), squares)[:1]
    stat_ref[...] = stat
    high = stat.astype(jnp.bfloat16).astype(jnp.float32)
    stat_row = lax.broadcasted_iota(jnp.int32, (STAT_ROWS, codes * streams), 0)
    stat_block = jnp.where(stat_row == 0, high, jnp.where(stat_row == 1, stat - high, 0.0))
    stat_block = stat_block.astype(jnp.bfloat16)
    scaled = resid * gain_ref[...]
    low_half, high_half = scaled[:, :, :depth], scaled[:, :, depth:]
    ordered = jnp.concatenate(
        [jnp.where(odd == 1, high_half, low_half), jnp.where(odd == 1, low_half, high_half)], axis=2
    ).astype(jnp.bfloat16)
    rows = codes * streams
    for k in range(count):
        block = jnp.concatenate(
            [
                product(ordered[c], jnp.concatenate([weight_ref[k, c], partner_ref[k, c]], axis=0))
                for c in range(codes)
            ],
            axis=0,
        )
        if k == 0:
            kept_ref[...] = block
        else:
            sends[k - 1][pl.ds(0, rows), :] = block.astype(jnp.bfloat16)
            sends[k - 1][pl.ds(rows, STAT_ROWS), :] = stat_block


def head_parts(place, gain, total, arrived, weight, partner):
    codes, streams, span = total.shape
    count, _, depth, part = weight.shape
    rows = codes * streams
    return pl.pallas_call(
        head_kernel,
        in_specs=[SMEM] + [VMEM] * 5,
        out_specs=[VMEM] * (count + 1),
        out_shape=[shape((rows, part), jnp.float32), shape((1, rows), jnp.float32)]
        + [shape((rows + STAT_ROWS, part), jnp.bfloat16)] * (count - 1),
        compiler_params=params(16),
        name="head",
    )(place, gain, total, arrived, weight, partner)


def logits_kernel(width, kept_ref, stat_ref, *rest):
    arrived, out_ref = rest[:-1], rest[-1]
    streams, codes, part = out_ref.shape
    rows = codes * streams
    total = kept_ref[...]
    stat = stat_ref[...]
    for block in arrived:
        wide = block[...].astype(jnp.float32)
        total = total + wide[:rows]
        stat = stat + wide[rows : rows + 1] + wide[rows + 1 : rows + 2]
    total = total * column_of(lax.rsqrt(stat / width + EPSILON))
    for c in range(codes):
        out_ref[:, c, :] = total[c * streams : (c + 1) * streams]


def finished_logits(kept, stat, arrived, codes, width):
    rows, part = kept.shape
    return pl.pallas_call(
        functools.partial(logits_kernel, width),
        in_specs=[VMEM] * (2 + len(arrived)),
        out_specs=VMEM,
        out_shape=shape((rows // codes, codes, part), jnp.float32),
        compiler_params=params(16),
        name="logits",
    )(kept, stat, *arrived)


def paired_device(
    hidden_in,
    temporal_gain,
    temporal_qkv,
    temporal_out_weight,
    cache_keys,
    cache_values,
    lengths,
    depth_in,
    depth_embed,
    depth_gain,
    depth_qkv,
    depth_out_weight,
    head_gain,
    head_weight,
    tokens,
):
    tp = lax.axis_size("tp")
    tp_place = lax.axis_index("tp")
    place = jnp.stack([tp_place, lax.axis_index("section")])
    far = tp // 2 - 1

    def to_pairs(blocks):
        return [
            lax.ppermute(block, "tp", [(i, i ^ 2 * (k + 1)) for i in range(tp)])
            for k, block in enumerate(blocks)
        ]

    def to_neighbour(block):
        return lax.ppermute(block, "tp", [(i, i ^ 1) for i in range(tp)])

    def summed(kept, sent):
        folded = kept + to_neighbour(sent).astype(jnp.float32)
        arrived = to_pairs([folded[k].astype(jnp.bfloat16) for k in range(1, far + 1)])
        return folded[0] + sum(block.astype(jnp.float32) for block in arrived)

    kept, sent = temporal_parts(
        place, hidden_in, temporal_gain, lengths, temporal_qkv, temporal_out_weight, cache_keys, cache_values, tp
    )
    sent, depth_in = lax.optimization_barrier((sent, depth_in))
    resid_in, embedded, near_in = prepared_entry(place, tokens, hidden_in, depth_embed, depth_in, tp)
    temporal = (resid_in.astype(jnp.float32) + summed(kept, sent)).astype(jnp.bfloat16)
    other_rows = lax.ppermute(temporal, "section", [(0, 1), (1, 0)])
    codes = depth_in.shape[0]
    width = depth_in.shape[2]
    hidden_rows = head_weight.shape[1]
    kept, sent = entry_parts(place, temporal, other_rows, embedded, near_in, tp)
    sent, depth_qkv = lax.optimization_barrier((sent, depth_qkv))
    own_gain, near_qkv, near_out, own_columns, other_columns = brought_near(
        place, depth_gain, depth_qkv, depth_out_weight, head_weight, tp
    )
    entry = summed(kept, sent)
    scaled = (entry * own_gain[None]).astype(jnp.bfloat16)
    near = jnp.stack([scaled] + to_pairs([scaled] * far))
    queries, own_pair, other_columns = depth_projections(
        place, near, to_neighbour(near), depth_gain, near_qkv, other_columns
    )
    prior_pair = passed_along(own_pair, "section", 1)
    partner_columns = to_neighbour(other_columns)
    kept, *blocks = mixed_parts(place, queries, own_pair, prior_pair, near_out, far)
    odd = tp_place % 2 == 1
    none = jnp.zeros_like(entry)
    total = kept + sum(block.astype(jnp.float32) for block in to_pairs(blocks))
    total = total + jnp.concatenate([jnp.where(odd, none, entry), jnp.where(odd, entry, none)], axis=2)
    pair_gain = lax.dynamic_slice_in_dim(head_gain, tp_place // 2 * 2 * hidden_rows, 2 * hidden_rows, 0)
    kept, stat, *blocks = head_parts(
        place,
        pair_gain.reshape(1, 1, -1),
        total,
        to_neighbour(total.astype(jnp.bfloat16)),
        own_columns,
        partner_columns,
    )
    logits = finished_logits(kept, stat, to_pairs(blocks), codes, width)
    return (temporal, logits)


def per_device(*arrays):
    hidden_in, temporal_qkv, depth_qkv, head_weight = arrays[0], arrays[2], arrays[10], arrays[13]
    tp = lax.axis_size("tp")
    pairs = hidden_in.shape[0] * (temporal_qkv.shape[2] // HEAD_DIM)
    whole_tiles = (
        pairs % 128 == 0
        and temporal_qkv.shape[2] % HEAD_DIM == 0
        and head_weight.shape[1] % 128 == 0
        and head_weight.shape[2] // tp % 128 == 0
        and depth_qkv.shape[3] % 128 == 0
        and tp >= 4
        and tp & (tp - 1) == 0
    )
    return (paired_device if whole_tiles else general_device)(*arrays)


def solution(mesh):
    return jax.shard_map(
        per_device,
        mesh=mesh,
        in_specs=(
            P(("grp", "section"), None),
            P(),
            P(None, None, "tp"),
            P("tp", None),
            P(("grp", "section"), None, "tp"),
            P(("grp", "section"), None, "tp"),
            P(("grp", "section")),
            P("section", "tp", None),
            P("section", "tp", None),
            P(),
            P("section", None, None, "tp"),
            P("section", "tp", None),
            P(),
            P("section", "tp", None),
            P("grp", "section"),
        ),
        out_specs=(P(("grp", "section"), "tp"), P("grp", "section", "tp")),
        check_vma=False,
    )
```

```python
import functools
import math

import jax
import jax.numpy as jnp
from jax import lax
from jax.experimental import pallas as pl
from jax.experimental.pallas import tpu as pltpu
from jax.sharding import PartitionSpec as P

HEAD_DIM = 128
DEPTH_HDIM = 64


EPSILON = 1e-05


def passed_along(block, axis, distance):
    devices = range(lax.axis_size(axis))
    route = [(i - distance, i) for i in devices if i - distance in devices]
    return lax.ppermute(block, axis, route)


def from_partner(shard, axis, distance):
    return lax.ppermute(shard, axis, [(i, i ^ 1 << distance) for i in range(lax.axis_size(axis))])


def rms_norm(values, scale):
    wide = values.astype(jnp.float32)
    return wide * lax.rsqrt(jnp.mean(wide * wide, axis=-1, keepdims=True) + EPSILON) * scale


def rotate(vectors, positions):
    halfdim = vectors.shape[-1] // 2
    spacing = jnp.arange(halfdim, dtype=jnp.float32) / halfdim
    inverse = jnp.exp(-math.log(10000.0) * spacing)
    angles = positions.astype(jnp.float32)[:, None, None] * inverse[None, None, :]
    cosine = jnp.cos(angles)
    sine = jnp.sin(angles)
    first = vectors[..., :halfdim]
    second = vectors[..., halfdim:]
    return jnp.concatenate(
        [first * cosine - second * sine, first * sine + second * cosine], axis=-1
    )


def scattered_sum(parts):
    moved = lax.all_to_all(parts.astype(jnp.bfloat16), "tp", 0, 0)
    return jnp.sum(moved.astype(jnp.float32), axis=0)


def gathered(block):
    size = lax.axis_size("tp")
    return lax.all_to_all(jnp.broadcast_to(block[None], (size,) + block.shape), "tp", 0, 0)


def general_device(
    hidden_in,
    temporal_gain,
    temporal_qkv,
    temporal_out_weight,
    cache_keys,
    cache_values,
    lengths,
    depth_in,
    depth_embed,
    depth_gain,
    depth_qkv,
    depth_out_weight,
    head_gain,
    head_weight,
    tokens,
):
    tp = lax.axis_size("tp")
    local_streams = hidden_in.shape[0]
    local_cols = temporal_qkv.shape[2]
    local_heads = local_cols // HEAD_DIM
    cache_len = cache_keys.shape[1]
    normed = rms_norm(hidden_in, temporal_gain).astype(jnp.bfloat16)
    projected = jnp.einsum("sd,tdf->tsf", normed, temporal_qkv, preferred_element_type=jnp.float32)
    layout = (local_streams, local_heads, HEAD_DIM)
    queries = rotate(projected[0].reshape(layout), lengths).astype(jnp.bfloat16)
    keys_new = rotate(projected[1].reshape(layout), lengths).astype(jnp.bfloat16)
    values_new = projected[2].reshape(layout).astype(jnp.bfloat16)
    cached_keys = cache_keys.reshape(local_streams, cache_len, local_heads, HEAD_DIM)
    cached_values = cache_values.reshape(local_streams, cache_len, local_heads, HEAD_DIM)
    factor = 1.0 / math.sqrt(HEAD_DIM)
    scores = (
        jnp.einsum("shd,sphd->shp", queries, cached_keys, preferred_element_type=jnp.float32)
        * factor
    )
    own_score = (
        jnp.sum(queries.astype(jnp.float32) * keys_new.astype(jnp.float32), axis=-1) * factor
    )
    valid = jnp.arange(cache_len, dtype=jnp.int32)[None, None, :] < lengths[:, None, None]
    scores = jnp.where(valid, scores, -jnp.inf)
    highest = jnp.maximum(jnp.max(scores, axis=-1), own_score)
    expo = jnp.exp(scores - highest[..., None])
    own_expo = jnp.exp(own_score - highest)
    totals = jnp.sum(expo, axis=-1) + own_expo
    weights = (expo / totals[..., None]).astype(jnp.bfloat16)
    own_weight = (own_expo / totals).astype(jnp.bfloat16)
    mixed = jnp.einsum("shp,sphd->shd", weights, cached_values, preferred_element_type=jnp.float32)
    mixed = mixed + own_weight.astype(jnp.float32)[..., None] * values_new.astype(jnp.float32)
    mixed = mixed.astype(jnp.bfloat16).reshape(local_streams, local_cols)
    partial_rows = jnp.dot(mixed, temporal_out_weight, preferred_element_type=jnp.float32)
    slice_width = partial_rows.shape[1] // tp
    by_slice = partial_rows.reshape(local_streams, tp, slice_width).transpose(1, 0, 2)
    summed = scattered_sum(by_slice)
    tp_place = lax.axis_index("tp")
    resid_in = lax.dynamic_slice_in_dim(hidden_in, tp_place * slice_width, slice_width, 1)
    temporal = (resid_in.astype(jnp.float32) + summed).astype(jnp.bfloat16)
    all_rows = lax.all_gather(temporal, "section", axis=0, tiled=True)
    streams = all_rows.shape[0]
    codes = depth_in.shape[0]
    width = depth_in.shape[2]
    vocab_local = depth_embed.shape[1]
    first_id = tp_place * vocab_local
    onehot = (
        tokens[:, :, None] == first_id + jnp.arange(vocab_local, dtype=jnp.int32)[None, None, :]
    ).astype(jnp.bfloat16)
    embedded = jnp.einsum("scv,cve->cse", onehot, depth_embed, preferred_element_type=jnp.float32)
    entry_terms = embedded + jnp.einsum(
        "sd,cde->cse", all_rows, depth_in, preferred_element_type=jnp.float32
    )
    hidden_rows = head_weight.shape[1]
    hidden_start = tp_place * hidden_rows
    entry = scattered_sum(entry_terms.reshape(codes, streams, tp, hidden_rows).transpose(2, 0, 1, 3))
    own_gain = lax.dynamic_slice_in_dim(depth_gain, hidden_start, hidden_rows, 0)
    scaled = (entry * own_gain).astype(jnp.bfloat16)
    rows = gathered(scaled)
    plain = rows.astype(jnp.float32) / depth_gain.reshape(tp, 1, 1, hidden_rows)
    inv_rms = lax.rsqrt(jnp.sum(plain * plain, axis=(0, 3)) / width + EPSILON)
    dproj = jnp.einsum(
        "tcse,cntef->ncsf",
        rows,
        depth_qkv.reshape(codes, 3, tp, hidden_rows, -1),
        preferred_element_type=jnp.float32,
    )
    dproj = (dproj * inv_rms[None, :, :, None]).astype(jnp.bfloat16)
    prior = passed_along(dproj[1:], "section", 1)
    depth_cols = dproj.shape[3]
    head_part = min(depth_cols, DEPTH_HDIM)
    local_parts = depth_cols // head_part
    sharers = DEPTH_HDIM // head_part
    both = jnp.concatenate([prior, dproj[1:]], axis=1)
    all_keys = both[0].reshape(2 * codes, streams, local_parts, head_part)
    all_values = both[1].reshape(2 * codes, streams, local_parts, head_part)
    depth_queries = dproj[0].reshape(codes, streams, local_parts, head_part)
    depth_scores = jnp.sum(
        depth_queries[:, None].astype(jnp.float32) * all_keys[None].astype(jnp.float32), axis=-1
    )
    for level in range(sharers.bit_length() - 1):
        depth_scores = depth_scores + from_partner(depth_scores, "tp", level)
    depth_scores = depth_scores * (1.0 / math.sqrt(DEPTH_HDIM))
    section_place = lax.axis_index("section")
    query_pos = jnp.arange(codes, dtype=jnp.int32)[:, None]
    key_pos = jnp.arange(2 * codes, dtype=jnp.int32)[None, :]
    allowed = jnp.where(key_pos < codes, section_place > 0, key_pos - codes <= query_pos)
    depth_scores = jnp.where(allowed[:, :, None, None], depth_scores, -jnp.inf)
    depth_top = jnp.max(depth_scores, axis=1, keepdims=True)
    depth_expo = jnp.exp(depth_scores - depth_top)
    depth_weights = (depth_expo / jnp.sum(depth_expo, axis=1, keepdims=True)).astype(jnp.bfloat16)
    depth_mixed = jnp.sum(
        depth_weights[..., None].astype(jnp.float32) * all_values[None].astype(jnp.float32), axis=1
    ).astype(jnp.bfloat16)
    depth_mixed = depth_mixed.reshape(codes, streams, depth_cols)
    depth_terms = jnp.einsum(
        "csf,cfe->cse", depth_mixed, depth_out_weight, preferred_element_type=jnp.float32
    )
    added = scattered_sum(depth_terms.reshape(codes, streams, tp, hidden_rows).transpose(2, 0, 1, 3))
    resid = entry + added
    own_head_gain = lax.dynamic_slice_in_dim(head_gain, hidden_start, hidden_rows, 0)
    own_hidden = (resid * own_head_gain).astype(jnp.bfloat16)
    squares = jnp.sum(resid * resid, axis=2)
    high = squares.astype(jnp.bfloat16)
    low = (squares - high.astype(jnp.float32)).astype(jnp.bfloat16)
    partial_logits = jnp.einsum(
        "cse,cev->csv", own_hidden, head_weight, preferred_element_type=jnp.float32
    )
    vocab_slice = partial_logits.shape[2] // tp
    outgoing = partial_logits.reshape(codes, streams, tp, vocab_slice).transpose(2, 0, 1, 3)
    outgoing = outgoing.astype(jnp.bfloat16).reshape(tp, codes * streams, vocab_slice)
    extra = jnp.stack([high.reshape(-1), low.reshape(-1)])
    extra = jnp.pad(extra, ((0, 14), (0, 0))).reshape(-1, vocab_slice)
    packed = jnp.concatenate(
        [outgoing, jnp.broadcast_to(extra[None], (tp,) + extra.shape)], axis=1
    )
    moved = lax.all_to_all(packed, "tp", 0, 0).astype(jnp.float32)
    rows_total = jnp.sum(moved, axis=0)
    stats = rows_total[codes * streams :].reshape(16, codes, streams)
    head_inv = lax.rsqrt((stats[0] + stats[1]) / width + EPSILON)
    logits = rows_total[: codes * streams].reshape(codes, streams, vocab_slice) * head_inv[..., None]
    return (temporal, logits.transpose(1, 0, 2))


HBM = pl.BlockSpec(memory_space=pltpu.HBM)
VMEM = pl.BlockSpec(memory_space=pltpu.VMEM)
SMEM = pl.BlockSpec(memory_space=pltpu.SMEM)


def params(mebibytes):
    return pltpu.CompilerParams(vmem_limit_bytes=mebibytes * 1024 * 1024)


def in_hbm(array):
    return pltpu.with_memory_space_constraint(array, pltpu.HBM)


def shape(dims, dtype):
    return jax.ShapeDtypeStruct(dims, dtype)


def vmem(dims, dtype):
    return pltpu.VMEM(dims, dtype)


def product(left, right):
    return jnp.dot(left, right, preferred_element_type=jnp.float32)


def product_t(left, right):
    return lax.dot_general(left, right, (((1,), (1,)), ((), ())), preferred_element_type=jnp.float32)


def column_of(row):
    size = row.shape[1]
    first = lax.broadcasted_iota(jnp.int32, (size, size), 0)
    second = lax.broadcasted_iota(jnp.int32, (size, size), 1)
    return jnp.sum(jnp.where(first == second, row, 0.0), axis=1, keepdims=True)


IN_FLIGHT = 6
IN_FLIGHT_BESIDE = 6
CHUNKS = 1


class Stream:
    def __init__(self, copies, in_flight):
        self.copies = copies
        self.in_flight = in_flight
        self.done = 0
        for copy in copies[:in_flight]:
            copy.start()

    def arrived(self, upto):
        while self.done <= upto:
            self.copies[self.done].wait()
            if self.done + self.in_flight < len(self.copies):
                self.copies[self.done + self.in_flight].start()
            self.done += 1


def temporal_kernel(
    place_ref, hidden_hbm, gain_hbm, lengths_hbm, qkv_hbm, out_hbm, keys_hbm, values_hbm, kept_ref, last_ref, sent_ref,
    hidden_buf, gain_buf, lengths_buf, qkv_buf, out_buf, keys_buf, values_buf, small_sems, sems,
):
    streams, depth = hidden_buf.shape
    cols = qkv_buf.shape[2]
    heads = cols // HEAD_DIM
    cache_len = keys_buf.shape[1]
    steps, halves = QKV_STEPS, CACHE_STEPS
    chunk = depth // steps
    batch = streams // halves
    count, _, width = kept_ref.shape
    odd = place_ref[0] % 2
    place = place_ref[0] // 2
    small = [
        pltpu.make_async_copy(hidden_hbm, hidden_buf, small_sems.at[0]),
        pltpu.make_async_copy(gain_hbm, gain_buf, small_sems.at[1]),
        pltpu.make_async_copy(lengths_hbm, lengths_buf, small_sems.at[2]),
    ]
    for copy in small:
        copy.start()
    pairs = []
    for n in (0, 1):
        pairs += [(qkv_hbm.at[n, pl.ds(i * chunk, chunk)], qkv_buf.at[n, pl.ds(i * chunk, chunk)]) for i in range(steps)]
    pairs += [(keys_hbm.at[pl.ds(i * batch, batch)], keys_buf.at[pl.ds(i * batch, batch)]) for i in range(halves)]
    pairs += [(qkv_hbm.at[2, pl.ds(i * chunk, chunk)], qkv_buf.at[2, pl.ds(i * chunk, chunk)]) for i in range(steps)]
    pairs += [(values_hbm.at[pl.ds(i * batch, batch)], values_buf.at[pl.ds(i * batch, batch)]) for i in range(halves)]
    pairs += [
        (out_hbm.at[:, pl.ds(pl.multiple_of((place ^ k) * 2 * width, 2 * width), 2 * width)], out_buf.at[k])
        for k in range(count)
    ]
    stream = Stream([pltpu.make_async_copy(src, dst, sems.at[i]) for i, (src, dst) in enumerate(pairs)], IN_FLIGHT)
    first_of = (0, steps, 2 * steps + halves)
    keys_end = 2 * steps + halves - 1
    values_end = 3 * steps + 2 * halves - 1

    for copy in small:
        copy.wait()
    wide = hidden_buf[...].astype(jnp.float32)
    inv = lax.rsqrt(jnp.mean(wide * wide, axis=1, keepdims=True) + EPSILON)
    normed = (wide * inv * gain_buf[...]).astype(jnp.bfloat16)

    def projected(n):
        total = None
        for i in range(steps):
            stream.arrived(first_of[n] + i)
            part = product(normed[:, i * chunk : (i + 1) * chunk], qkv_buf[n, pl.ds(i * chunk, chunk), :])
            total = part if total is None else total + part
        return total

    lengths_row = lengths_buf[...].astype(jnp.float32)
    lengths_col = column_of(lengths_row)
    half = HEAD_DIM // 2
    lane = lax.broadcasted_iota(jnp.int32, (streams, HEAD_DIM), 1)
    spacing = (lane & (half - 1)).astype(jnp.float32) / half
    angles = lengths_col * jnp.exp(-math.log(10000.0) * spacing)
    cosine = jnp.cos(angles)
    sine = jnp.where(lane < half, -1.0, 1.0) * jnp.sin(angles)

    def rotated(block):
        pieces = []
        for h in range(heads):
            piece = block[:, h * HEAD_DIM : (h + 1) * HEAD_DIM]
            pieces.append(piece * cosine + pltpu.roll(piece, half, 1) * sine)
        return jnp.concatenate(pieces, axis=1)

    queries = rotated(projected(0))
    keys_new = rotated(projected(1)).astype(jnp.bfloat16)
    head_lane = lax.broadcasted_iota(jnp.int32, (streams, cols), 1) // HEAD_DIM
    spread = jnp.concatenate(
        [jnp.where(head_lane == h, queries, 0.0) for h in range(heads)], axis=0
    ).astype(jnp.bfloat16)
    pairs = heads * streams
    factor = 1.0 / math.sqrt(HEAD_DIM)
    pair = lax.broadcasted_iota(jnp.int32, (1, pairs), 1)
    pair_stream = pair % streams
    own = product_t(keys_new, spread) * factor
    stream_row = lax.broadcasted_iota(jnp.int32, (streams, pairs), 0)
    own_score = jnp.sum(jnp.where(stream_row == pair_stream, own, 0.0), axis=0, keepdims=True)
    tiled = jnp.sum(jnp.where(stream_row == pair_stream, lengths_col, 0.0), axis=0, keepdims=True)
    first_row = pair_stream * cache_len
    last_row = first_row + tiled.astype(jnp.int32)
    stream.arrived(keys_end)
    rows = streams * cache_len
    scores = product_t(keys_buf[...].reshape(rows, cols), spread) * factor
    row = lax.broadcasted_iota(jnp.int32, (rows, pairs), 0)
    scores = jnp.where((row >= first_row) & (row < last_row), scores, -jnp.inf)
    highest = jnp.maximum(jnp.max(scores, axis=0, keepdims=True), own_score)
    expo = jnp.exp(scores - highest)
    own_expo = jnp.exp(own_score - highest)
    inverse = 1.0 / (jnp.sum(expo, axis=0, keepdims=True) + own_expo)
    weights = (expo * inverse).astype(jnp.bfloat16)
    own_weight = (own_expo * inverse).astype(jnp.bfloat16).astype(jnp.float32)
    values_new = projected(2).astype(jnp.bfloat16).astype(jnp.float32)
    stream.arrived(values_end)
    mixed_all = lax.dot_general(
        weights,
        values_buf[...].reshape(rows, cols),
        (((0,), (0,)), ((), ())),
        preferred_element_type=jnp.float32,
    )
    pair_lane = lax.broadcasted_iota(jnp.int32, (streams, pairs), 1)
    pair_row = lax.broadcasted_iota(jnp.int32, (streams, pairs), 0)
    mixed = []
    for h in range(heads):
        own_col = jnp.sum(
            jnp.where(pair_lane == pair_row + h * streams, own_weight, 0.0), axis=1, keepdims=True
        )
        lanes = slice(h * HEAD_DIM, (h + 1) * HEAD_DIM)
        mixed.append(
            mixed_all[h * streams : (h + 1) * streams, lanes] + own_col * values_new[:, lanes]
        )
    mixed = jnp.concatenate(mixed, axis=1).astype(jnp.bfloat16)
    for k in range(count):
        stream.arrived(values_end + 1 + k)
        block = product(mixed, out_buf[k])
        even_side, odd_side = block[:, :width], block[:, width:]
        kept_ref[k] = jnp.where(odd == 1, odd_side, even_side)
        sent = jnp.where(odd == 1, even_side, odd_side).astype(jnp.bfloat16)
        if k == 0:
            last_ref[...] = sent
        else:
            sent_ref[k - 1] = sent


QKV_STEPS = 4
CACHE_STEPS = 2


def temporal_parts(place, hidden_in, gain, lengths, qkv, out_weight, keys, values, places):
    streams, depth = hidden_in.shape
    bf16 = jnp.bfloat16
    count, width = places // 2, out_weight.shape[1] // places
    block = (count, streams, width)
    return pl.pallas_call(
        temporal_kernel,
        in_specs=[SMEM] + [HBM] * 7,
        out_specs=[VMEM] * 3,
        out_shape=[vmem(block, jnp.float32), vmem(block[1:], bf16), vmem((count - 1,) + block[1:], bf16)],
        scratch_shapes=[
            pltpu.VMEM(hidden_in.shape, bf16),
            pltpu.VMEM((1, depth), jnp.float32),
            pltpu.VMEM((1, streams), jnp.int32),
            pltpu.VMEM(qkv.shape, bf16),
            pltpu.VMEM((count, out_weight.shape[0], 2 * width), bf16),
            pltpu.VMEM(keys.shape, bf16),
            pltpu.VMEM(values.shape, bf16),
            pltpu.SemaphoreType.DMA((3,)),
            pltpu.SemaphoreType.DMA((3 * QKV_STEPS + 2 * CACHE_STEPS + count,)),
        ],
        compiler_params=params(30),
        name="temporal",
    )(
        place,
        in_hbm(hidden_in),
        in_hbm(gain.reshape(1, depth)),
        in_hbm(lengths.reshape(1, streams)),
        in_hbm(qkv),
        in_hbm(out_weight),
        in_hbm(keys),
        in_hbm(values),
    )


def prepare_kernel(
    place_ref, tokens_ref, hidden_hbm, embed_hbm, weight_hbm, resid_ref, embedded_ref, weight_ref, embed_buf, sem, sems
):
    codes, vocab, _ = embed_buf.shape
    streams = tokens_ref.shape[0]
    part = resid_ref.shape[1]
    start = pl.multiple_of(place_ref[0] * part, part)
    resid = pltpu.make_async_copy(hidden_hbm.at[:, pl.ds(start, part)], resid_ref, sem)
    resid.start()
    embed = [pltpu.make_async_copy(embed_hbm.at[c], embed_buf.at[c], sems.at[0, c]) for c in range(codes)]
    weight = [pltpu.make_async_copy(weight_hbm.at[c], weight_ref.at[c], sems.at[1, c]) for c in range(codes)]
    stream = Stream(embed + weight, IN_FLIGHT_BESIDE)
    vocab_lane = lax.broadcasted_iota(jnp.int32, (streams, vocab), 1) + place_ref[0] * vocab
    for c in range(codes):
        hit = tokens_ref[:, c : c + 1] == vocab_lane
        onehot = jnp.where(hit, 1.0, 0.0).astype(jnp.bfloat16)
        stream.arrived(c)
        embedded_ref[c] = product(onehot, embed_buf[c])
    stream.arrived(2 * codes - 1)
    resid.wait()


def prepared_entry(place, tokens, hidden_in, embed, weight, places):
    codes, _, width = weight.shape
    streams = tokens.shape[0]
    resid_shape = (hidden_in.shape[0], hidden_in.shape[1] // places)
    return pl.pallas_call(
        prepare_kernel,
        in_specs=[SMEM, VMEM, HBM, HBM, HBM],
        out_specs=[VMEM] * 3,
        out_shape=[
            vmem(resid_shape, jnp.bfloat16),
            vmem((codes, streams, width), jnp.float32),
            vmem(weight.shape, jnp.bfloat16),
        ],
        scratch_shapes=[
            pltpu.VMEM(embed.shape, jnp.bfloat16),
            pltpu.SemaphoreType.DMA(()),
            pltpu.SemaphoreType.DMA((2, codes)),
        ],
        compiler_params=params(16),
        name="entry_prepare",
    )(place, tokens, in_hbm(hidden_in), in_hbm(embed), in_hbm(weight))


def near_kernel(place_ref, token_ref, gain_ref, qkv_hbm, out_hbm, own_ref, qkv_ref, out_ref, sems):
    del token_ref
    copies = [
        pltpu.make_async_copy(source.at[c], target.at[c], sems.at[i, c])
        for i, (source, target) in enumerate(((qkv_hbm, qkv_ref), (out_hbm, out_ref)))
        for c in range(source.shape[0])
    ]
    stream = Stream(copies, IN_FLIGHT_BESIDE)
    part = own_ref.shape[1]
    own_ref[...] = gain_ref[:, pl.ds(pl.multiple_of(place_ref[0] * part, part), part)]
    stream.arrived(len(copies) - 1)


def brought_near(place, token, gain, qkv, out_weight, places):
    width = gain.shape[0]
    return pl.pallas_call(
        near_kernel,
        in_specs=[SMEM, VMEM, VMEM, HBM, HBM],
        out_specs=[VMEM] * 3,
        out_shape=[
            vmem((1, width // places), jnp.float32),
            vmem(qkv.shape, jnp.bfloat16),
            vmem(out_weight.shape, jnp.bfloat16),
        ],
        scratch_shapes=[pltpu.SemaphoreType.DMA((2, qkv.shape[0]))],
        compiler_params=params(16),
        name="brought_near",
    )(place, token, gain.reshape(1, width), in_hbm(qkv), in_hbm(out_weight))


def split_kernel(place_ref, head_hbm, far_ref, *rest):
    outs, sems = rest[:-1], rest[-1]
    count, half, _, part = far_ref.shape
    each = outs[0].shape[1]
    odd = place_ref[0] % 2
    place = place_ref[0] // 2
    blocks = [(far_ref, place_ref[2] * half, half, 1 - odd)]
    blocks += [(out, n * each, each, odd) for n, out in enumerate(outs)]
    copies = []
    for n, (out, first, size, side) in enumerate(blocks):
        for k in range(count):
            start = pl.multiple_of(((place ^ k) * 2 + side) * part, part)
            copies.append(
                pltpu.make_async_copy(
                    head_hbm.at[pl.ds(first, size), :, pl.ds(start, part)], out.at[k], sems.at[n, k]
                )
            )
    for copy in copies:
        copy.start()
    for copy in copies:
        copy.wait()


def split_columns(place, weight, places):
    codes, depth, vocab = weight.shape

    def block(size):
        return vmem((places // 2, size, depth, vocab // places), jnp.bfloat16)

    return pl.pallas_call(
        split_kernel,
        in_specs=[SMEM, HBM],
        out_specs=[VMEM] * (1 + CHUNKS),
        out_shape=[block(codes // 2)] + [block(codes // CHUNKS)] * CHUNKS,
        scratch_shapes=[pltpu.SemaphoreType.DMA((1 + CHUNKS, places // 2))],
        compiler_params=params(16),
        name="split_columns",
    )(place, in_hbm(weight))


def entry_kernel(place_ref, own_ref, other_ref, embedded_ref, weight_ref, after_ref, kept_ref, last_ref, sent_ref, token_ref, total_buf):
    del after_ref
    token_ref[...] = jnp.zeros_like(token_ref)
    codes = weight_ref.shape[0]
    count, _, _, part = kept_ref.shape
    odd = place_ref[0] % 2
    place = place_ref[0] // 2
    first_section = place_ref[1] == 0
    own, other = own_ref[...], other_ref[...]
    rows = jnp.concatenate(
        [jnp.where(first_section, own, other), jnp.where(first_section, other, own)], axis=0
    )
    for c in range(codes):
        total_buf[...] = embedded_ref[c] + product(rows, weight_ref[c])
        for k in range(count):
            pair = (place ^ k) * 2
            kept_ref[k, c] = total_buf[:, pl.ds(pl.multiple_of((pair + odd) * part, part), part)]
            sent = total_buf[:, pl.ds(pl.multiple_of((pair + 1 - odd) * part, part), part)].astype(jnp.bfloat16)
            if k == 0:
                last_ref[c] = sent
            else:
                sent_ref[k - 1, c] = sent


def entry_parts(place, own, other, embedded, weight, after, places):
    codes, _, width = weight.shape
    streams = 2 * own.shape[0]
    block = (places // 2, codes, streams, width // places)
    return pl.pallas_call(
        entry_kernel,
        in_specs=[SMEM] + [VMEM] * 5,
        out_specs=[VMEM] * 4,
        out_shape=[
            vmem(block, jnp.float32),
            vmem(block[1:], jnp.bfloat16),
            vmem((places // 2 - 1,) + block[1:], jnp.bfloat16),
            vmem((8, 128), jnp.float32),
        ],
        scratch_shapes=[pltpu.VMEM((streams, width), jnp.float32)],
        compiler_params=params(16),
        name="entry",
    )(place, own, other, embedded, weight, after)


def qkv_kernel(count, place_ref, gain_ref, weight_ref, far_ref, *rest):
    near_refs, (last_ref, queries_ref, pair_ref) = rest[:count], rest[count:]
    codes, _, width, cols = weight_ref.shape
    part = last_ref.shape[2]
    odd = place_ref[0] % 2
    place = place_ref[0] // 2
    starts = [
        pl.multiple_of(((place ^ k) * 2 + side) * part, part) for side in (odd, 1 - odd) for k in range(count)
    ]
    inverse_gain = 1.0 / jnp.concatenate([gain_ref[:, pl.ds(start, part)] for start in starts], axis=1)
    for c in range(codes):
        blocks = [ref[c] for ref in near_refs] + [last_ref[c]] + [far_ref[k, c] for k in range(count - 1)]
        row = jnp.concatenate(blocks, axis=1)
        plain = row.astype(jnp.float32) * inverse_gain
        inv = lax.rsqrt(jnp.sum(plain * plain, axis=1, keepdims=True) / width + EPSILON)
        for n in range(3):
            weight = jnp.concatenate([weight_ref[c, n, pl.ds(start, part), :] for start in starts], axis=0)
            value = (product(row, weight) * inv).astype(jnp.bfloat16)
            if n == 0:
                queries_ref[c] = value
            else:
                pair_ref[n - 1, c] = value


def depth_projections(place, near, last, far, gain, weight):
    codes, _, width, cols = weight.shape
    streams = last.shape[1]
    bf16 = jnp.bfloat16
    return pl.pallas_call(
        functools.partial(qkv_kernel, len(near)),
        in_specs=[SMEM] + [VMEM] * (4 + len(near)),
        out_specs=[VMEM] * 2,
        out_shape=[vmem((codes, streams, cols), bf16), vmem((2, codes, streams, cols), bf16)],
        compiler_params=params(16),
        name="depth_qkv",
    )(place, gain.reshape(1, width), weight, far, *near, last)


def mix_kernel(terms, place_ref, queries_ref, own_ref, prior_ref, weight_ref, *rest):
    entry_refs, outs, total_buf = rest[:terms], rest[terms:-1], rest[-1]
    codes, streams, cols = queries_ref.shape
    each, _, span = outs[0].shape
    count = len(outs) // CHUNKS
    has_prior = place_ref[1] > 0
    first = lax.broadcasted_iota(jnp.int32, (2 * cols, cols), 0) % cols
    second = lax.broadcasted_iota(jnp.int32, (2 * cols, cols), 1)
    same = jnp.where(first // DEPTH_HDIM == second // DEPTH_HDIM, 1.0, 0.0).astype(jnp.bfloat16)
    keys = [prior_ref[0, j].astype(jnp.float32) for j in range(codes)]
    keys += [own_ref[0, j].astype(jnp.float32) for j in range(codes)]
    values = [prior_ref[1, j].astype(jnp.float32) for j in range(codes)]
    values += [own_ref[1, j].astype(jnp.float32) for j in range(codes)]
    factor = 1.0 / math.sqrt(DEPTH_HDIM)
    mixed = []
    for q in range(codes):
        query = queries_ref[q].astype(jnp.float32)
        reach = codes + q + 1
        pieces = []
        for j in range(reach):
            exact = query * keys[j]
            high = exact.astype(jnp.bfloat16)
            low = (exact - high.astype(jnp.float32)).astype(jnp.bfloat16)
            pieces.append(jnp.concatenate([high, low], axis=1))
        scores = product(jnp.concatenate(pieces, axis=0), same) * factor
        score = [scores[j * streams : (j + 1) * streams] for j in range(reach)]
        score = [jnp.where(has_prior, s, -jnp.inf) if j < codes else s for j, s in enumerate(score)]
        top = score[0]
        for s in score[1:]:
            top = jnp.maximum(top, s)
        expo = [jnp.exp(s - top) for s in score]
        inverse = 1.0 / sum(expo)
        total = jnp.zeros_like(query)
        for j in range(reach):
            total = total + (expo[j] * inverse).astype(jnp.bfloat16).astype(jnp.float32) * values[j]
        mixed.append(total.astype(jnp.bfloat16))
    for q in range(codes):
        total_buf[q] = product(mixed[q], weight_ref[q])
    part = entry_refs[0].shape[2]
    own_part = pl.ds(pl.multiple_of(place_ref[0] * part, part), part)
    total_buf[:, :, own_part] += sum(ref[...].astype(jnp.float32) for ref in entry_refs)
    place = place_ref[0] // 2
    for n, out in enumerate(outs):
        chunk, k = divmod(n, count)
        start = pl.multiple_of((place ^ k) * span, span)
        block = total_buf[pl.ds(chunk * each, each), :, pl.ds(start, span)]
        out[...] = block if k == 0 else block.astype(jnp.bfloat16)


def mixed_parts(place, queries, own, prior, weight, entry_terms, far):
    codes, streams, cols = queries.shape
    width = weight.shape[2]
    block = (codes // CHUNKS, streams, width // (far + 1))
    outs = pl.pallas_call(
        functools.partial(mix_kernel, len(entry_terms)),
        in_specs=[SMEM] + [VMEM] * (4 + len(entry_terms)),
        out_specs=[VMEM] * ((far + 1) * CHUNKS),
        out_shape=([vmem(block, jnp.float32)] + [vmem(block, jnp.bfloat16)] * far) * CHUNKS,
        scratch_shapes=[pltpu.VMEM((codes, streams, width), jnp.float32)],
        compiler_params=params(16),
        name="depth_mix",
    )(place, queries, own, prior, weight, *entry_terms)
    return [outs[n * (far + 1) : (n + 1) * (far + 1)] for n in range(CHUNKS)]


STAT_ROWS = 16


def head_kernel(
    first, place_ref, gain_ref, total_ref, arrived_ref, weight_ref, early_ref, late_ref, kept_ref, stat_ref, *sends
):
    half = early_ref.shape[1]

    def partner(k, c):
        side, index = divmod(first + c, half)
        return jnp.where(place_ref[2] == side, early_ref[k, index], late_ref[k, index])

    codes, streams, span = total_ref.shape
    count, _, depth, part = weight_ref.shape
    odd = place_ref[0] % 2
    resid = total_ref[...] + arrived_ref[...].astype(jnp.float32)
    flat = resid.reshape(codes * streams, span)
    squares = flat * flat
    stat = product_t(jnp.ones((STAT_ROWS // 2, span), jnp.float32), squares)[:1]
    stat_ref[...] = stat
    high = stat.astype(jnp.bfloat16).astype(jnp.float32)
    stat_row = lax.broadcasted_iota(jnp.int32, (STAT_ROWS, codes * streams), 0)
    stat_block = jnp.where(stat_row == 0, high, jnp.where(stat_row == 1, stat - high, 0.0))
    if part > codes * streams:
        rest = jnp.zeros((STAT_ROWS, part - codes * streams), jnp.float32)
        stat_block = jnp.concatenate([stat_block, rest], axis=1)
    stat_block = stat_block.astype(jnp.bfloat16)
    scaled = resid * gain_ref[...]
    low_half, high_half = scaled[:, :, :depth], scaled[:, :, depth:]
    ordered = jnp.concatenate(
        [jnp.where(odd == 1, high_half, low_half), jnp.where(odd == 1, low_half, high_half)], axis=2
    ).astype(jnp.bfloat16)
    rows = codes * streams
    for k in range(count):
        block = jnp.concatenate(
            [
                product(ordered[c], jnp.concatenate([weight_ref[k, c], partner(k, c)], axis=0))
                for c in range(codes)
            ],
            axis=0,
        )
        if k == 0:
            kept_ref[...] = block
        else:
            sends[k - 1][pl.ds(0, rows), :] = block.astype(jnp.bfloat16)
            sends[k - 1][pl.ds(rows, STAT_ROWS), :] = stat_block


def head_parts(first, place, gain, total, arrived, weight, early, late):
    codes, streams, span = total.shape
    count, _, depth, part = weight.shape
    rows = codes * streams
    return pl.pallas_call(
        functools.partial(head_kernel, first),
        in_specs=[SMEM] + [VMEM] * 6,
        out_specs=[VMEM] * (count + 1),
        out_shape=[vmem((rows, part), jnp.float32), vmem((1, rows), jnp.float32)]
        + [vmem((rows + STAT_ROWS, part), jnp.bfloat16)] * (count - 1),
        compiler_params=params(16),
        name="head",
    )(place, gain, total, arrived, weight, early, late)


def logits_kernel(width, *refs):
    out_ref = refs[-1]
    streams, codes, part = out_ref.shape
    each = codes // CHUNKS
    rows = each * streams
    count = (len(refs) - 1) // CHUNKS
    for n in range(CHUNKS):
        kept_ref, stat_ref, *arrived = refs[n * count : (n + 1) * count]
        total = kept_ref[...]
        stat = stat_ref[...]
        for block in arrived:
            wide = block[...].astype(jnp.float32)
            total = total + wide[:rows]
            stat = stat + wide[rows : rows + 1, :rows] + wide[rows + 1 : rows + 2, :rows]
        total = total * column_of(lax.rsqrt(stat / width + EPSILON))
        for c in range(each):
            out_ref[:, n * each + c, :] = total[c * streams : (c + 1) * streams]


def finished_logits(chunks, streams, codes, width):
    part = chunks[0][0].shape[1]
    arrays = [array for chunk in chunks for array in chunk]
    return pl.pallas_call(
        functools.partial(logits_kernel, width),
        in_specs=[VMEM] * len(arrays),
        out_specs=VMEM,
        out_shape=shape((streams, codes, part), jnp.float32),
        compiler_params=params(16),
        name="logits",
    )(*arrays)


def paired_device(
    hidden_in,
    temporal_gain,
    temporal_qkv,
    temporal_out_weight,
    cache_keys,
    cache_values,
    lengths,
    depth_in,
    depth_embed,
    depth_gain,
    depth_qkv,
    depth_out_weight,
    head_gain,
    head_weight,
    tokens,
):
    tp = lax.axis_size("tp")
    tp_place = lax.axis_index("tp")
    place = jnp.stack([tp_place, lax.axis_index("section"), lax.axis_index("grp") % 2])
    far = tp // 2 - 1

    def to_pairs(blocks):
        arrived = [None] * len(blocks)
        for k in reversed(range(len(blocks))):
            arrived[k] = lax.ppermute(blocks[k], "tp", [(i, i ^ 2 * (k + 1)) for i in range(tp)])
        return arrived

    def to_neighbour(block):
        return lax.ppermute(block, "tp", [(i, i ^ 1) for i in range(tp)])

    def summed(kept, last, sent):
        folded = kept[1:] + to_neighbour(sent).astype(jnp.float32)
        arrived = to_pairs([folded[k].astype(jnp.bfloat16) for k in range(far)])
        return [kept[0]] + arrived + [to_neighbour(last)]

    def added(terms):
        return sum(term.astype(jnp.float32) for term in terms)

    kept, last, sent = temporal_parts(
        place, hidden_in, temporal_gain, lengths, temporal_qkv, temporal_out_weight, cache_keys, cache_values, tp
    )
    sent, depth_in, head_weight = lax.optimization_barrier((sent, depth_in, head_weight))
    neighbour_columns, *own_columns = split_columns(place, head_weight, tp)
    early = to_neighbour(neighbour_columns)
    resid_in, embedded, near_in = prepared_entry(place, tokens, hidden_in, depth_embed, depth_in, tp)
    temporal = (resid_in.astype(jnp.float32) + added(summed(kept, last, sent))).astype(jnp.bfloat16)
    other_rows = lax.ppermute(temporal, "section", [(0, 1), (1, 0)])
    codes = depth_in.shape[0]
    width = depth_in.shape[2]
    hidden_rows = head_weight.shape[1]
    kept, last, sent, token = entry_parts(place, temporal, other_rows, embedded, near_in, early, tp)
    late = lax.ppermute(early, "grp", [(i, i ^ 1) for i in range(lax.axis_size("grp"))])
    own_gain, near_qkv, near_out = brought_near(place, token, depth_gain, depth_qkv, depth_out_weight, tp)
    entry_terms = summed(kept, last, sent)
    scaled = (added(entry_terms) * own_gain[None]).astype(jnp.bfloat16)
    near = [scaled] + to_pairs([scaled] * far)
    last = to_neighbour(scaled)
    queries, own_pair = depth_projections(
        place, near, last, to_neighbour(jnp.stack(near[1:])), depth_gain, near_qkv
    )
    prior_pair = passed_along(own_pair, "section", 1)
    chunks = mixed_parts(place, queries, own_pair, prior_pair, near_out, entry_terms, far)
    pair_gain = lax.dynamic_slice_in_dim(head_gain, tp_place // 2 * 2 * hidden_rows, 2 * hidden_rows, 0)
    each = codes // CHUNKS
    arrived = [to_pairs(blocks) for _, *blocks in chunks]
    totals = [
        kept + added(blocks) for (kept, *_), blocks in zip(chunks, arrived)
    ]
    others = [to_neighbour(total.astype(jnp.bfloat16)) for total in totals]
    heads = [
        head_parts(n * each, place, pair_gain.reshape(1, 1, -1), total, other, own, early, late)
        for n, (total, other, own) in enumerate(zip(totals, others, own_columns))
    ]
    finished = [[kept, stat, *to_pairs(blocks)] for kept, stat, *blocks in heads]
    logits = finished_logits(finished, sent.shape[2], codes, width)
    return (temporal, logits)


def per_device(*arrays):
    hidden_in, temporal_qkv, depth_qkv, head_weight = arrays[0], arrays[2], arrays[10], arrays[13]
    depth_in, tokens = arrays[7], arrays[14]
    tp = lax.axis_size("tp")
    pairs = hidden_in.shape[0] * (temporal_qkv.shape[2] // HEAD_DIM)
    whole_tiles = (
        pairs % 128 == 0
        and temporal_qkv.shape[2] % HEAD_DIM == 0
        and head_weight.shape[1] % 128 == 0
        and head_weight.shape[2] // tp % 128 == 0
        and depth_qkv.shape[3] % 128 == 0
        and tp >= 4
        and depth_in.shape[0] % (2 * CHUNKS) == 0
        and lax.axis_size("grp") % 2 == 0
        and depth_in.shape[0] // CHUNKS * tokens.shape[0] <= head_weight.shape[2] // tp
        and tp & (tp - 1) == 0
    )
    return (paired_device if whole_tiles else general_device)(*arrays)


def solution(mesh):
    return jax.shard_map(
        per_device,
        mesh=mesh,
        in_specs=(
            P(("grp", "section"), None),
            P(),
            P(None, None, "tp"),
            P("tp", None),
            P(("grp", "section"), None, "tp"),
            P(("grp", "section"), None, "tp"),
            P(("grp", "section")),
            P("section", "tp", None),
            P("section", "tp", None),
            P(),
            P("section", None, None, "tp"),
            P("section", "tp", None),
            P(),
            P("section", "tp", None),
            P("grp", "section"),
        ),
        out_specs=(P(("grp", "section"), "tp"), P("grp", "section", "tp")),
        check_vma=False,
    )
```

```python
import functools
import math

import jax
import jax.numpy as jnp
from jax import lax
from jax.experimental import pallas as pl
from jax.experimental.pallas import tpu as pltpu
from jax.sharding import PartitionSpec as P

HEAD_DIM = 128
DEPTH_HDIM = 64


EPSILON = 1e-05


def passed_along(block, axis, distance):
    devices = range(lax.axis_size(axis))
    route = [(i - distance, i) for i in devices if i - distance in devices]
    return lax.ppermute(block, axis, route)


def from_partner(shard, axis, distance):
    return lax.ppermute(shard, axis, [(i, i ^ 1 << distance) for i in range(lax.axis_size(axis))])


def rms_norm(values, scale):
    wide = values.astype(jnp.float32)
    return wide * lax.rsqrt(jnp.mean(wide * wide, axis=-1, keepdims=True) + EPSILON) * scale


def rotate(vectors, positions):
    halfdim = vectors.shape[-1] // 2
    spacing = jnp.arange(halfdim, dtype=jnp.float32) / halfdim
    inverse = jnp.exp(-math.log(10000.0) * spacing)
    angles = positions.astype(jnp.float32)[:, None, None] * inverse[None, None, :]
    cosine = jnp.cos(angles)
    sine = jnp.sin(angles)
    first = vectors[..., :halfdim]
    second = vectors[..., halfdim:]
    return jnp.concatenate(
        [first * cosine - second * sine, first * sine + second * cosine], axis=-1
    )


def scattered_sum(parts):
    moved = lax.all_to_all(parts.astype(jnp.bfloat16), "tp", 0, 0)
    return jnp.sum(moved.astype(jnp.float32), axis=0)


def gathered(block):
    size = lax.axis_size("tp")
    return lax.all_to_all(jnp.broadcast_to(block[None], (size,) + block.shape), "tp", 0, 0)


def general_device(
    hidden_in,
    temporal_gain,
    temporal_qkv,
    temporal_out_weight,
    cache_keys,
    cache_values,
    lengths,
    depth_in,
    depth_embed,
    depth_gain,
    depth_qkv,
    depth_out_weight,
    head_gain,
    head_weight,
    tokens,
):
    tp = lax.axis_size("tp")
    local_streams = hidden_in.shape[0]
    local_cols = temporal_qkv.shape[2]
    local_heads = local_cols // HEAD_DIM
    cache_len = cache_keys.shape[1]
    normed = rms_norm(hidden_in, temporal_gain).astype(jnp.bfloat16)
    projected = jnp.einsum("sd,tdf->tsf", normed, temporal_qkv, preferred_element_type=jnp.float32)
    layout = (local_streams, local_heads, HEAD_DIM)
    queries = rotate(projected[0].reshape(layout), lengths).astype(jnp.bfloat16)
    keys_new = rotate(projected[1].reshape(layout), lengths).astype(jnp.bfloat16)
    values_new = projected[2].reshape(layout).astype(jnp.bfloat16)
    cached_keys = cache_keys.reshape(local_streams, cache_len, local_heads, HEAD_DIM)
    cached_values = cache_values.reshape(local_streams, cache_len, local_heads, HEAD_DIM)
    factor = 1.0 / math.sqrt(HEAD_DIM)
    scores = (
        jnp.einsum("shd,sphd->shp", queries, cached_keys, preferred_element_type=jnp.float32)
        * factor
    )
    own_score = (
        jnp.sum(queries.astype(jnp.float32) * keys_new.astype(jnp.float32), axis=-1) * factor
    )
    valid = jnp.arange(cache_len, dtype=jnp.int32)[None, None, :] < lengths[:, None, None]
    scores = jnp.where(valid, scores, -jnp.inf)
    highest = jnp.maximum(jnp.max(scores, axis=-1), own_score)
    expo = jnp.exp(scores - highest[..., None])
    own_expo = jnp.exp(own_score - highest)
    totals = jnp.sum(expo, axis=-1) + own_expo
    weights = (expo / totals[..., None]).astype(jnp.bfloat16)
    own_weight = (own_expo / totals).astype(jnp.bfloat16)
    mixed = jnp.einsum("shp,sphd->shd", weights, cached_values, preferred_element_type=jnp.float32)
    mixed = mixed + own_weight.astype(jnp.float32)[..., None] * values_new.astype(jnp.float32)
    mixed = mixed.astype(jnp.bfloat16).reshape(local_streams, local_cols)
    partial_rows = jnp.dot(mixed, temporal_out_weight, preferred_element_type=jnp.float32)
    slice_width = partial_rows.shape[1] // tp
    by_slice = partial_rows.reshape(local_streams, tp, slice_width).transpose(1, 0, 2)
    summed = scattered_sum(by_slice)
    tp_place = lax.axis_index("tp")
    resid_in = lax.dynamic_slice_in_dim(hidden_in, tp_place * slice_width, slice_width, 1)
    temporal = (resid_in.astype(jnp.float32) + summed).astype(jnp.bfloat16)
    all_rows = lax.all_gather(temporal, "section", axis=0, tiled=True)
    streams = all_rows.shape[0]
    codes = depth_in.shape[0]
    width = depth_in.shape[2]
    vocab_local = depth_embed.shape[1]
    first_id = tp_place * vocab_local
    onehot = (
        tokens[:, :, None] == first_id + jnp.arange(vocab_local, dtype=jnp.int32)[None, None, :]
    ).astype(jnp.bfloat16)
    embedded = jnp.einsum("scv,cve->cse", onehot, depth_embed, preferred_element_type=jnp.float32)
    entry_terms = embedded + jnp.einsum(
        "sd,cde->cse", all_rows, depth_in, preferred_element_type=jnp.float32
    )
    hidden_rows = head_weight.shape[1]
    hidden_start = tp_place * hidden_rows
    entry = scattered_sum(entry_terms.reshape(codes, streams, tp, hidden_rows).transpose(2, 0, 1, 3))
    own_gain = lax.dynamic_slice_in_dim(depth_gain, hidden_start, hidden_rows, 0)
    scaled = (entry * own_gain).astype(jnp.bfloat16)
    rows = gathered(scaled)
    plain = rows.astype(jnp.float32) / depth_gain.reshape(tp, 1, 1, hidden_rows)
    inv_rms = lax.rsqrt(jnp.sum(plain * plain, axis=(0, 3)) / width + EPSILON)
    dproj = jnp.einsum(
        "tcse,cntef->ncsf",
        rows,
        depth_qkv.reshape(codes, 3, tp, hidden_rows, -1),
        preferred_element_type=jnp.float32,
    )
    dproj = (dproj * inv_rms[None, :, :, None]).astype(jnp.bfloat16)
    prior = passed_along(dproj[1:], "section", 1)
    depth_cols = dproj.shape[3]
    head_part = min(depth_cols, DEPTH_HDIM)
    local_parts = depth_cols // head_part
    sharers = DEPTH_HDIM // head_part
    both = jnp.concatenate([prior, dproj[1:]], axis=1)
    all_keys = both[0].reshape(2 * codes, streams, local_parts, head_part)
    all_values = both[1].reshape(2 * codes, streams, local_parts, head_part)
    depth_queries = dproj[0].reshape(codes, streams, local_parts, head_part)
    depth_scores = jnp.sum(
        depth_queries[:, None].astype(jnp.float32) * all_keys[None].astype(jnp.float32), axis=-1
    )
    for level in range(sharers.bit_length() - 1):
        depth_scores = depth_scores + from_partner(depth_scores, "tp", level)
    depth_scores = depth_scores * (1.0 / math.sqrt(DEPTH_HDIM))
    section_place = lax.axis_index("section")
    query_pos = jnp.arange(codes, dtype=jnp.int32)[:, None]
    key_pos = jnp.arange(2 * codes, dtype=jnp.int32)[None, :]
    allowed = jnp.where(key_pos < codes, section_place > 0, key_pos - codes <= query_pos)
    depth_scores = jnp.where(allowed[:, :, None, None], depth_scores, -jnp.inf)
    depth_top = jnp.max(depth_scores, axis=1, keepdims=True)
    depth_expo = jnp.exp(depth_scores - depth_top)
    depth_weights = (depth_expo / jnp.sum(depth_expo, axis=1, keepdims=True)).astype(jnp.bfloat16)
    depth_mixed = jnp.sum(
        depth_weights[..., None].astype(jnp.float32) * all_values[None].astype(jnp.float32), axis=1
    ).astype(jnp.bfloat16)
    depth_mixed = depth_mixed.reshape(codes, streams, depth_cols)
    depth_terms = jnp.einsum(
        "csf,cfe->cse", depth_mixed, depth_out_weight, preferred_element_type=jnp.float32
    )
    added = scattered_sum(depth_terms.reshape(codes, streams, tp, hidden_rows).transpose(2, 0, 1, 3))
    resid = entry + added
    own_head_gain = lax.dynamic_slice_in_dim(head_gain, hidden_start, hidden_rows, 0)
    own_hidden = (resid * own_head_gain).astype(jnp.bfloat16)
    squares = jnp.sum(resid * resid, axis=2)
    high = squares.astype(jnp.bfloat16)
    low = (squares - high.astype(jnp.float32)).astype(jnp.bfloat16)
    partial_logits = jnp.einsum(
        "cse,cev->csv", own_hidden, head_weight, preferred_element_type=jnp.float32
    )
    vocab_slice = partial_logits.shape[2] // tp
    outgoing = partial_logits.reshape(codes, streams, tp, vocab_slice).transpose(2, 0, 1, 3)
    outgoing = outgoing.astype(jnp.bfloat16).reshape(tp, codes * streams, vocab_slice)
    extra = jnp.stack([high.reshape(-1), low.reshape(-1)])
    extra = jnp.pad(extra, ((0, 14), (0, 0))).reshape(-1, vocab_slice)
    packed = jnp.concatenate(
        [outgoing, jnp.broadcast_to(extra[None], (tp,) + extra.shape)], axis=1
    )
    moved = lax.all_to_all(packed, "tp", 0, 0).astype(jnp.float32)
    rows_total = jnp.sum(moved, axis=0)
    stats = rows_total[codes * streams :].reshape(16, codes, streams)
    head_inv = lax.rsqrt((stats[0] + stats[1]) / width + EPSILON)
    logits = rows_total[: codes * streams].reshape(codes, streams, vocab_slice) * head_inv[..., None]
    return (temporal, logits.transpose(1, 0, 2))


HBM = pl.BlockSpec(memory_space=pltpu.HBM)
VMEM = pl.BlockSpec(memory_space=pltpu.VMEM)
SMEM = pl.BlockSpec(memory_space=pltpu.SMEM)


def params(mebibytes):
    return pltpu.CompilerParams(vmem_limit_bytes=mebibytes * 1024 * 1024)


def in_hbm(array):
    return pltpu.with_memory_space_constraint(array, pltpu.HBM)


def shape(dims, dtype):
    return jax.ShapeDtypeStruct(dims, dtype)


def vmem(dims, dtype):
    return pltpu.VMEM(dims, dtype)


def product(left, right):
    return jnp.dot(left, right, preferred_element_type=jnp.float32)


def product_t(left, right):
    return lax.dot_general(left, right, (((1,), (1,)), ((), ())), preferred_element_type=jnp.float32)


def column_of(row):
    size = row.shape[1]
    first = lax.broadcasted_iota(jnp.int32, (size, size), 0)
    second = lax.broadcasted_iota(jnp.int32, (size, size), 1)
    return jnp.sum(jnp.where(first == second, row, 0.0), axis=1, keepdims=True)


IN_FLIGHT = 6
CHUNKS = 1


class Stream:
    def __init__(self, copies, in_flight):
        self.copies = copies
        self.in_flight = in_flight
        self.done = 0
        for copy in copies[:in_flight]:
            copy.start()

    def arrived(self, upto):
        while self.done <= upto:
            self.copies[self.done].wait()
            if self.done + self.in_flight < len(self.copies):
                self.copies[self.done + self.in_flight].start()
            self.done += 1


def temporal_kernel(
    place_ref, hidden_hbm, gain_hbm, lengths_hbm, qkv_hbm, out_hbm, keys_hbm, values_hbm, head_hbm, kept_ref, last_ref, sent_ref, columns_ref,
    hidden_buf, gain_buf, lengths_buf, qkv_buf, out_buf, keys_buf, values_buf, small_sems, sems, column_sems,
):
    streams, depth = hidden_buf.shape
    cols = qkv_buf.shape[2]
    heads = cols // HEAD_DIM
    cache_len = keys_buf.shape[1]
    steps, halves = QKV_STEPS, CACHE_STEPS
    chunk = depth // steps
    batch = streams // halves
    count, _, width = kept_ref.shape
    odd = place_ref[0] % 2
    place = place_ref[0] // 2
    small = [
        pltpu.make_async_copy(hidden_hbm, hidden_buf, small_sems.at[0]),
        pltpu.make_async_copy(gain_hbm, gain_buf, small_sems.at[1]),
        pltpu.make_async_copy(lengths_hbm, lengths_buf, small_sems.at[2]),
    ]
    for copy in small:
        copy.start()
    pairs = []
    for n in (0, 1):
        pairs += [(qkv_hbm.at[n, pl.ds(i * chunk, chunk)], qkv_buf.at[n, pl.ds(i * chunk, chunk)]) for i in range(steps)]
    pairs += [(keys_hbm.at[pl.ds(i * batch, batch)], keys_buf.at[pl.ds(i * batch, batch)]) for i in range(halves)]
    pairs += [(qkv_hbm.at[2, pl.ds(i * chunk, chunk)], qkv_buf.at[2, pl.ds(i * chunk, chunk)]) for i in range(steps)]
    pairs += [(values_hbm.at[pl.ds(i * batch, batch)], values_buf.at[pl.ds(i * batch, batch)]) for i in range(halves)]
    pairs += [
        (out_hbm.at[:, pl.ds(pl.multiple_of((place ^ k) * 2 * width, 2 * width), 2 * width)], out_buf.at[k])
        for k in range(count)
    ]
    _, half_codes, _, part = columns_ref.shape
    columns = []
    for k in range(count):
        start = pl.multiple_of(((place ^ k) * 2 + 1 - odd) * part, part)
        source = head_hbm.at[pl.ds(place_ref[2] * half_codes, half_codes), :, pl.ds(start, part)]
        columns.append(pltpu.make_async_copy(source, columns_ref.at[k], column_sems.at[k]))
    stream = Stream([pltpu.make_async_copy(src, dst, sems.at[i]) for i, (src, dst) in enumerate(pairs)], IN_FLIGHT)
    first_of = (0, steps, 2 * steps + halves)
    keys_end = 2 * steps + halves - 1
    values_end = 3 * steps + 2 * halves - 1

    for copy in small:
        copy.wait()
    wide = hidden_buf[...].astype(jnp.float32)
    inv = lax.rsqrt(jnp.mean(wide * wide, axis=1, keepdims=True) + EPSILON)
    normed = (wide * inv * gain_buf[...]).astype(jnp.bfloat16)

    def projected(n):
        total = None
        for i in range(steps):
            stream.arrived(first_of[n] + i)
            part = product(normed[:, i * chunk : (i + 1) * chunk], qkv_buf[n, pl.ds(i * chunk, chunk), :])
            total = part if total is None else total + part
        return total

    lengths_row = lengths_buf[...].astype(jnp.float32)
    lengths_col = column_of(lengths_row)
    half = HEAD_DIM // 2
    lane = lax.broadcasted_iota(jnp.int32, (streams, HEAD_DIM), 1)
    spacing = (lane & (half - 1)).astype(jnp.float32) / half
    angles = lengths_col * jnp.exp(-math.log(10000.0) * spacing)
    cosine = jnp.cos(angles)
    sine = jnp.where(lane < half, -1.0, 1.0) * jnp.sin(angles)

    def rotated(block):
        pieces = []
        for h in range(heads):
            piece = block[:, h * HEAD_DIM : (h + 1) * HEAD_DIM]
            pieces.append(piece * cosine + pltpu.roll(piece, half, 1) * sine)
        return jnp.concatenate(pieces, axis=1)

    queries = rotated(projected(0))
    for copy in columns:
        copy.start()
    keys_new = rotated(projected(1)).astype(jnp.bfloat16)
    head_lane = lax.broadcasted_iota(jnp.int32, (streams, cols), 1) // HEAD_DIM
    spread = jnp.concatenate(
        [jnp.where(head_lane == h, queries, 0.0) for h in range(heads)], axis=0
    ).astype(jnp.bfloat16)
    pairs = heads * streams
    factor = 1.0 / math.sqrt(HEAD_DIM)
    pair = lax.broadcasted_iota(jnp.int32, (1, pairs), 1)
    pair_stream = pair % streams
    own = product_t(keys_new, spread) * factor
    stream_row = lax.broadcasted_iota(jnp.int32, (streams, pairs), 0)
    own_score = jnp.sum(jnp.where(stream_row == pair_stream, own, 0.0), axis=0, keepdims=True)
    tiled = jnp.sum(jnp.where(stream_row == pair_stream, lengths_col, 0.0), axis=0, keepdims=True)
    first_row = pair_stream * cache_len
    last_row = first_row + tiled.astype(jnp.int32)
    stream.arrived(keys_end)
    rows = streams * cache_len
    scores = product_t(keys_buf[...].reshape(rows, cols), spread) * factor
    row = lax.broadcasted_iota(jnp.int32, (rows, pairs), 0)
    scores = jnp.where((row >= first_row) & (row < last_row), scores, -jnp.inf)
    highest = jnp.maximum(jnp.max(scores, axis=0, keepdims=True), own_score)
    expo = jnp.exp(scores - highest)
    own_expo = jnp.exp(own_score - highest)
    inverse = 1.0 / (jnp.sum(expo, axis=0, keepdims=True) + own_expo)
    weights = (expo * inverse).astype(jnp.bfloat16)
    own_weight = (own_expo * inverse).astype(jnp.bfloat16).astype(jnp.float32)
    values_new = projected(2).astype(jnp.bfloat16).astype(jnp.float32)
    stream.arrived(values_end)
    mixed_all = lax.dot_general(
        weights,
        values_buf[...].reshape(rows, cols),
        (((0,), (0,)), ((), ())),
        preferred_element_type=jnp.float32,
    )
    pair_lane = lax.broadcasted_iota(jnp.int32, (streams, pairs), 1)
    pair_row = lax.broadcasted_iota(jnp.int32, (streams, pairs), 0)
    mixed = []
    for h in range(heads):
        own_col = jnp.sum(
            jnp.where(pair_lane == pair_row + h * streams, own_weight, 0.0), axis=1, keepdims=True
        )
        lanes = slice(h * HEAD_DIM, (h + 1) * HEAD_DIM)
        mixed.append(
            mixed_all[h * streams : (h + 1) * streams, lanes] + own_col * values_new[:, lanes]
        )
    mixed = jnp.concatenate(mixed, axis=1).astype(jnp.bfloat16)
    for copy in columns:
        copy.wait()
    for k in range(count):
        stream.arrived(values_end + 1 + k)
        block = product(mixed, out_buf[k])
        even_side, odd_side = block[:, :width], block[:, width:]
        kept_ref[k] = jnp.where(odd == 1, odd_side, even_side)
        sent = jnp.where(odd == 1, even_side, odd_side).astype(jnp.bfloat16)
        if k == 0:
            last_ref[...] = sent
        else:
            sent_ref[k - 1] = sent


QKV_STEPS = 4
CACHE_STEPS = 2


def temporal_parts(place, hidden_in, gain, lengths, qkv, out_weight, keys, values, head_weight, places):
    codes, head_depth, vocab = head_weight.shape
    streams, depth = hidden_in.shape
    bf16 = jnp.bfloat16
    count, width = places // 2, out_weight.shape[1] // places
    block = (count, streams, width)
    return pl.pallas_call(
        temporal_kernel,
        in_specs=[SMEM] + [HBM] * 8,
        out_specs=[VMEM] * 4,
        out_shape=[
            vmem(block, jnp.float32),
            vmem(block[1:], bf16),
            vmem((count - 1,) + block[1:], bf16),
            vmem((count, codes // 2, head_depth, vocab // places), bf16),
        ],
        scratch_shapes=[
            pltpu.VMEM(hidden_in.shape, bf16),
            pltpu.VMEM((1, depth), jnp.float32),
            pltpu.VMEM((1, streams), jnp.int32),
            pltpu.VMEM(qkv.shape, bf16),
            pltpu.VMEM((count, out_weight.shape[0], 2 * width), bf16),
            pltpu.VMEM(keys.shape, bf16),
            pltpu.VMEM(values.shape, bf16),
            pltpu.SemaphoreType.DMA((3,)),
            pltpu.SemaphoreType.DMA((3 * QKV_STEPS + 2 * CACHE_STEPS + count,)),
            pltpu.SemaphoreType.DMA((count,)),
        ],
        compiler_params=params(30),
        name="temporal",
    )(
        place,
        in_hbm(hidden_in),
        in_hbm(gain.reshape(1, depth)),
        in_hbm(lengths.reshape(1, streams)),
        in_hbm(qkv),
        in_hbm(out_weight),
        in_hbm(keys),
        in_hbm(values),
        in_hbm(head_weight),
    )


def prepare_kernel(
    place_ref, tokens_ref, hidden_hbm, embed_hbm, weight_hbm, resid_ref, embedded_ref, weight_ref, embed_buf, sem, sems
):
    codes, vocab, _ = embed_buf.shape
    streams = tokens_ref.shape[0]
    part = resid_ref.shape[1]
    start = pl.multiple_of(place_ref[0] * part, part)
    resid = pltpu.make_async_copy(hidden_hbm.at[:, pl.ds(start, part)], resid_ref, sem)
    resid.start()
    embed = [pltpu.make_async_copy(embed_hbm.at[c], embed_buf.at[c], sems.at[0, c]) for c in range(codes)]
    weight = [pltpu.make_async_copy(weight_hbm.at[c], weight_ref.at[c], sems.at[1, c]) for c in range(codes)]
    stream = Stream(embed + weight, IN_FLIGHT)
    vocab_lane = lax.broadcasted_iota(jnp.int32, (streams, vocab), 1) + place_ref[0] * vocab
    for c in range(codes):
        hit = tokens_ref[:, c : c + 1] == vocab_lane
        onehot = jnp.where(hit, 1.0, 0.0).astype(jnp.bfloat16)
        stream.arrived(c)
        embedded_ref[c] = product(onehot, embed_buf[c])
    stream.arrived(2 * codes - 1)
    resid.wait()


def prepared_entry(place, tokens, hidden_in, embed, weight, places):
    codes, _, width = weight.shape
    streams = tokens.shape[0]
    resid_shape = (hidden_in.shape[0], hidden_in.shape[1] // places)
    return pl.pallas_call(
        prepare_kernel,
        in_specs=[SMEM, VMEM, HBM, HBM, HBM],
        out_specs=[VMEM] * 3,
        out_shape=[
            vmem(resid_shape, jnp.bfloat16),
            vmem((codes, streams, width), jnp.float32),
            vmem(weight.shape, jnp.bfloat16),
        ],
        scratch_shapes=[
            pltpu.VMEM(embed.shape, jnp.bfloat16),
            pltpu.SemaphoreType.DMA(()),
            pltpu.SemaphoreType.DMA((2, codes)),
        ],
        compiler_params=params(16),
        name="entry_prepare",
    )(place, tokens, in_hbm(hidden_in), in_hbm(embed), in_hbm(weight))


def near_kernel(place_ref, token_ref, gain_ref, qkv_hbm, out_hbm, head_hbm, own_ref, qkv_ref, out_ref, *rest):
    column_refs, (sems, column_sems) = rest[:-2], rest[-2:]
    del token_ref
    copies = [
        pltpu.make_async_copy(source.at[c], target.at[c], sems.at[i, c])
        for i, (source, target) in enumerate(((qkv_hbm, qkv_ref), (out_hbm, out_ref)))
        for c in range(source.shape[0])
    ]
    for n, out in enumerate(column_refs):
        count, codes, _, vocab_part = out.shape
        for k in range(count):
            start = pl.multiple_of(((place_ref[0] // 2 ^ k) * 2 + place_ref[0] % 2) * vocab_part, vocab_part)
            source = head_hbm.at[pl.ds(n * codes, codes), :, pl.ds(start, vocab_part)]
            copies.append(pltpu.make_async_copy(source, out.at[k], column_sems.at[n, k]))
    stream = Stream(copies, IN_FLIGHT)
    part = own_ref.shape[1]
    own_ref[...] = gain_ref[:, pl.ds(pl.multiple_of(place_ref[0] * part, part), part)]
    stream.arrived(len(copies) - 1)


def brought_near(place, token, gain, qkv, out_weight, head_weight, places):
    width = gain.shape[0]
    codes, depth, vocab = head_weight.shape
    columns = vmem((places // 2, codes // CHUNKS, depth, vocab // places), jnp.bfloat16)
    return pl.pallas_call(
        near_kernel,
        in_specs=[SMEM, VMEM, VMEM, HBM, HBM, HBM],
        out_specs=[VMEM] * (3 + CHUNKS),
        out_shape=[
            vmem((1, width // places), jnp.float32),
            vmem(qkv.shape, jnp.bfloat16),
            vmem(out_weight.shape, jnp.bfloat16),
        ]
        + [columns] * CHUNKS,
        scratch_shapes=[
            pltpu.SemaphoreType.DMA((2, qkv.shape[0])),
            pltpu.SemaphoreType.DMA((CHUNKS, places // 2)),
        ],
        compiler_params=params(16),
        name="brought_near",
    )(place, token, gain.reshape(1, width), in_hbm(qkv), in_hbm(out_weight), in_hbm(head_weight))


def entry_kernel(place_ref, own_ref, other_ref, embedded_ref, weight_ref, after_ref, kept_ref, last_ref, sent_ref, token_ref, total_buf):
    del after_ref
    token_ref[...] = jnp.zeros_like(token_ref)
    codes = weight_ref.shape[0]
    count, _, _, part = kept_ref.shape
    odd = place_ref[0] % 2
    place = place_ref[0] // 2
    first_section = place_ref[1] == 0
    own, other = own_ref[...], other_ref[...]
    rows = jnp.concatenate(
        [jnp.where(first_section, own, other), jnp.where(first_section, other, own)], axis=0
    )
    for c in range(codes):
        total_buf[...] = embedded_ref[c] + product(rows, weight_ref[c])
        for k in range(count):
            pair = (place ^ k) * 2
            kept_ref[k, c] = total_buf[:, pl.ds(pl.multiple_of((pair + odd) * part, part), part)]
            sent = total_buf[:, pl.ds(pl.multiple_of((pair + 1 - odd) * part, part), part)].astype(jnp.bfloat16)
            if k == 0:
                last_ref[c] = sent
            else:
                sent_ref[k - 1, c] = sent


def entry_parts(place, own, other, embedded, weight, after, places):
    codes, _, width = weight.shape
    streams = 2 * own.shape[0]
    block = (places // 2, codes, streams, width // places)
    return pl.pallas_call(
        entry_kernel,
        in_specs=[SMEM] + [VMEM] * 5,
        out_specs=[VMEM] * 4,
        out_shape=[
            vmem(block, jnp.float32),
            vmem(block[1:], jnp.bfloat16),
            vmem((places // 2 - 1,) + block[1:], jnp.bfloat16),
            vmem((8, 128), jnp.float32),
        ],
        scratch_shapes=[pltpu.VMEM((streams, width), jnp.float32)],
        compiler_params=params(16),
        name="entry",
    )(place, own, other, embedded, weight, after)


def nearest_last(far):
    return list(range(1, far)) + [0]


def qkv_kernel(count, place_ref, gain_ref, weight_ref, far_ref, *rest):
    near_refs, (last_ref, queries_ref, pair_ref) = rest[:count], rest[count:]
    codes, _, width, cols = weight_ref.shape
    part = last_ref.shape[2]
    odd = place_ref[0] % 2
    place = place_ref[0] // 2
    order = [0] + [k + 1 for k in nearest_last(count - 1)]
    starts = [pl.multiple_of(((place ^ k) * 2 + side) * part, part) for side in (odd, 1 - odd) for k in order]
    inverse_gain = 1.0 / jnp.concatenate([gain_ref[:, pl.ds(start, part)] for start in starts], axis=1)
    for c in range(codes):
        blocks = [ref[c] for ref in near_refs] + [last_ref[c]] + [far_ref[k, c] for k in range(count - 1)]
        row = jnp.concatenate(blocks, axis=1)
        plain = row.astype(jnp.float32) * inverse_gain
        inv = lax.rsqrt(jnp.sum(plain * plain, axis=1, keepdims=True) / width + EPSILON)
        for n in range(3):
            weight = jnp.concatenate([weight_ref[c, n, pl.ds(start, part), :] for start in starts], axis=0)
            value = (product(row, weight) * inv).astype(jnp.bfloat16)
            if n == 0:
                queries_ref[c] = value
            else:
                pair_ref[n - 1, c] = value


def depth_projections(place, near, last, far, gain, weight):
    codes, _, width, cols = weight.shape
    streams = last.shape[1]
    bf16 = jnp.bfloat16
    return pl.pallas_call(
        functools.partial(qkv_kernel, len(near)),
        in_specs=[SMEM] + [VMEM] * (4 + len(near)),
        out_specs=[VMEM] * 2,
        out_shape=[vmem((codes, streams, cols), bf16), vmem((2, codes, streams, cols), bf16)],
        compiler_params=params(16),
        name="depth_qkv",
    )(place, gain.reshape(1, width), weight, far, *near, last)


def mix_kernel(terms, place_ref, queries_ref, own_ref, prior_ref, weight_ref, *rest):
    entry_refs, outs, total_buf = rest[:terms], rest[terms:-1], rest[-1]
    codes, streams, cols = queries_ref.shape
    each, _, span = outs[0].shape
    count = len(outs) // CHUNKS
    has_prior = place_ref[1] > 0
    first = lax.broadcasted_iota(jnp.int32, (2 * cols, cols), 0) % cols
    second = lax.broadcasted_iota(jnp.int32, (2 * cols, cols), 1)
    same = jnp.where(first // DEPTH_HDIM == second // DEPTH_HDIM, 1.0, 0.0).astype(jnp.bfloat16)
    keys = [prior_ref[0, j].astype(jnp.float32) for j in range(codes)]
    keys += [own_ref[0, j].astype(jnp.float32) for j in range(codes)]
    values = [prior_ref[1, j].astype(jnp.float32) for j in range(codes)]
    values += [own_ref[1, j].astype(jnp.float32) for j in range(codes)]
    factor = 1.0 / math.sqrt(DEPTH_HDIM)
    mixed = []
    for q in range(codes):
        query = queries_ref[q].astype(jnp.float32)
        reach = codes + q + 1
        pieces = []
        for j in range(reach):
            exact = query * keys[j]
            high = exact.astype(jnp.bfloat16)
            low = (exact - high.astype(jnp.float32)).astype(jnp.bfloat16)
            pieces.append(jnp.concatenate([high, low], axis=1))
        scores = product(jnp.concatenate(pieces, axis=0), same) * factor
        score = [scores[j * streams : (j + 1) * streams] for j in range(reach)]
        score = [jnp.where(has_prior, s, -jnp.inf) if j < codes else s for j, s in enumerate(score)]
        top = score[0]
        for s in score[1:]:
            top = jnp.maximum(top, s)
        expo = [jnp.exp(s - top) for s in score]
        inverse = 1.0 / sum(expo)
        total = jnp.zeros_like(query)
        for j in range(reach):
            total = total + (expo[j] * inverse).astype(jnp.bfloat16).astype(jnp.float32) * values[j]
        mixed.append(total.astype(jnp.bfloat16))
    for q in range(codes):
        total_buf[q] = product(mixed[q], weight_ref[q])
    part = entry_refs[0].shape[2]
    own_part = pl.ds(pl.multiple_of(place_ref[0] * part, part), part)
    total_buf[:, :, own_part] += sum(ref[...].astype(jnp.float32) for ref in entry_refs)
    place = place_ref[0] // 2
    for n, out in enumerate(outs):
        chunk, k = divmod(n, count)
        start = pl.multiple_of((place ^ k) * span, span)
        block = total_buf[pl.ds(chunk * each, each), :, pl.ds(start, span)]
        out[...] = block if k == 0 else block.astype(jnp.bfloat16)


def mixed_parts(place, queries, own, prior, weight, entry_terms, far):
    codes, streams, cols = queries.shape
    width = weight.shape[2]
    block = (codes // CHUNKS, streams, width // (far + 1))
    outs = pl.pallas_call(
        functools.partial(mix_kernel, len(entry_terms)),
        in_specs=[SMEM] + [VMEM] * (4 + len(entry_terms)),
        out_specs=[VMEM] * ((far + 1) * CHUNKS),
        out_shape=([vmem(block, jnp.float32)] + [vmem(block, jnp.bfloat16)] * far) * CHUNKS,
        scratch_shapes=[pltpu.VMEM((codes, streams, width), jnp.float32)],
        compiler_params=params(16),
        name="depth_mix",
    )(place, queries, own, prior, weight, *entry_terms)
    return [outs[n * (far + 1) : (n + 1) * (far + 1)] for n in range(CHUNKS)]


STAT_ROWS = 16


def head_kernel(
    first, place_ref, gain_ref, total_ref, arrived_ref, weight_ref, early_ref, late_ref, kept_ref, stat_ref, *sends
):
    half = early_ref.shape[1]

    def partner(k, c):
        side, index = divmod(first + c, half)
        return jnp.where(place_ref[2] == side, early_ref[k, index], late_ref[k, index])

    codes, streams, span = total_ref.shape
    count, _, depth, part = weight_ref.shape
    odd = place_ref[0] % 2
    resid = total_ref[...] + arrived_ref[...].astype(jnp.float32)
    flat = resid.reshape(codes * streams, span)
    squares = flat * flat
    stat = product_t(jnp.ones((STAT_ROWS // 2, span), jnp.float32), squares)[:1]
    stat_ref[...] = stat
    high = stat.astype(jnp.bfloat16).astype(jnp.float32)
    stat_row = lax.broadcasted_iota(jnp.int32, (STAT_ROWS, codes * streams), 0)
    stat_block = jnp.where(stat_row == 0, high, jnp.where(stat_row == 1, stat - high, 0.0))
    if part > codes * streams:
        rest = jnp.zeros((STAT_ROWS, part - codes * streams), jnp.float32)
        stat_block = jnp.concatenate([stat_block, rest], axis=1)
    stat_block = stat_block.astype(jnp.bfloat16)
    scaled = resid * gain_ref[...]
    low_half, high_half = scaled[:, :, :depth], scaled[:, :, depth:]
    ordered = jnp.concatenate(
        [jnp.where(odd == 1, high_half, low_half), jnp.where(odd == 1, low_half, high_half)], axis=2
    ).astype(jnp.bfloat16)
    rows = codes * streams
    for k in range(count):
        block = jnp.concatenate(
            [
                product(ordered[c], jnp.concatenate([weight_ref[k, c], partner(k, c)], axis=0))
                for c in range(codes)
            ],
            axis=0,
        )
        if k == 0:
            kept_ref[...] = block
        else:
            sends[k - 1][pl.ds(0, rows), :] = block.astype(jnp.bfloat16)
            sends[k - 1][pl.ds(rows, STAT_ROWS), :] = stat_block


def head_parts(first, place, gain, total, arrived, weight, early, late):
    codes, streams, span = total.shape
    count, _, depth, part = weight.shape
    rows = codes * streams
    return pl.pallas_call(
        functools.partial(head_kernel, first),
        in_specs=[SMEM] + [VMEM] * 6,
        out_specs=[VMEM] * (count + 1),
        out_shape=[vmem((rows, part), jnp.float32), vmem((1, rows), jnp.float32)]
        + [vmem((rows + STAT_ROWS, part), jnp.bfloat16)] * (count - 1),
        compiler_params=params(16),
        name="head",
    )(place, gain, total, arrived, weight, early, late)


def logits_kernel(width, *refs):
    out_ref = refs[-1]
    streams, codes, part = out_ref.shape
    each = codes // CHUNKS
    rows = each * streams
    count = (len(refs) - 1) // CHUNKS
    for n in range(CHUNKS):
        kept_ref, stat_ref, *arrived = refs[n * count : (n + 1) * count]
        total = kept_ref[...]
        stat = stat_ref[...]
        for block in arrived:
            wide = block[...].astype(jnp.float32)
            total = total + wide[:rows]
            stat = stat + wide[rows : rows + 1, :rows] + wide[rows + 1 : rows + 2, :rows]
        total = total * column_of(lax.rsqrt(stat / width + EPSILON))
        for c in range(each):
            out_ref[:, n * each + c, :] = total[c * streams : (c + 1) * streams]


def finished_logits(chunks, streams, codes, width):
    part = chunks[0][0].shape[1]
    arrays = [array for chunk in chunks for array in chunk]
    return pl.pallas_call(
        functools.partial(logits_kernel, width),
        in_specs=[VMEM] * len(arrays),
        out_specs=VMEM,
        out_shape=shape((streams, codes, part), jnp.float32),
        compiler_params=params(16),
        name="logits",
    )(*arrays)


def paired_device(
    hidden_in,
    temporal_gain,
    temporal_qkv,
    temporal_out_weight,
    cache_keys,
    cache_values,
    lengths,
    depth_in,
    depth_embed,
    depth_gain,
    depth_qkv,
    depth_out_weight,
    head_gain,
    head_weight,
    tokens,
):
    tp = lax.axis_size("tp")
    tp_place = lax.axis_index("tp")
    place = jnp.stack([tp_place, lax.axis_index("section"), lax.axis_index("grp") % 2])
    far = tp // 2 - 1

    def to_pairs(blocks):
        arrived = [None] * len(blocks)
        for k in reversed(range(len(blocks))):
            arrived[k] = lax.ppermute(blocks[k], "tp", [(i, i ^ 2 * (k + 1)) for i in range(tp)])
        return arrived

    order = nearest_last(far)

    def in_order(blocks, order):
        return [blocks[k] for k in order]

    def to_neighbour(block):
        return lax.ppermute(block, "tp", [(i, i ^ 1) for i in range(tp)])

    def summed(kept, last, sent, order):
        folded = kept[1:] + to_neighbour(sent).astype(jnp.float32)
        arrived = to_pairs([folded[k].astype(jnp.bfloat16) for k in range(far)])
        return [kept[0]] + [arrived[k] for k in order] + [to_neighbour(last)]

    def added(terms):
        return sum(term.astype(jnp.float32) for term in terms)

    kept, last, sent, neighbour_columns = temporal_parts(
        place,
        hidden_in,
        temporal_gain,
        lengths,
        temporal_qkv,
        temporal_out_weight,
        cache_keys,
        cache_values,
        head_weight,
        tp,
    )
    sent, depth_in = lax.optimization_barrier((sent, depth_in))
    early = to_neighbour(neighbour_columns)
    resid_in, embedded, near_in = prepared_entry(place, tokens, hidden_in, depth_embed, depth_in, tp)
    temporal = (resid_in.astype(jnp.float32) + added(summed(kept, last, sent, order))).astype(jnp.bfloat16)
    other_rows = lax.ppermute(temporal, "section", [(0, 1), (1, 0)])
    codes = depth_in.shape[0]
    width = depth_in.shape[2]
    hidden_rows = head_weight.shape[1]
    kept, last, sent, token = entry_parts(place, temporal, other_rows, embedded, near_in, early, tp)
    late = lax.ppermute(early, "grp", [(i, i ^ 1) for i in range(lax.axis_size("grp"))])
    own_gain, near_qkv, near_out, *own_columns = brought_near(
        place, token, depth_gain, depth_qkv, depth_out_weight, head_weight, tp
    )
    entry_terms = summed(kept, last, sent, order)
    scaled = (added(entry_terms) * own_gain[None]).astype(jnp.bfloat16)
    near = [scaled] + in_order(to_pairs([scaled] * far), order)
    last = to_neighbour(scaled)
    queries, own_pair = depth_projections(
        place, near, last, to_neighbour(jnp.stack(near[1:])), depth_gain, near_qkv
    )
    prior_pair = passed_along(own_pair, "section", 1)
    chunks = mixed_parts(place, queries, own_pair, prior_pair, near_out, entry_terms, far)
    pair_gain = lax.dynamic_slice_in_dim(head_gain, tp_place // 2 * 2 * hidden_rows, 2 * hidden_rows, 0)
    each = codes // CHUNKS
    arrived = [in_order(to_pairs(blocks), order) for _, *blocks in chunks]
    totals = [
        kept + added(blocks) for (kept, *_), blocks in zip(chunks, arrived)
    ]
    others = [to_neighbour(total.astype(jnp.bfloat16)) for total in totals]
    heads = [
        head_parts(n * each, place, pair_gain.reshape(1, 1, -1), total, other, own, early, late)
        for n, (total, other, own) in enumerate(zip(totals, others, own_columns))
    ]
    finished = [[kept, stat, *in_order(to_pairs(blocks), order)] for kept, stat, *blocks in heads]
    logits = finished_logits(finished, sent.shape[2], codes, width)
    return (temporal, logits)


def per_device(*arrays):
    hidden_in, temporal_qkv, depth_qkv, head_weight = arrays[0], arrays[2], arrays[10], arrays[13]
    depth_in, tokens = arrays[7], arrays[14]
    tp = lax.axis_size("tp")
    pairs = hidden_in.shape[0] * (temporal_qkv.shape[2] // HEAD_DIM)
    whole_tiles = (
        pairs % 128 == 0
        and temporal_qkv.shape[2] % HEAD_DIM == 0
        and head_weight.shape[1] % 128 == 0
        and head_weight.shape[2] // tp % 128 == 0
        and depth_qkv.shape[3] % 128 == 0
        and tp >= 4
        and depth_in.shape[0] % (2 * CHUNKS) == 0
        and lax.axis_size("grp") % 2 == 0
        and depth_in.shape[0] // CHUNKS * tokens.shape[0] <= head_weight.shape[2] // tp
        and tp & (tp - 1) == 0
    )
    return (paired_device if whole_tiles else general_device)(*arrays)


def solution(mesh):
    return jax.shard_map(
        per_device,
        mesh=mesh,
        in_specs=(
            P(("grp", "section"), None),
            P(),
            P(None, None, "tp"),
            P("tp", None),
            P(("grp", "section"), None, "tp"),
            P(("grp", "section"), None, "tp"),
            P(("grp", "section")),
            P("section", "tp", None),
            P("section", "tp", None),
            P(),
            P("section", None, None, "tp"),
            P("section", "tp", None),
            P(),
            P("section", "tp", None),
            P("grp", "section"),
        ),
        out_specs=(P(("grp", "section"), "tp"), P("grp", "section", "tp")),
        check_vma=False,
    )
```

```python
import functools
import math

import jax
import jax.numpy as jnp
from jax import lax
from jax.experimental import pallas as pl
from jax.experimental.pallas import tpu as pltpu
from jax.sharding import PartitionSpec as P

HEAD_DIM = 128
DEPTH_HDIM = 64


EPSILON = 1e-05


def passed_along(block, axis, distance):
    devices = range(lax.axis_size(axis))
    route = [(i - distance, i) for i in devices if i - distance in devices]
    return lax.ppermute(block, axis, route)


def from_partner(shard, axis, distance):
    return lax.ppermute(shard, axis, [(i, i ^ 1 << distance) for i in range(lax.axis_size(axis))])


def rms_norm(values, scale):
    wide = values.astype(jnp.float32)
    return wide * lax.rsqrt(jnp.mean(wide * wide, axis=-1, keepdims=True) + EPSILON) * scale


def rotate(vectors, positions):
    halfdim = vectors.shape[-1] // 2
    spacing = jnp.arange(halfdim, dtype=jnp.float32) / halfdim
    inverse = jnp.exp(-math.log(10000.0) * spacing)
    angles = positions.astype(jnp.float32)[:, None, None] * inverse[None, None, :]
    cosine = jnp.cos(angles)
    sine = jnp.sin(angles)
    first = vectors[..., :halfdim]
    second = vectors[..., halfdim:]
    return jnp.concatenate(
        [first * cosine - second * sine, first * sine + second * cosine], axis=-1
    )


def scattered_sum(parts):
    moved = lax.all_to_all(parts.astype(jnp.bfloat16), "tp", 0, 0)
    return jnp.sum(moved.astype(jnp.float32), axis=0)


def gathered(block):
    size = lax.axis_size("tp")
    return lax.all_to_all(jnp.broadcast_to(block[None], (size,) + block.shape), "tp", 0, 0)


def general_device(
    hidden_in,
    temporal_gain,
    temporal_qkv,
    temporal_out_weight,
    cache_keys,
    cache_values,
    lengths,
    depth_in,
    depth_embed,
    depth_gain,
    depth_qkv,
    depth_out_weight,
    head_gain,
    head_weight,
    tokens,
):
    tp = lax.axis_size("tp")
    local_streams = hidden_in.shape[0]
    local_cols = temporal_qkv.shape[2]
    local_heads = local_cols // HEAD_DIM
    cache_len = cache_keys.shape[1]
    normed = rms_norm(hidden_in, temporal_gain).astype(jnp.bfloat16)
    projected = jnp.einsum("sd,tdf->tsf", normed, temporal_qkv, preferred_element_type=jnp.float32)
    layout = (local_streams, local_heads, HEAD_DIM)
    queries = rotate(projected[0].reshape(layout), lengths).astype(jnp.bfloat16)
    keys_new = rotate(projected[1].reshape(layout), lengths).astype(jnp.bfloat16)
    values_new = projected[2].reshape(layout).astype(jnp.bfloat16)
    cached_keys = cache_keys.reshape(local_streams, cache_len, local_heads, HEAD_DIM)
    cached_values = cache_values.reshape(local_streams, cache_len, local_heads, HEAD_DIM)
    factor = 1.0 / math.sqrt(HEAD_DIM)
    scores = (
        jnp.einsum("shd,sphd->shp", queries, cached_keys, preferred_element_type=jnp.float32)
        * factor
    )
    own_score = (
        jnp.sum(queries.astype(jnp.float32) * keys_new.astype(jnp.float32), axis=-1) * factor
    )
    valid = jnp.arange(cache_len, dtype=jnp.int32)[None, None, :] < lengths[:, None, None]
    scores = jnp.where(valid, scores, -jnp.inf)
    highest = jnp.maximum(jnp.max(scores, axis=-1), own_score)
    expo = jnp.exp(scores - highest[..., None])
    own_expo = jnp.exp(own_score - highest)
    totals = jnp.sum(expo, axis=-1) + own_expo
    weights = (expo / totals[..., None]).astype(jnp.bfloat16)
    own_weight = (own_expo / totals).astype(jnp.bfloat16)
    mixed = jnp.einsum("shp,sphd->shd", weights, cached_values, preferred_element_type=jnp.float32)
    mixed = mixed + own_weight.astype(jnp.float32)[..., None] * values_new.astype(jnp.float32)
    mixed = mixed.astype(jnp.bfloat16).reshape(local_streams, local_cols)
    partial_rows = jnp.dot(mixed, temporal_out_weight, preferred_element_type=jnp.float32)
    slice_width = partial_rows.shape[1] // tp
    by_slice = partial_rows.reshape(local_streams, tp, slice_width).transpose(1, 0, 2)
    summed = scattered_sum(by_slice)
    tp_place = lax.axis_index("tp")
    resid_in = lax.dynamic_slice_in_dim(hidden_in, tp_place * slice_width, slice_width, 1)
    temporal = (resid_in.astype(jnp.float32) + summed).astype(jnp.bfloat16)
    all_rows = lax.all_gather(temporal, "section", axis=0, tiled=True)
    streams = all_rows.shape[0]
    codes = depth_in.shape[0]
    width = depth_in.shape[2]
    vocab_local = depth_embed.shape[1]
    first_id = tp_place * vocab_local
    onehot = (
        tokens[:, :, None] == first_id + jnp.arange(vocab_local, dtype=jnp.int32)[None, None, :]
    ).astype(jnp.bfloat16)
    embedded = jnp.einsum("scv,cve->cse", onehot, depth_embed, preferred_element_type=jnp.float32)
    entry_terms = embedded + jnp.einsum(
        "sd,cde->cse", all_rows, depth_in, preferred_element_type=jnp.float32
    )
    hidden_rows = head_weight.shape[1]
    hidden_start = tp_place * hidden_rows
    entry = scattered_sum(entry_terms.reshape(codes, streams, tp, hidden_rows).transpose(2, 0, 1, 3))
    own_gain = lax.dynamic_slice_in_dim(depth_gain, hidden_start, hidden_rows, 0)
    scaled = (entry * own_gain).astype(jnp.bfloat16)
    rows = gathered(scaled)
    plain = rows.astype(jnp.float32) / depth_gain.reshape(tp, 1, 1, hidden_rows)
    inv_rms = lax.rsqrt(jnp.sum(plain * plain, axis=(0, 3)) / width + EPSILON)
    dproj = jnp.einsum(
        "tcse,cntef->ncsf",
        rows,
        depth_qkv.reshape(codes, 3, tp, hidden_rows, -1),
        preferred_element_type=jnp.float32,
    )
    dproj = (dproj * inv_rms[None, :, :, None]).astype(jnp.bfloat16)
    prior = passed_along(dproj[1:], "section", 1)
    depth_cols = dproj.shape[3]
    head_part = min(depth_cols, DEPTH_HDIM)
    local_parts = depth_cols // head_part
    sharers = DEPTH_HDIM // head_part
    both = jnp.concatenate([prior, dproj[1:]], axis=1)
    all_keys = both[0].reshape(2 * codes, streams, local_parts, head_part)
    all_values = both[1].reshape(2 * codes, streams, local_parts, head_part)
    depth_queries = dproj[0].reshape(codes, streams, local_parts, head_part)
    depth_scores = jnp.sum(
        depth_queries[:, None].astype(jnp.float32) * all_keys[None].astype(jnp.float32), axis=-1
    )
    for level in range(sharers.bit_length() - 1):
        depth_scores = depth_scores + from_partner(depth_scores, "tp", level)
    depth_scores = depth_scores * (1.0 / math.sqrt(DEPTH_HDIM))
    section_place = lax.axis_index("section")
    query_pos = jnp.arange(codes, dtype=jnp.int32)[:, None]
    key_pos = jnp.arange(2 * codes, dtype=jnp.int32)[None, :]
    allowed = jnp.where(key_pos < codes, section_place > 0, key_pos - codes <= query_pos)
    depth_scores = jnp.where(allowed[:, :, None, None], depth_scores, -jnp.inf)
    depth_top = jnp.max(depth_scores, axis=1, keepdims=True)
    depth_expo = jnp.exp(depth_scores - depth_top)
    depth_weights = (depth_expo / jnp.sum(depth_expo, axis=1, keepdims=True)).astype(jnp.bfloat16)
    depth_mixed = jnp.sum(
        depth_weights[..., None].astype(jnp.float32) * all_values[None].astype(jnp.float32), axis=1
    ).astype(jnp.bfloat16)
    depth_mixed = depth_mixed.reshape(codes, streams, depth_cols)
    depth_terms = jnp.einsum(
        "csf,cfe->cse", depth_mixed, depth_out_weight, preferred_element_type=jnp.float32
    )
    added = scattered_sum(depth_terms.reshape(codes, streams, tp, hidden_rows).transpose(2, 0, 1, 3))
    resid = entry + added
    own_head_gain = lax.dynamic_slice_in_dim(head_gain, hidden_start, hidden_rows, 0)
    own_hidden = (resid * own_head_gain).astype(jnp.bfloat16)
    squares = jnp.sum(resid * resid, axis=2)
    high = squares.astype(jnp.bfloat16)
    low = (squares - high.astype(jnp.float32)).astype(jnp.bfloat16)
    partial_logits = jnp.einsum(
        "cse,cev->csv", own_hidden, head_weight, preferred_element_type=jnp.float32
    )
    vocab_slice = partial_logits.shape[2] // tp
    outgoing = partial_logits.reshape(codes, streams, tp, vocab_slice).transpose(2, 0, 1, 3)
    outgoing = outgoing.astype(jnp.bfloat16).reshape(tp, codes * streams, vocab_slice)
    extra = jnp.stack([high.reshape(-1), low.reshape(-1)])
    extra = jnp.pad(extra, ((0, 14), (0, 0))).reshape(-1, vocab_slice)
    packed = jnp.concatenate(
        [outgoing, jnp.broadcast_to(extra[None], (tp,) + extra.shape)], axis=1
    )
    moved = lax.all_to_all(packed, "tp", 0, 0).astype(jnp.float32)
    rows_total = jnp.sum(moved, axis=0)
    stats = rows_total[codes * streams :].reshape(16, codes, streams)
    head_inv = lax.rsqrt((stats[0] + stats[1]) / width + EPSILON)
    logits = rows_total[: codes * streams].reshape(codes, streams, vocab_slice) * head_inv[..., None]
    return (temporal, logits.transpose(1, 0, 2))


HBM = pl.BlockSpec(memory_space=pltpu.HBM)
VMEM = pl.BlockSpec(memory_space=pltpu.VMEM)
SMEM = pl.BlockSpec(memory_space=pltpu.SMEM)


def params(mebibytes):
    return pltpu.CompilerParams(vmem_limit_bytes=mebibytes * 1024 * 1024)


def in_hbm(array):
    return pltpu.with_memory_space_constraint(array, pltpu.HBM)


def shape(dims, dtype):
    return jax.ShapeDtypeStruct(dims, dtype)


def vmem(dims, dtype):
    return pltpu.VMEM(dims, dtype)


def product(left, right):
    return jnp.dot(left, right, preferred_element_type=jnp.float32)


def product_t(left, right):
    return lax.dot_general(left, right, (((1,), (1,)), ((), ())), preferred_element_type=jnp.float32)


def column_of(row):
    size = row.shape[1]
    first = lax.broadcasted_iota(jnp.int32, (size, size), 0)
    second = lax.broadcasted_iota(jnp.int32, (size, size), 1)
    return jnp.sum(jnp.where(first == second, row, 0.0), axis=1, keepdims=True)


IN_FLIGHT = 6
CHUNKS = 1


class Stream:
    def __init__(self, copies, in_flight):
        self.copies = copies
        self.in_flight = in_flight
        self.done = 0
        for copy in copies[:in_flight]:
            copy.start()

    def arrived(self, upto):
        while self.done <= upto:
            self.copies[self.done].wait()
            if self.done + self.in_flight < len(self.copies):
                self.copies[self.done + self.in_flight].start()
            self.done += 1


def temporal_kernel(
    place_ref, hidden_hbm, gain_hbm, lengths_hbm, qkv_hbm, out_hbm, keys_hbm, values_hbm, head_hbm, kept_ref, last_ref, sent_ref, columns_ref,
    hidden_buf, gain_buf, lengths_buf, qkv_buf, out_buf, keys_buf, values_buf, small_sems, sems, column_sems,
):
    streams, depth = hidden_buf.shape
    cols = qkv_buf.shape[2]
    heads = cols // HEAD_DIM
    cache_len = keys_buf.shape[1]
    steps, halves = QKV_STEPS, CACHE_STEPS
    chunk = depth // steps
    batch = streams // halves
    count, _, width = kept_ref.shape
    odd = place_ref[0] % 2
    place = place_ref[0] // 2
    small = [
        pltpu.make_async_copy(hidden_hbm, hidden_buf, small_sems.at[0]),
        pltpu.make_async_copy(gain_hbm, gain_buf, small_sems.at[1]),
        pltpu.make_async_copy(lengths_hbm, lengths_buf, small_sems.at[2]),
    ]
    for copy in small:
        copy.start()
    pairs = []
    for n in (0, 1):
        pairs += [(qkv_hbm.at[n, pl.ds(i * chunk, chunk)], qkv_buf.at[n, pl.ds(i * chunk, chunk)]) for i in range(steps)]
    pairs += [(keys_hbm.at[pl.ds(i * batch, batch)], keys_buf.at[pl.ds(i * batch, batch)]) for i in range(halves)]
    pairs += [(qkv_hbm.at[2, pl.ds(i * chunk, chunk)], qkv_buf.at[2, pl.ds(i * chunk, chunk)]) for i in range(steps)]
    pairs += [(values_hbm.at[pl.ds(i * batch, batch)], values_buf.at[pl.ds(i * batch, batch)]) for i in range(halves)]
    pairs += [
        (out_hbm.at[:, pl.ds(pl.multiple_of((place ^ k) * 2 * width, 2 * width), 2 * width)], out_buf.at[k])
        for k in range(count)
    ]
    _, half_codes, _, part = columns_ref.shape
    columns = []
    for k in range(count):
        start = pl.multiple_of(((place ^ k) * 2 + 1 - odd) * part, part)
        source = head_hbm.at[pl.ds(place_ref[2] * half_codes, half_codes), :, pl.ds(start, part)]
        columns.append(pltpu.make_async_copy(source, columns_ref.at[k], column_sems.at[k]))
    stream = Stream([pltpu.make_async_copy(src, dst, sems.at[i]) for i, (src, dst) in enumerate(pairs)], IN_FLIGHT)
    first_of = (0, steps, 2 * steps + halves)
    keys_end = 2 * steps + halves - 1
    values_end = 3 * steps + 2 * halves - 1

    for copy in small:
        copy.wait()
    wide = hidden_buf[...].astype(jnp.float32)
    inv = lax.rsqrt(jnp.mean(wide * wide, axis=1, keepdims=True) + EPSILON)
    normed = (wide * inv * gain_buf[...]).astype(jnp.bfloat16)

    def projected(n):
        total = None
        for i in range(steps):
            stream.arrived(first_of[n] + i)
            part = product(normed[:, i * chunk : (i + 1) * chunk], qkv_buf[n, pl.ds(i * chunk, chunk), :])
            total = part if total is None else total + part
        return total

    lengths_row = lengths_buf[...].astype(jnp.float32)
    lengths_col = column_of(lengths_row)
    half = HEAD_DIM // 2
    lane = lax.broadcasted_iota(jnp.int32, (streams, HEAD_DIM), 1)
    spacing = (lane & (half - 1)).astype(jnp.float32) / half
    angles = lengths_col * jnp.exp(-math.log(10000.0) * spacing)
    cosine = jnp.cos(angles)
    sine = jnp.where(lane < half, -1.0, 1.0) * jnp.sin(angles)

    def rotated(block):
        pieces = []
        for h in range(heads):
            piece = block[:, h * HEAD_DIM : (h + 1) * HEAD_DIM]
            pieces.append(piece * cosine + pltpu.roll(piece, half, 1) * sine)
        return jnp.concatenate(pieces, axis=1)

    queries = rotated(projected(0))
    for copy in columns:
        copy.start()
    keys_new = rotated(projected(1)).astype(jnp.bfloat16)
    head_lane = lax.broadcasted_iota(jnp.int32, (streams, cols), 1) // HEAD_DIM
    spread = jnp.concatenate(
        [jnp.where(head_lane == h, queries, 0.0) for h in range(heads)], axis=0
    ).astype(jnp.bfloat16)
    pairs = heads * streams
    factor = 1.0 / math.sqrt(HEAD_DIM)
    pair = lax.broadcasted_iota(jnp.int32, (1, pairs), 1)
    pair_stream = pair % streams
    own = product_t(keys_new, spread) * factor
    stream_row = lax.broadcasted_iota(jnp.int32, (streams, pairs), 0)
    own_score = jnp.sum(jnp.where(stream_row == pair_stream, own, 0.0), axis=0, keepdims=True)
    tiled = jnp.sum(jnp.where(stream_row == pair_stream, lengths_col, 0.0), axis=0, keepdims=True)
    first_row = pair_stream * cache_len
    last_row = first_row + tiled.astype(jnp.int32)
    stream.arrived(keys_end)
    rows = streams * cache_len
    scores = product_t(keys_buf[...].reshape(rows, cols), spread) * factor
    row = lax.broadcasted_iota(jnp.int32, (rows, pairs), 0)
    scores = jnp.where((row >= first_row) & (row < last_row), scores, -jnp.inf)
    highest = jnp.maximum(jnp.max(scores, axis=0, keepdims=True), own_score)
    expo = jnp.exp(scores - highest)
    own_expo = jnp.exp(own_score - highest)
    inverse = 1.0 / (jnp.sum(expo, axis=0, keepdims=True) + own_expo)
    weights = (expo * inverse).astype(jnp.bfloat16)
    own_weight = (own_expo * inverse).astype(jnp.bfloat16).astype(jnp.float32)
    values_new = projected(2).astype(jnp.bfloat16).astype(jnp.float32)
    stream.arrived(values_end)
    mixed_all = lax.dot_general(
        weights,
        values_buf[...].reshape(rows, cols),
        (((0,), (0,)), ((), ())),
        preferred_element_type=jnp.float32,
    )
    pair_lane = lax.broadcasted_iota(jnp.int32, (streams, pairs), 1)
    pair_row = lax.broadcasted_iota(jnp.int32, (streams, pairs), 0)
    mixed = []
    for h in range(heads):
        own_col = jnp.sum(
            jnp.where(pair_lane == pair_row + h * streams, own_weight, 0.0), axis=1, keepdims=True
        )
        lanes = slice(h * HEAD_DIM, (h + 1) * HEAD_DIM)
        mixed.append(
            mixed_all[h * streams : (h + 1) * streams, lanes] + own_col * values_new[:, lanes]
        )
    mixed = jnp.concatenate(mixed, axis=1).astype(jnp.bfloat16)
    for copy in columns:
        copy.wait()
    for k in range(count):
        stream.arrived(values_end + 1 + k)
        block = product(mixed, out_buf[k])
        even_side, odd_side = block[:, :width], block[:, width:]
        kept_ref[k] = jnp.where(odd == 1, odd_side, even_side)
        sent = jnp.where(odd == 1, even_side, odd_side).astype(jnp.bfloat16)
        if k == 0:
            last_ref[...] = sent
        else:
            sent_ref[k - 1] = sent


QKV_STEPS = 4
CACHE_STEPS = 2


def temporal_parts(place, hidden_in, gain, lengths, qkv, out_weight, keys, values, head_weight, places):
    codes, head_depth, vocab = head_weight.shape
    streams, depth = hidden_in.shape
    bf16 = jnp.bfloat16
    count, width = places // 2, out_weight.shape[1] // places
    block = (count, streams, width)
    return pl.pallas_call(
        temporal_kernel,
        in_specs=[SMEM] + [HBM] * 8,
        out_specs=[VMEM] * 4,
        out_shape=[
            vmem(block, jnp.float32),
            vmem(block[1:], bf16),
            vmem((count - 1,) + block[1:], bf16),
            vmem((count, codes // 2, head_depth, vocab // places), bf16),
        ],
        scratch_shapes=[
            pltpu.VMEM(hidden_in.shape, bf16),
            pltpu.VMEM((1, depth), jnp.float32),
            pltpu.VMEM((1, streams), jnp.int32),
            pltpu.VMEM(qkv.shape, bf16),
            pltpu.VMEM((count, out_weight.shape[0], 2 * width), bf16),
            pltpu.VMEM(keys.shape, bf16),
            pltpu.VMEM(values.shape, bf16),
            pltpu.SemaphoreType.DMA((3,)),
            pltpu.SemaphoreType.DMA((3 * QKV_STEPS + 2 * CACHE_STEPS + count,)),
            pltpu.SemaphoreType.DMA((count,)),
        ],
        compiler_params=params(30),
        name="temporal",
    )(
        place,
        in_hbm(hidden_in),
        in_hbm(gain.reshape(1, depth)),
        in_hbm(lengths.reshape(1, streams)),
        in_hbm(qkv),
        in_hbm(out_weight),
        in_hbm(keys),
        in_hbm(values),
        in_hbm(head_weight),
    )


def prepare_kernel(
    place_ref, tokens_ref, hidden_hbm, embed_hbm, weight_hbm, resid_ref, embedded_ref, weight_ref, embed_buf, sem, sems
):
    codes, vocab, _ = embed_buf.shape
    streams = tokens_ref.shape[0]
    part = resid_ref.shape[1]
    start = pl.multiple_of(place_ref[0] * part, part)
    resid = pltpu.make_async_copy(hidden_hbm.at[:, pl.ds(start, part)], resid_ref, sem)
    resid.start()
    embed = [pltpu.make_async_copy(embed_hbm.at[c], embed_buf.at[c], sems.at[0, c]) for c in range(codes)]
    weight = [pltpu.make_async_copy(weight_hbm.at[c], weight_ref.at[c], sems.at[1, c]) for c in range(codes)]
    stream = Stream(embed + weight, IN_FLIGHT)
    vocab_lane = lax.broadcasted_iota(jnp.int32, (streams, vocab), 1) + place_ref[0] * vocab
    for c in range(codes):
        hit = tokens_ref[:, c : c + 1] == vocab_lane
        onehot = jnp.where(hit, 1.0, 0.0).astype(jnp.bfloat16)
        stream.arrived(c)
        embedded_ref[c] = product(onehot, embed_buf[c])
    stream.arrived(2 * codes - 1)
    resid.wait()


def prepared_entry(place, tokens, hidden_in, embed, weight, places):
    codes, _, width = weight.shape
    streams = tokens.shape[0]
    resid_shape = (hidden_in.shape[0], hidden_in.shape[1] // places)
    return pl.pallas_call(
        prepare_kernel,
        in_specs=[SMEM, VMEM, HBM, HBM, HBM],
        out_specs=[VMEM] * 3,
        out_shape=[
            vmem(resid_shape, jnp.bfloat16),
            vmem((codes, streams, width), jnp.float32),
            vmem(weight.shape, jnp.bfloat16),
        ],
        scratch_shapes=[
            pltpu.VMEM(embed.shape, jnp.bfloat16),
            pltpu.SemaphoreType.DMA(()),
            pltpu.SemaphoreType.DMA((2, codes)),
        ],
        compiler_params=params(16),
        name="entry_prepare",
    )(place, tokens, in_hbm(hidden_in), in_hbm(embed), in_hbm(weight))


def near_kernel(place_ref, token_ref, gain_ref, qkv_hbm, out_hbm, head_hbm, own_ref, qkv_ref, out_ref, *rest):
    column_refs, (sems, column_sems) = rest[:-2], rest[-2:]
    del token_ref
    copies = [
        pltpu.make_async_copy(source.at[c], target.at[c], sems.at[i, c])
        for i, (source, target) in enumerate(((qkv_hbm, qkv_ref), (out_hbm, out_ref)))
        for c in range(source.shape[0])
    ]
    for n, out in enumerate(column_refs):
        count, codes, _, vocab_part = out.shape
        for k in range(count):
            start = pl.multiple_of(((place_ref[0] // 2 ^ k) * 2 + place_ref[0] % 2) * vocab_part, vocab_part)
            source = head_hbm.at[pl.ds(n * codes, codes), :, pl.ds(start, vocab_part)]
            copies.append(pltpu.make_async_copy(source, out.at[k], column_sems.at[n, k]))
    stream = Stream(copies, IN_FLIGHT)
    part = own_ref.shape[1]
    own_ref[...] = gain_ref[:, pl.ds(pl.multiple_of(place_ref[0] * part, part), part)]
    stream.arrived(len(copies) - 1)


def brought_near(place, token, gain, qkv, out_weight, head_weight, places):
    width = gain.shape[0]
    codes, depth, vocab = head_weight.shape
    columns = vmem((places // 2, codes // CHUNKS, depth, vocab // places), jnp.bfloat16)
    return pl.pallas_call(
        near_kernel,
        in_specs=[SMEM, VMEM, VMEM, HBM, HBM, HBM],
        out_specs=[VMEM] * (3 + CHUNKS),
        out_shape=[
            vmem((1, width // places), jnp.float32),
            vmem(qkv.shape, jnp.bfloat16),
            vmem(out_weight.shape, jnp.bfloat16),
        ]
        + [columns] * CHUNKS,
        scratch_shapes=[
            pltpu.SemaphoreType.DMA((2, qkv.shape[0])),
            pltpu.SemaphoreType.DMA((CHUNKS, places // 2)),
        ],
        compiler_params=params(16),
        name="brought_near",
    )(place, token, gain.reshape(1, width), in_hbm(qkv), in_hbm(out_weight), in_hbm(head_weight))


def entry_kernel(
    place_ref, own_ref, other_ref, embedded_ref, weight_ref, kept_ref, last_ref, sent_ref, token_ref, total_buf
):
    token_ref[...] = jnp.zeros_like(token_ref)
    codes = weight_ref.shape[0]
    count, _, _, part = kept_ref.shape
    odd = place_ref[0] % 2
    place = place_ref[0] // 2
    first_section = place_ref[1] == 0
    own, other = own_ref[...], other_ref[...]
    rows = jnp.concatenate(
        [jnp.where(first_section, own, other), jnp.where(first_section, other, own)], axis=0
    )
    for c in range(codes):
        total_buf[...] = embedded_ref[c] + product(rows, weight_ref[c])
        for k in range(count):
            pair = (place ^ k) * 2
            kept_ref[k, c] = total_buf[:, pl.ds(pl.multiple_of((pair + odd) * part, part), part)]
            sent = total_buf[:, pl.ds(pl.multiple_of((pair + 1 - odd) * part, part), part)].astype(jnp.bfloat16)
            if k == 0:
                last_ref[c] = sent
            else:
                sent_ref[k - 1, c] = sent


def entry_parts(place, own, other, embedded, weight, places):
    codes, _, width = weight.shape
    streams = 2 * own.shape[0]
    block = (places // 2, codes, streams, width // places)
    return pl.pallas_call(
        entry_kernel,
        in_specs=[SMEM] + [VMEM] * 4,
        out_specs=[VMEM] * 4,
        out_shape=[
            vmem(block, jnp.float32),
            vmem(block[1:], jnp.bfloat16),
            vmem((places // 2 - 1,) + block[1:], jnp.bfloat16),
            vmem((8, 128), jnp.float32),
        ],
        scratch_shapes=[pltpu.VMEM((streams, width), jnp.float32)],
        compiler_params=params(16),
        name="entry",
    )(place, own, other, embedded, weight)


def nearest_last(far):
    return list(range(1, far)) + [0]


def qkv_kernel(count, place_ref, gain_ref, weight_ref, far_ref, *rest):
    near_refs, (last_ref, queries_ref, pair_ref) = rest[:count], rest[count:]
    codes, _, width, cols = weight_ref.shape
    part = last_ref.shape[2]
    odd = place_ref[0] % 2
    place = place_ref[0] // 2
    order = [0] + [k + 1 for k in nearest_last(count - 1)]
    starts = [pl.multiple_of(((place ^ k) * 2 + side) * part, part) for side in (odd, 1 - odd) for k in order]
    inverse_gain = 1.0 / jnp.concatenate([gain_ref[:, pl.ds(start, part)] for start in starts], axis=1)
    for c in range(codes):
        blocks = [ref[c] for ref in near_refs] + [last_ref[c]] + [far_ref[k, c] for k in range(count - 1)]
        row = jnp.concatenate(blocks, axis=1)
        plain = row.astype(jnp.float32) * inverse_gain
        inv = lax.rsqrt(jnp.sum(plain * plain, axis=1, keepdims=True) / width + EPSILON)
        for n in range(3):
            weight = jnp.concatenate([weight_ref[c, n, pl.ds(start, part), :] for start in starts], axis=0)
            value = (product(row, weight) * inv).astype(jnp.bfloat16)
            if n == 0:
                queries_ref[c] = value
            else:
                pair_ref[n - 1, c] = value


def depth_projections(place, near, last, far, gain, weight):
    codes, _, width, cols = weight.shape
    streams = last.shape[1]
    bf16 = jnp.bfloat16
    return pl.pallas_call(
        functools.partial(qkv_kernel, len(near)),
        in_specs=[SMEM] + [VMEM] * (4 + len(near)),
        out_specs=[VMEM] * 2,
        out_shape=[vmem((codes, streams, cols), bf16), vmem((2, codes, streams, cols), bf16)],
        compiler_params=params(16),
        name="depth_qkv",
    )(place, gain.reshape(1, width), weight, far, *near, last)


def mix_kernel(terms, place_ref, queries_ref, own_ref, prior_ref, weight_ref, *rest):
    entry_refs, outs, total_buf = rest[:terms], rest[terms:-1], rest[-1]
    codes, streams, cols = queries_ref.shape
    each, _, span = outs[0].shape
    count = len(outs) // CHUNKS
    has_prior = place_ref[1] > 0
    first = lax.broadcasted_iota(jnp.int32, (2 * cols, cols), 0) % cols
    second = lax.broadcasted_iota(jnp.int32, (2 * cols, cols), 1)
    same = jnp.where(first // DEPTH_HDIM == second // DEPTH_HDIM, 1.0, 0.0).astype(jnp.bfloat16)
    keys = [prior_ref[0, j].astype(jnp.float32) for j in range(codes)]
    keys += [own_ref[0, j].astype(jnp.float32) for j in range(codes)]
    values = [prior_ref[1, j].astype(jnp.float32) for j in range(codes)]
    values += [own_ref[1, j].astype(jnp.float32) for j in range(codes)]
    factor = 1.0 / math.sqrt(DEPTH_HDIM)
    mixed = []
    for q in range(codes):
        query = queries_ref[q].astype(jnp.float32)
        reach = codes + q + 1
        pieces = []
        for j in range(reach):
            exact = query * keys[j]
            high = exact.astype(jnp.bfloat16)
            low = (exact - high.astype(jnp.float32)).astype(jnp.bfloat16)
            pieces.append(jnp.concatenate([high, low], axis=1))
        scores = product(jnp.concatenate(pieces, axis=0), same) * factor
        score = [scores[j * streams : (j + 1) * streams] for j in range(reach)]
        score = [jnp.where(has_prior, s, -jnp.inf) if j < codes else s for j, s in enumerate(score)]
        top = score[0]
        for s in score[1:]:
            top = jnp.maximum(top, s)
        expo = [jnp.exp(s - top) for s in score]
        inverse = 1.0 / sum(expo)
        total = jnp.zeros_like(query)
        for j in range(reach):
            total = total + (expo[j] * inverse).astype(jnp.bfloat16).astype(jnp.float32) * values[j]
        mixed.append(total.astype(jnp.bfloat16))
    for q in range(codes):
        total_buf[q] = product(mixed[q], weight_ref[q])
    part = entry_refs[0].shape[2]
    own_part = pl.ds(pl.multiple_of(place_ref[0] * part, part), part)
    total_buf[:, :, own_part] += sum(ref[...].astype(jnp.float32) for ref in entry_refs)
    place = place_ref[0] // 2
    for n, out in enumerate(outs):
        chunk, k = divmod(n, count)
        start = pl.multiple_of((place ^ k) * span, span)
        block = total_buf[pl.ds(chunk * each, each), :, pl.ds(start, span)]
        out[...] = block if k == 0 else block.astype(jnp.bfloat16)


def mixed_parts(place, queries, own, prior, weight, entry_terms, far):
    codes, streams, cols = queries.shape
    width = weight.shape[2]
    block = (codes // CHUNKS, streams, width // (far + 1))
    outs = pl.pallas_call(
        functools.partial(mix_kernel, len(entry_terms)),
        in_specs=[SMEM] + [VMEM] * (4 + len(entry_terms)),
        out_specs=[VMEM] * ((far + 1) * CHUNKS),
        out_shape=([vmem(block, jnp.float32)] + [vmem(block, jnp.bfloat16)] * far) * CHUNKS,
        scratch_shapes=[pltpu.VMEM((codes, streams, width), jnp.float32)],
        compiler_params=params(16),
        name="depth_mix",
    )(place, queries, own, prior, weight, *entry_terms)
    return [outs[n * (far + 1) : (n + 1) * (far + 1)] for n in range(CHUNKS)]


STAT_ROWS = 16


def head_kernel(
    first, place_ref, gain_ref, total_ref, arrived_ref, weight_ref, early_ref, late_ref, kept_ref, stat_ref, *sends
):
    half = early_ref.shape[1]

    def partner(k, c):
        side, index = divmod(first + c, half)
        return jnp.where(place_ref[2] == side, early_ref[k, index], late_ref[k, index])

    codes, streams, span = total_ref.shape
    count, _, depth, part = weight_ref.shape
    odd = place_ref[0] % 2
    resid = total_ref[...] + arrived_ref[...].astype(jnp.float32)
    flat = resid.reshape(codes * streams, span)
    squares = flat * flat
    stat = product_t(jnp.ones((STAT_ROWS // 2, span), jnp.float32), squares)[:1]
    stat_ref[...] = stat
    high = stat.astype(jnp.bfloat16).astype(jnp.float32)
    stat_row = lax.broadcasted_iota(jnp.int32, (STAT_ROWS, codes * streams), 0)
    stat_block = jnp.where(stat_row == 0, high, jnp.where(stat_row == 1, stat - high, 0.0))
    if part > codes * streams:
        rest = jnp.zeros((STAT_ROWS, part - codes * streams), jnp.float32)
        stat_block = jnp.concatenate([stat_block, rest], axis=1)
    stat_block = stat_block.astype(jnp.bfloat16)
    scaled = resid * gain_ref[...]
    low_half, high_half = scaled[:, :, :depth], scaled[:, :, depth:]
    ordered = jnp.concatenate(
        [jnp.where(odd == 1, high_half, low_half), jnp.where(odd == 1, low_half, high_half)], axis=2
    ).astype(jnp.bfloat16)
    rows = codes * streams
    for k in range(count):
        block = jnp.concatenate(
            [
                product(ordered[c], jnp.concatenate([weight_ref[k, c], partner(k, c)], axis=0))
                for c in range(codes)
            ],
            axis=0,
        )
        if k == 0:
            kept_ref[...] = block
        else:
            sends[k - 1][pl.ds(0, rows), :] = block.astype(jnp.bfloat16)
            sends[k - 1][pl.ds(rows, STAT_ROWS), :] = stat_block


def head_parts(first, place, gain, total, arrived, weight, early, late):
    codes, streams, span = total.shape
    count, _, depth, part = weight.shape
    rows = codes * streams
    return pl.pallas_call(
        functools.partial(head_kernel, first),
        in_specs=[SMEM] + [VMEM] * 6,
        out_specs=[VMEM] * (count + 1),
        out_shape=[vmem((rows, part), jnp.float32), vmem((1, rows), jnp.float32)]
        + [vmem((rows + STAT_ROWS, part), jnp.bfloat16)] * (count - 1),
        compiler_params=params(16),
        name="head",
    )(place, gain, total, arrived, weight, early, late)


def logits_kernel(width, *refs):
    out_ref = refs[-1]
    streams, codes, part = out_ref.shape
    each = codes // CHUNKS
    rows = each * streams
    count = (len(refs) - 1) // CHUNKS
    for n in range(CHUNKS):
        kept_ref, stat_ref, *arrived = refs[n * count : (n + 1) * count]
        total = kept_ref[...]
        stat = stat_ref[...]
        for block in arrived:
            wide = block[...].astype(jnp.float32)
            total = total + wide[:rows]
            stat = stat + wide[rows : rows + 1, :rows] + wide[rows + 1 : rows + 2, :rows]
        total = total * column_of(lax.rsqrt(stat / width + EPSILON))
        for c in range(each):
            out_ref[:, n * each + c, :] = total[c * streams : (c + 1) * streams]


def finished_logits(chunks, streams, codes, width):
    part = chunks[0][0].shape[1]
    arrays = [array for chunk in chunks for array in chunk]
    return pl.pallas_call(
        functools.partial(logits_kernel, width),
        in_specs=[VMEM] * len(arrays),
        out_specs=VMEM,
        out_shape=shape((streams, codes, part), jnp.float32),
        compiler_params=params(16),
        name="logits",
    )(*arrays)


def paired_device(
    hidden_in,
    temporal_gain,
    temporal_qkv,
    temporal_out_weight,
    cache_keys,
    cache_values,
    lengths,
    depth_in,
    depth_embed,
    depth_gain,
    depth_qkv,
    depth_out_weight,
    head_gain,
    head_weight,
    tokens,
):
    tp = lax.axis_size("tp")
    tp_place = lax.axis_index("tp")
    place = jnp.stack([tp_place, lax.axis_index("section"), lax.axis_index("grp") % 2])
    far = tp // 2 - 1

    def to_pairs(blocks):
        arrived = [None] * len(blocks)
        for k in reversed(range(len(blocks))):
            arrived[k] = lax.ppermute(blocks[k], "tp", [(i, i ^ 2 * (k + 1)) for i in range(tp)])
        return arrived

    order = nearest_last(far)

    def in_order(blocks, order):
        return [blocks[k] for k in order]

    def to_neighbour(block):
        return lax.ppermute(block, "tp", [(i, i ^ 1) for i in range(tp)])

    def summed(kept, last, sent, order):
        folded = kept[1:] + to_neighbour(sent).astype(jnp.float32)
        arrived = to_pairs([folded[k].astype(jnp.bfloat16) for k in range(far)])
        return [kept[0]] + [arrived[k] for k in order] + [to_neighbour(last)]

    def added(terms):
        return sum(term.astype(jnp.float32) for term in terms)

    kept, last, sent, neighbour_columns = temporal_parts(
        place,
        hidden_in,
        temporal_gain,
        lengths,
        temporal_qkv,
        temporal_out_weight,
        cache_keys,
        cache_values,
        head_weight,
        tp,
    )
    sent, depth_in = lax.optimization_barrier((sent, depth_in))
    early = to_neighbour(neighbour_columns)
    resid_in, embedded, near_in = prepared_entry(place, tokens, hidden_in, depth_embed, depth_in, tp)
    temporal = (resid_in.astype(jnp.float32) + added(summed(kept, last, sent, order))).astype(jnp.bfloat16)
    other_rows = lax.ppermute(temporal, "section", [(0, 1), (1, 0)])
    codes = depth_in.shape[0]
    width = depth_in.shape[2]
    hidden_rows = head_weight.shape[1]
    kept, last, sent, token = entry_parts(place, temporal, other_rows, embedded, near_in, tp)
    sent, early = lax.optimization_barrier((sent, early))
    late = lax.ppermute(early, "grp", [(i, i ^ 1) for i in range(lax.axis_size("grp"))])
    own_gain, near_qkv, near_out, *own_columns = brought_near(
        place, token, depth_gain, depth_qkv, depth_out_weight, head_weight, tp
    )
    entry_terms = summed(kept, last, sent, order)
    scaled = (added(entry_terms) * own_gain[None]).astype(jnp.bfloat16)
    near = [scaled] + in_order(to_pairs([scaled] * far), order)
    last = to_neighbour(scaled)
    queries, own_pair = depth_projections(
        place, near, last, to_neighbour(jnp.stack(near[1:])), depth_gain, near_qkv
    )
    prior_pair = passed_along(own_pair, "section", 1)
    chunks = mixed_parts(place, queries, own_pair, prior_pair, near_out, entry_terms, far)
    pair_gain = lax.dynamic_slice_in_dim(head_gain, tp_place // 2 * 2 * hidden_rows, 2 * hidden_rows, 0)
    each = codes // CHUNKS
    arrived = [in_order(to_pairs(blocks), order) for _, *blocks in chunks]
    totals = [
        kept + added(blocks) for (kept, *_), blocks in zip(chunks, arrived)
    ]
    others = [to_neighbour(total.astype(jnp.bfloat16)) for total in totals]
    heads = [
        head_parts(n * each, place, pair_gain.reshape(1, 1, -1), total, other, own, early, late)
        for n, (total, other, own) in enumerate(zip(totals, others, own_columns))
    ]
    finished = [[kept, stat, *in_order(to_pairs(blocks), order)] for kept, stat, *blocks in heads]
    logits = finished_logits(finished, sent.shape[2], codes, width)
    return (temporal, logits)


def per_device(*arrays):
    hidden_in, temporal_qkv, depth_qkv, head_weight = arrays[0], arrays[2], arrays[10], arrays[13]
    depth_in, tokens = arrays[7], arrays[14]
    tp = lax.axis_size("tp")
    pairs = hidden_in.shape[0] * (temporal_qkv.shape[2] // HEAD_DIM)
    whole_tiles = (
        pairs % 128 == 0
        and temporal_qkv.shape[2] % HEAD_DIM == 0
        and head_weight.shape[1] % 128 == 0
        and head_weight.shape[2] // tp % 128 == 0
        and depth_qkv.shape[3] % 128 == 0
        and tp >= 4
        and depth_in.shape[0] % (2 * CHUNKS) == 0
        and lax.axis_size("grp") % 2 == 0
        and depth_in.shape[0] // CHUNKS * tokens.shape[0] <= head_weight.shape[2] // tp
        and tp & (tp - 1) == 0
    )
    return (paired_device if whole_tiles else general_device)(*arrays)


def solution(mesh):
    return jax.shard_map(
        per_device,
        mesh=mesh,
        in_specs=(
            P(("grp", "section"), None),
            P(),
            P(None, None, "tp"),
            P("tp", None),
            P(("grp", "section"), None, "tp"),
            P(("grp", "section"), None, "tp"),
            P(("grp", "section")),
            P("section", "tp", None),
            P("section", "tp", None),
            P(),
            P("section", None, None, "tp"),
            P("section", "tp", None),
            P(),
            P("section", "tp", None),
            P("grp", "section"),
        ),
        out_specs=(P(("grp", "section"), "tp"), P("grp", "section", "tp")),
        check_vma=False,
    )
```

```python
import functools
import math

import jax
import jax.numpy as jnp
from jax import lax
from jax.experimental import pallas as pl
from jax.experimental.pallas import tpu as pltpu
from jax.sharding import PartitionSpec as P

HEAD_DIM = 128
DEPTH_HDIM = 64


EPSILON = 1e-05


def passed_along(block, axis, distance):
    devices = range(lax.axis_size(axis))
    route = [(i - distance, i) for i in devices if i - distance in devices]
    return lax.ppermute(block, axis, route)


def from_partner(shard, axis, distance):
    return lax.ppermute(shard, axis, [(i, i ^ 1 << distance) for i in range(lax.axis_size(axis))])


def rms_norm(values, scale):
    wide = values.astype(jnp.float32)
    return wide * lax.rsqrt(jnp.mean(wide * wide, axis=-1, keepdims=True) + EPSILON) * scale


def rotate(vectors, positions):
    halfdim = vectors.shape[-1] // 2
    spacing = jnp.arange(halfdim, dtype=jnp.float32) / halfdim
    inverse = jnp.exp(-math.log(10000.0) * spacing)
    angles = positions.astype(jnp.float32)[:, None, None] * inverse[None, None, :]
    cosine = jnp.cos(angles)
    sine = jnp.sin(angles)
    first = vectors[..., :halfdim]
    second = vectors[..., halfdim:]
    return jnp.concatenate(
        [first * cosine - second * sine, first * sine + second * cosine], axis=-1
    )


def scattered_sum(parts):
    moved = lax.all_to_all(parts.astype(jnp.bfloat16), "tp", 0, 0)
    return jnp.sum(moved.astype(jnp.float32), axis=0)


def gathered(block):
    size = lax.axis_size("tp")
    return lax.all_to_all(jnp.broadcast_to(block[None], (size,) + block.shape), "tp", 0, 0)


def general_device(
    hidden_in,
    temporal_gain,
    temporal_qkv,
    temporal_out_weight,
    cache_keys,
    cache_values,
    lengths,
    depth_in,
    depth_embed,
    depth_gain,
    depth_qkv,
    depth_out_weight,
    head_gain,
    head_weight,
    tokens,
):
    tp = lax.axis_size("tp")
    local_streams = hidden_in.shape[0]
    local_cols = temporal_qkv.shape[2]
    local_heads = local_cols // HEAD_DIM
    cache_len = cache_keys.shape[1]
    normed = rms_norm(hidden_in, temporal_gain).astype(jnp.bfloat16)
    projected = jnp.einsum("sd,tdf->tsf", normed, temporal_qkv, preferred_element_type=jnp.float32)
    layout = (local_streams, local_heads, HEAD_DIM)
    queries = rotate(projected[0].reshape(layout), lengths).astype(jnp.bfloat16)
    keys_new = rotate(projected[1].reshape(layout), lengths).astype(jnp.bfloat16)
    values_new = projected[2].reshape(layout).astype(jnp.bfloat16)
    cached_keys = cache_keys.reshape(local_streams, cache_len, local_heads, HEAD_DIM)
    cached_values = cache_values.reshape(local_streams, cache_len, local_heads, HEAD_DIM)
    factor = 1.0 / math.sqrt(HEAD_DIM)
    scores = (
        jnp.einsum("shd,sphd->shp", queries, cached_keys, preferred_element_type=jnp.float32)
        * factor
    )
    own_score = (
        jnp.sum(queries.astype(jnp.float32) * keys_new.astype(jnp.float32), axis=-1) * factor
    )
    valid = jnp.arange(cache_len, dtype=jnp.int32)[None, None, :] < lengths[:, None, None]
    scores = jnp.where(valid, scores, -jnp.inf)
    highest = jnp.maximum(jnp.max(scores, axis=-1), own_score)
    expo = jnp.exp(scores - highest[..., None])
    own_expo = jnp.exp(own_score - highest)
    totals = jnp.sum(expo, axis=-1) + own_expo
    weights = (expo / totals[..., None]).astype(jnp.bfloat16)
    own_weight = (own_expo / totals).astype(jnp.bfloat16)
    mixed = jnp.einsum("shp,sphd->shd", weights, cached_values, preferred_element_type=jnp.float32)
    mixed = mixed + own_weight.astype(jnp.float32)[..., None] * values_new.astype(jnp.float32)
    mixed = mixed.astype(jnp.bfloat16).reshape(local_streams, local_cols)
    partial_rows = jnp.dot(mixed, temporal_out_weight, preferred_element_type=jnp.float32)
    slice_width = partial_rows.shape[1] // tp
    by_slice = partial_rows.reshape(local_streams, tp, slice_width).transpose(1, 0, 2)
    summed = scattered_sum(by_slice)
    tp_place = lax.axis_index("tp")
    resid_in = lax.dynamic_slice_in_dim(hidden_in, tp_place * slice_width, slice_width, 1)
    temporal = (resid_in.astype(jnp.float32) + summed).astype(jnp.bfloat16)
    all_rows = lax.all_gather(temporal, "section", axis=0, tiled=True)
    streams = all_rows.shape[0]
    codes = depth_in.shape[0]
    width = depth_in.shape[2]
    vocab_local = depth_embed.shape[1]
    first_id = tp_place * vocab_local
    onehot = (
        tokens[:, :, None] == first_id + jnp.arange(vocab_local, dtype=jnp.int32)[None, None, :]
    ).astype(jnp.bfloat16)
    embedded = jnp.einsum("scv,cve->cse", onehot, depth_embed, preferred_element_type=jnp.float32)
    entry_terms = embedded + jnp.einsum(
        "sd,cde->cse", all_rows, depth_in, preferred_element_type=jnp.float32
    )
    hidden_rows = head_weight.shape[1]
    hidden_start = tp_place * hidden_rows
    entry = scattered_sum(entry_terms.reshape(codes, streams, tp, hidden_rows).transpose(2, 0, 1, 3))
    own_gain = lax.dynamic_slice_in_dim(depth_gain, hidden_start, hidden_rows, 0)
    scaled = (entry * own_gain).astype(jnp.bfloat16)
    rows = gathered(scaled)
    plain = rows.astype(jnp.float32) / depth_gain.reshape(tp, 1, 1, hidden_rows)
    inv_rms = lax.rsqrt(jnp.sum(plain * plain, axis=(0, 3)) / width + EPSILON)
    dproj = jnp.einsum(
        "tcse,cntef->ncsf",
        rows,
        depth_qkv.reshape(codes, 3, tp, hidden_rows, -1),
        preferred_element_type=jnp.float32,
    )
    dproj = (dproj * inv_rms[None, :, :, None]).astype(jnp.bfloat16)
    prior = passed_along(dproj[1:], "section", 1)
    depth_cols = dproj.shape[3]
    head_part = min(depth_cols, DEPTH_HDIM)
    local_parts = depth_cols // head_part
    sharers = DEPTH_HDIM // head_part
    both = jnp.concatenate([prior, dproj[1:]], axis=1)
    all_keys = both[0].reshape(2 * codes, streams, local_parts, head_part)
    all_values = both[1].reshape(2 * codes, streams, local_parts, head_part)
    depth_queries = dproj[0].reshape(codes, streams, local_parts, head_part)
    depth_scores = jnp.sum(
        depth_queries[:, None].astype(jnp.float32) * all_keys[None].astype(jnp.float32), axis=-1
    )
    for level in range(sharers.bit_length() - 1):
        depth_scores = depth_scores + from_partner(depth_scores, "tp", level)
    depth_scores = depth_scores * (1.0 / math.sqrt(DEPTH_HDIM))
    section_place = lax.axis_index("section")
    query_pos = jnp.arange(codes, dtype=jnp.int32)[:, None]
    key_pos = jnp.arange(2 * codes, dtype=jnp.int32)[None, :]
    allowed = jnp.where(key_pos < codes, section_place > 0, key_pos - codes <= query_pos)
    depth_scores = jnp.where(allowed[:, :, None, None], depth_scores, -jnp.inf)
    depth_top = jnp.max(depth_scores, axis=1, keepdims=True)
    depth_expo = jnp.exp(depth_scores - depth_top)
    depth_weights = (depth_expo / jnp.sum(depth_expo, axis=1, keepdims=True)).astype(jnp.bfloat16)
    depth_mixed = jnp.sum(
        depth_weights[..., None].astype(jnp.float32) * all_values[None].astype(jnp.float32), axis=1
    ).astype(jnp.bfloat16)
    depth_mixed = depth_mixed.reshape(codes, streams, depth_cols)
    depth_terms = jnp.einsum(
        "csf,cfe->cse", depth_mixed, depth_out_weight, preferred_element_type=jnp.float32
    )
    added = scattered_sum(depth_terms.reshape(codes, streams, tp, hidden_rows).transpose(2, 0, 1, 3))
    resid = entry + added
    own_head_gain = lax.dynamic_slice_in_dim(head_gain, hidden_start, hidden_rows, 0)
    own_hidden = (resid * own_head_gain).astype(jnp.bfloat16)
    squares = jnp.sum(resid * resid, axis=2)
    high = squares.astype(jnp.bfloat16)
    low = (squares - high.astype(jnp.float32)).astype(jnp.bfloat16)
    partial_logits = jnp.einsum(
        "cse,cev->csv", own_hidden, head_weight, preferred_element_type=jnp.float32
    )
    vocab_slice = partial_logits.shape[2] // tp
    outgoing = partial_logits.reshape(codes, streams, tp, vocab_slice).transpose(2, 0, 1, 3)
    outgoing = outgoing.astype(jnp.bfloat16).reshape(tp, codes * streams, vocab_slice)
    extra = jnp.stack([high.reshape(-1), low.reshape(-1)])
    extra = jnp.pad(extra, ((0, 14), (0, 0))).reshape(-1, vocab_slice)
    packed = jnp.concatenate(
        [outgoing, jnp.broadcast_to(extra[None], (tp,) + extra.shape)], axis=1
    )
    moved = lax.all_to_all(packed, "tp", 0, 0).astype(jnp.float32)
    rows_total = jnp.sum(moved, axis=0)
    stats = rows_total[codes * streams :].reshape(16, codes, streams)
    head_inv = lax.rsqrt((stats[0] + stats[1]) / width + EPSILON)
    logits = rows_total[: codes * streams].reshape(codes, streams, vocab_slice) * head_inv[..., None]
    return (temporal, logits.transpose(1, 0, 2))


HBM = pl.BlockSpec(memory_space=pltpu.HBM)
VMEM = pl.BlockSpec(memory_space=pltpu.VMEM)
SMEM = pl.BlockSpec(memory_space=pltpu.SMEM)


def params(mebibytes):
    return pltpu.CompilerParams(vmem_limit_bytes=mebibytes * 1024 * 1024)


def in_hbm(array):
    return pltpu.with_memory_space_constraint(array, pltpu.HBM)


def shape(dims, dtype):
    return jax.ShapeDtypeStruct(dims, dtype)


def vmem(dims, dtype):
    return pltpu.VMEM(dims, dtype)


def product(left, right):
    return jnp.dot(left, right, preferred_element_type=jnp.float32)


def product_t(left, right):
    return lax.dot_general(left, right, (((1,), (1,)), ((), ())), preferred_element_type=jnp.float32)


def column_of(row):
    size = row.shape[1]
    first = lax.broadcasted_iota(jnp.int32, (size, size), 0)
    second = lax.broadcasted_iota(jnp.int32, (size, size), 1)
    return jnp.sum(jnp.where(first == second, row, 0.0), axis=1, keepdims=True)


IN_FLIGHT = 6
CHUNKS = 1


class Stream:
    def __init__(self, copies, in_flight):
        self.copies = copies
        self.in_flight = in_flight
        self.done = 0
        for copy in copies[:in_flight]:
            copy.start()

    def arrived(self, upto):
        while self.done <= upto:
            self.copies[self.done].wait()
            if self.done + self.in_flight < len(self.copies):
                self.copies[self.done + self.in_flight].start()
            self.done += 1


def temporal_kernel(
    place_ref, hidden_hbm, gain_hbm, lengths_hbm, qkv_hbm, out_hbm, keys_hbm, values_hbm, head_hbm, kept_ref, last_ref, sent_ref, columns_ref,
    hidden_buf, gain_buf, lengths_buf, qkv_buf, out_buf, keys_buf, values_buf, small_sems, sems, column_sems,
):
    streams, depth = hidden_buf.shape
    cols = qkv_buf.shape[2]
    heads = cols // HEAD_DIM
    cache_len = keys_buf.shape[1]
    steps, halves = QKV_STEPS, CACHE_STEPS
    chunk = depth // steps
    batch = streams // halves
    count, _, width = kept_ref.shape
    odd = place_ref[0] % 2
    place = place_ref[0] // 2
    small = [
        pltpu.make_async_copy(hidden_hbm, hidden_buf, small_sems.at[0]),
        pltpu.make_async_copy(gain_hbm, gain_buf, small_sems.at[1]),
        pltpu.make_async_copy(lengths_hbm, lengths_buf, small_sems.at[2]),
    ]
    for copy in small:
        copy.start()
    pairs = []
    for n in (0, 1):
        pairs += [(qkv_hbm.at[n, pl.ds(i * chunk, chunk)], qkv_buf.at[n, pl.ds(i * chunk, chunk)]) for i in range(steps)]
    pairs += [(keys_hbm.at[pl.ds(i * batch, batch)], keys_buf.at[pl.ds(i * batch, batch)]) for i in range(halves)]
    pairs += [(qkv_hbm.at[2, pl.ds(i * chunk, chunk)], qkv_buf.at[2, pl.ds(i * chunk, chunk)]) for i in range(steps)]
    pairs += [(values_hbm.at[pl.ds(i * batch, batch)], values_buf.at[pl.ds(i * batch, batch)]) for i in range(halves)]
    pairs += [
        (out_hbm.at[:, pl.ds(pl.multiple_of((place ^ k) * 2 * width, 2 * width), 2 * width)], out_buf.at[k])
        for k in range(count)
    ]
    _, half_codes, _, part = columns_ref.shape
    columns = []
    for k in range(count):
        start = pl.multiple_of(((place ^ k) * 2 + 1 - odd) * part, part)
        source = head_hbm.at[pl.ds(place_ref[2] * half_codes, half_codes), :, pl.ds(start, part)]
        columns.append(pltpu.make_async_copy(source, columns_ref.at[k], column_sems.at[k]))
    stream = Stream([pltpu.make_async_copy(src, dst, sems.at[i]) for i, (src, dst) in enumerate(pairs)], IN_FLIGHT)
    first_of = (0, steps, 2 * steps + halves)
    keys_end = 2 * steps + halves - 1
    values_end = 3 * steps + 2 * halves - 1

    for copy in small:
        copy.wait()
    wide = hidden_buf[...].astype(jnp.float32)
    inv = lax.rsqrt(jnp.mean(wide * wide, axis=1, keepdims=True) + EPSILON)
    normed = (wide * inv * gain_buf[...]).astype(jnp.bfloat16)

    def projected(n):
        total = None
        for i in range(steps):
            stream.arrived(first_of[n] + i)
            part = product(normed[:, i * chunk : (i + 1) * chunk], qkv_buf[n, pl.ds(i * chunk, chunk), :])
            total = part if total is None else total + part
        return total

    lengths_row = lengths_buf[...].astype(jnp.float32)
    lengths_col = column_of(lengths_row)
    half = HEAD_DIM // 2
    lane = lax.broadcasted_iota(jnp.int32, (streams, HEAD_DIM), 1)
    spacing = (lane & (half - 1)).astype(jnp.float32) / half
    angles = lengths_col * jnp.exp(-math.log(10000.0) * spacing)
    cosine = jnp.cos(angles)
    sine = jnp.where(lane < half, -1.0, 1.0) * jnp.sin(angles)

    def rotated(block):
        pieces = []
        for h in range(heads):
            piece = block[:, h * HEAD_DIM : (h + 1) * HEAD_DIM]
            pieces.append(piece * cosine + pltpu.roll(piece, half, 1) * sine)
        return jnp.concatenate(pieces, axis=1)

    queries = rotated(projected(0))
    for copy in columns:
        copy.start()
    keys_new = rotated(projected(1)).astype(jnp.bfloat16)
    head_lane = lax.broadcasted_iota(jnp.int32, (streams, cols), 1) // HEAD_DIM
    spread = jnp.concatenate(
        [jnp.where(head_lane == h, queries, 0.0) for h in range(heads)], axis=0
    ).astype(jnp.bfloat16)
    pairs = heads * streams
    factor = 1.0 / math.sqrt(HEAD_DIM)
    pair = lax.broadcasted_iota(jnp.int32, (1, pairs), 1)
    pair_stream = pair % streams
    own = product_t(keys_new, spread) * factor
    stream_row = lax.broadcasted_iota(jnp.int32, (streams, pairs), 0)
    own_score = jnp.sum(jnp.where(stream_row == pair_stream, own, 0.0), axis=0, keepdims=True)
    tiled = jnp.sum(jnp.where(stream_row == pair_stream, lengths_col, 0.0), axis=0, keepdims=True)
    first_row = pair_stream * cache_len
    last_row = first_row + tiled.astype(jnp.int32)
    stream.arrived(keys_end)
    rows = streams * cache_len
    scores = product_t(keys_buf[...].reshape(rows, cols), spread) * factor
    row = lax.broadcasted_iota(jnp.int32, (rows, pairs), 0)
    scores = jnp.where((row >= first_row) & (row < last_row), scores, -jnp.inf)
    highest = jnp.maximum(jnp.max(scores, axis=0, keepdims=True), own_score)
    expo = jnp.exp(scores - highest)
    own_expo = jnp.exp(own_score - highest)
    inverse = 1.0 / (jnp.sum(expo, axis=0, keepdims=True) + own_expo)
    weights = (expo * inverse).astype(jnp.bfloat16)
    own_weight = (own_expo * inverse).astype(jnp.bfloat16).astype(jnp.float32)
    values_new = projected(2).astype(jnp.bfloat16).astype(jnp.float32)
    stream.arrived(values_end)
    mixed_all = lax.dot_general(
        weights,
        values_buf[...].reshape(rows, cols),
        (((0,), (0,)), ((), ())),
        preferred_element_type=jnp.float32,
    )
    pair_lane = lax.broadcasted_iota(jnp.int32, (streams, pairs), 1)
    pair_row = lax.broadcasted_iota(jnp.int32, (streams, pairs), 0)
    mixed = []
    for h in range(heads):
        own_col = jnp.sum(
            jnp.where(pair_lane == pair_row + h * streams, own_weight, 0.0), axis=1, keepdims=True
        )
        lanes = slice(h * HEAD_DIM, (h + 1) * HEAD_DIM)
        mixed.append(
            mixed_all[h * streams : (h + 1) * streams, lanes] + own_col * values_new[:, lanes]
        )
    mixed = jnp.concatenate(mixed, axis=1).astype(jnp.bfloat16)
    for copy in columns:
        copy.wait()
    for k in range(count):
        stream.arrived(values_end + 1 + k)
        block = product(mixed, out_buf[k])
        even_side, odd_side = block[:, :width], block[:, width:]
        kept_ref[k] = jnp.where(odd == 1, odd_side, even_side)
        sent = jnp.where(odd == 1, even_side, odd_side).astype(jnp.bfloat16)
        if k == 0:
            last_ref[...] = sent
        else:
            sent_ref[k - 1] = sent


QKV_STEPS = 4
CACHE_STEPS = 2


def temporal_parts(place, hidden_in, gain, lengths, qkv, out_weight, keys, values, head_weight, places):
    codes, head_depth, vocab = head_weight.shape
    streams, depth = hidden_in.shape
    bf16 = jnp.bfloat16
    count, width = places // 2, out_weight.shape[1] // places
    block = (count, streams, width)
    return pl.pallas_call(
        temporal_kernel,
        in_specs=[SMEM] + [HBM] * 8,
        out_specs=[VMEM] * 4,
        out_shape=[
            vmem(block, jnp.float32),
            vmem(block[1:], bf16),
            vmem((count - 1,) + block[1:], bf16),
            vmem((count, codes // 2, head_depth, vocab // places), bf16),
        ],
        scratch_shapes=[
            pltpu.VMEM(hidden_in.shape, bf16),
            pltpu.VMEM((1, depth), jnp.float32),
            pltpu.VMEM((1, streams), jnp.int32),
            pltpu.VMEM(qkv.shape, bf16),
            pltpu.VMEM((count, out_weight.shape[0], 2 * width), bf16),
            pltpu.VMEM(keys.shape, bf16),
            pltpu.VMEM(values.shape, bf16),
            pltpu.SemaphoreType.DMA((3,)),
            pltpu.SemaphoreType.DMA((3 * QKV_STEPS + 2 * CACHE_STEPS + count,)),
            pltpu.SemaphoreType.DMA((count,)),
        ],
        compiler_params=params(30),
        name="temporal",
    )(
        place,
        in_hbm(hidden_in),
        in_hbm(gain.reshape(1, depth)),
        in_hbm(lengths.reshape(1, streams)),
        in_hbm(qkv),
        in_hbm(out_weight),
        in_hbm(keys),
        in_hbm(values),
        in_hbm(head_weight),
    )


def prepare_kernel(
    place_ref, tokens_ref, hidden_hbm, embed_hbm, weight_hbm, resid_ref, embedded_ref, weight_ref, embed_buf, sem, sems
):
    codes, vocab, _ = embed_buf.shape
    streams = tokens_ref.shape[0]
    part = resid_ref.shape[1]
    start = pl.multiple_of(place_ref[0] * part, part)
    resid = pltpu.make_async_copy(hidden_hbm.at[:, pl.ds(start, part)], resid_ref, sem)
    resid.start()
    embed = [pltpu.make_async_copy(embed_hbm.at[c], embed_buf.at[c], sems.at[0, c]) for c in range(codes)]
    weight = [pltpu.make_async_copy(weight_hbm.at[c], weight_ref.at[c], sems.at[1, c]) for c in range(codes)]
    stream = Stream(embed + weight, IN_FLIGHT)
    vocab_lane = lax.broadcasted_iota(jnp.int32, (streams, vocab), 1) + place_ref[0] * vocab
    for c in range(codes):
        hit = tokens_ref[:, c : c + 1] == vocab_lane
        onehot = jnp.where(hit, 1.0, 0.0).astype(jnp.bfloat16)
        stream.arrived(c)
        embedded_ref[c] = product(onehot, embed_buf[c])
    stream.arrived(2 * codes - 1)
    resid.wait()


def prepared_entry(place, tokens, hidden_in, embed, weight, places):
    codes, _, width = weight.shape
    streams = tokens.shape[0]
    resid_shape = (hidden_in.shape[0], hidden_in.shape[1] // places)
    return pl.pallas_call(
        prepare_kernel,
        in_specs=[SMEM, VMEM, HBM, HBM, HBM],
        out_specs=[VMEM] * 3,
        out_shape=[
            vmem(resid_shape, jnp.bfloat16),
            vmem((codes, streams, width), jnp.float32),
            vmem(weight.shape, jnp.bfloat16),
        ],
        scratch_shapes=[
            pltpu.VMEM(embed.shape, jnp.bfloat16),
            pltpu.SemaphoreType.DMA(()),
            pltpu.SemaphoreType.DMA((2, codes)),
        ],
        compiler_params=params(16),
        name="entry_prepare",
    )(place, tokens, in_hbm(hidden_in), in_hbm(embed), in_hbm(weight))


def near_kernel(place_ref, token_ref, gain_ref, qkv_hbm, out_hbm, head_hbm, own_ref, qkv_ref, out_ref, *rest):
    column_refs, (sems, column_sems) = rest[:-2], rest[-2:]
    del token_ref
    copies = [
        pltpu.make_async_copy(source.at[c], target.at[c], sems.at[i, c])
        for i, (source, target) in enumerate(((qkv_hbm, qkv_ref), (out_hbm, out_ref)))
        for c in range(source.shape[0])
    ]
    for n, out in enumerate(column_refs):
        count, codes, _, vocab_part = out.shape
        for k in range(count):
            start = pl.multiple_of(((place_ref[0] // 2 ^ k) * 2 + place_ref[0] % 2) * vocab_part, vocab_part)
            source = head_hbm.at[pl.ds(n * codes, codes), :, pl.ds(start, vocab_part)]
            copies.append(pltpu.make_async_copy(source, out.at[k], column_sems.at[n, k]))
    stream = Stream(copies, IN_FLIGHT)
    part = own_ref.shape[1]
    own_ref[...] = gain_ref[:, pl.ds(pl.multiple_of(place_ref[0] * part, part), part)]
    stream.arrived(len(copies) - 1)


def brought_near(place, token, gain, qkv, out_weight, head_weight, places):
    width = gain.shape[0]
    codes, depth, vocab = head_weight.shape
    columns = vmem((places // 2, codes // CHUNKS, depth, vocab // places), jnp.bfloat16)
    return pl.pallas_call(
        near_kernel,
        in_specs=[SMEM, VMEM, VMEM, HBM, HBM, HBM],
        out_specs=[VMEM] * (3 + CHUNKS),
        out_shape=[
            vmem((1, width // places), jnp.float32),
            vmem(qkv.shape, jnp.bfloat16),
            vmem(out_weight.shape, jnp.bfloat16),
        ]
        + [columns] * CHUNKS,
        scratch_shapes=[
            pltpu.SemaphoreType.DMA((2, qkv.shape[0])),
            pltpu.SemaphoreType.DMA((CHUNKS, places // 2)),
        ],
        compiler_params=params(16),
        name="brought_near",
    )(place, token, gain.reshape(1, width), in_hbm(qkv), in_hbm(out_weight), in_hbm(head_weight))


def entry_kernel(
    place_ref, own_ref, other_ref, embedded_ref, weight_ref, kept_ref, last_ref, sent_ref, token_ref, total_buf
):
    token_ref[...] = jnp.zeros_like(token_ref)
    codes = weight_ref.shape[0]
    count, _, _, part = kept_ref.shape
    odd = place_ref[0] % 2
    place = place_ref[0] // 2
    first_section = place_ref[1] == 0
    own, other = own_ref[...], other_ref[...]
    rows = jnp.concatenate(
        [jnp.where(first_section, own, other), jnp.where(first_section, other, own)], axis=0
    )
    for c in range(codes):
        total_buf[...] = embedded_ref[c] + product(rows, weight_ref[c])
        for k in range(count):
            pair = (place ^ k) * 2
            kept_ref[k, c] = total_buf[:, pl.ds(pl.multiple_of((pair + odd) * part, part), part)]
            sent = total_buf[:, pl.ds(pl.multiple_of((pair + 1 - odd) * part, part), part)].astype(jnp.bfloat16)
            if k == 0:
                last_ref[c] = sent
            else:
                sent_ref[k - 1, c] = sent


def entry_parts(place, own, other, embedded, weight, places):
    codes, _, width = weight.shape
    streams = 2 * own.shape[0]
    block = (places // 2, codes, streams, width // places)
    return pl.pallas_call(
        entry_kernel,
        in_specs=[SMEM] + [VMEM] * 4,
        out_specs=[VMEM] * 4,
        out_shape=[
            vmem(block, jnp.float32),
            vmem(block[1:], jnp.bfloat16),
            vmem((places // 2 - 1,) + block[1:], jnp.bfloat16),
            vmem((8, 128), jnp.float32),
        ],
        scratch_shapes=[pltpu.VMEM((streams, width), jnp.float32)],
        compiler_params=params(16),
        name="entry",
    )(place, own, other, embedded, weight)


def nearest_last(far):
    return list(range(1, far)) + [0]


def qkv_kernel(count, place_ref, gain_ref, weight_ref, far_ref, *rest):
    near_refs, (last_ref, queries_ref, pair_ref) = rest[:count], rest[count:]
    codes, _, width, cols = weight_ref.shape
    part = last_ref.shape[2]
    odd = place_ref[0] % 2
    place = place_ref[0] // 2
    order = [0] + [k + 1 for k in nearest_last(count - 1)]
    starts = [pl.multiple_of(((place ^ k) * 2 + side) * part, part) for side in (odd, 1 - odd) for k in order]
    inverse_gain = 1.0 / jnp.concatenate([gain_ref[:, pl.ds(start, part)] for start in starts], axis=1)
    for c in range(codes):
        blocks = [ref[c] for ref in near_refs] + [last_ref[c]] + [far_ref[k, c] for k in range(count - 1)]
        row = jnp.concatenate(blocks, axis=1)
        plain = row.astype(jnp.float32) * inverse_gain
        inv = lax.rsqrt(jnp.sum(plain * plain, axis=1, keepdims=True) / width + EPSILON)
        for n in range(3):
            weight = jnp.concatenate([weight_ref[c, n, pl.ds(start, part), :] for start in starts], axis=0)
            value = (product(row, weight) * inv).astype(jnp.bfloat16)
            if n == 0:
                queries_ref[c] = value
            else:
                pair_ref[n - 1, c] = value


def depth_projections(place, near, last, far, gain, weight):
    codes, _, width, cols = weight.shape
    streams = last.shape[1]
    bf16 = jnp.bfloat16
    return pl.pallas_call(
        functools.partial(qkv_kernel, len(near)),
        in_specs=[SMEM] + [VMEM] * (4 + len(near)),
        out_specs=[VMEM] * 2,
        out_shape=[vmem((codes, streams, cols), bf16), vmem((2, codes, streams, cols), bf16)],
        compiler_params=params(16),
        name="depth_qkv",
    )(place, gain.reshape(1, width), weight, far, *near, last)


def mix_kernel(terms, place_ref, queries_ref, own_ref, prior_ref, weight_ref, *rest):
    entry_refs, outs, total_buf = rest[:terms], rest[terms:-1], rest[-1]
    codes, streams, cols = queries_ref.shape
    each, _, span = outs[0].shape
    count = len(outs) // CHUNKS
    has_prior = place_ref[1] > 0
    first = lax.broadcasted_iota(jnp.int32, (2 * cols, cols), 0) % cols
    second = lax.broadcasted_iota(jnp.int32, (2 * cols, cols), 1)
    same = jnp.where(first // DEPTH_HDIM == second // DEPTH_HDIM, 1.0, 0.0).astype(jnp.bfloat16)
    keys = [prior_ref[0, j].astype(jnp.float32) for j in range(codes)]
    keys += [own_ref[0, j].astype(jnp.float32) for j in range(codes)]
    values = [prior_ref[1, j].astype(jnp.float32) for j in range(codes)]
    values += [own_ref[1, j].astype(jnp.float32) for j in range(codes)]
    factor = 1.0 / math.sqrt(DEPTH_HDIM)
    mixed = []
    for q in range(codes):
        query = queries_ref[q].astype(jnp.float32)
        reach = codes + q + 1
        pieces = []
        for j in range(reach):
            exact = query * keys[j]
            high = exact.astype(jnp.bfloat16)
            low = (exact - high.astype(jnp.float32)).astype(jnp.bfloat16)
            pieces.append(jnp.concatenate([high, low], axis=1))
        scores = product(jnp.concatenate(pieces, axis=0), same) * factor
        score = [scores[j * streams : (j + 1) * streams] for j in range(reach)]
        score = [jnp.where(has_prior, s, -jnp.inf) if j < codes else s for j, s in enumerate(score)]
        top = score[0]
        for s in score[1:]:
            top = jnp.maximum(top, s)
        expo = [jnp.exp(s - top) for s in score]
        inverse = 1.0 / sum(expo)
        total = jnp.zeros_like(query)
        for j in range(reach):
            total = total + (expo[j] * inverse).astype(jnp.bfloat16).astype(jnp.float32) * values[j]
        mixed.append(total.astype(jnp.bfloat16))
    for q in range(codes):
        total_buf[q] = product(mixed[q], weight_ref[q])
    part = entry_refs[0].shape[2]
    own_part = pl.ds(pl.multiple_of(place_ref[0] * part, part), part)
    total_buf[:, :, own_part] += sum(ref[...].astype(jnp.float32) for ref in entry_refs)
    place = place_ref[0] // 2
    for n, out in enumerate(outs):
        chunk, k = divmod(n, count)
        start = pl.multiple_of((place ^ k) * span, span)
        block = total_buf[pl.ds(chunk * each, each), :, pl.ds(start, span)]
        out[...] = block if k == 0 else block.astype(jnp.bfloat16)


def mixed_parts(place, queries, own, prior, weight, entry_terms, far):
    codes, streams, cols = queries.shape
    width = weight.shape[2]
    block = (codes // CHUNKS, streams, width // (far + 1))
    outs = pl.pallas_call(
        functools.partial(mix_kernel, len(entry_terms)),
        in_specs=[SMEM] + [VMEM] * (4 + len(entry_terms)),
        out_specs=[VMEM] * ((far + 1) * CHUNKS),
        out_shape=([vmem(block, jnp.float32)] + [vmem(block, jnp.bfloat16)] * far) * CHUNKS,
        scratch_shapes=[pltpu.VMEM((codes, streams, width), jnp.float32)],
        compiler_params=params(16),
        name="depth_mix",
    )(place, queries, own, prior, weight, *entry_terms)
    return [outs[n * (far + 1) : (n + 1) * (far + 1)] for n in range(CHUNKS)]


STAT_ROWS = 16


def head_kernel(
    first, place_ref, gain_ref, total_ref, arrived_ref, weight_ref, early_ref, late_ref, kept_ref, stat_ref, *sends
):
    half = early_ref.shape[1]

    def partner(k, c):
        side, index = divmod(first + c, half)
        return jnp.where(place_ref[2] == side, early_ref[k, index], late_ref[k, index])

    codes, streams, span = total_ref.shape
    count, _, depth, part = weight_ref.shape
    odd = place_ref[0] % 2
    resid = total_ref[...] + arrived_ref[...].astype(jnp.float32)
    flat = resid.reshape(codes * streams, span)
    squares = flat * flat
    stat = product_t(jnp.ones((STAT_ROWS // 2, span), jnp.float32), squares)[:1]
    stat_ref[...] = stat
    high = stat.astype(jnp.bfloat16).astype(jnp.float32)
    stat_row = lax.broadcasted_iota(jnp.int32, (STAT_ROWS, codes * streams), 0)
    stat_block = jnp.where(stat_row == 0, high, jnp.where(stat_row == 1, stat - high, 0.0))
    if part > codes * streams:
        rest = jnp.zeros((STAT_ROWS, part - codes * streams), jnp.float32)
        stat_block = jnp.concatenate([stat_block, rest], axis=1)
    stat_block = stat_block.astype(jnp.bfloat16)
    scaled = resid * gain_ref[...]
    low_half, high_half = scaled[:, :, :depth], scaled[:, :, depth:]
    ordered = jnp.concatenate(
        [jnp.where(odd == 1, high_half, low_half), jnp.where(odd == 1, low_half, high_half)], axis=2
    ).astype(jnp.bfloat16)
    rows = codes * streams
    for k in range(count):
        block = jnp.concatenate(
            [
                product(ordered[c], jnp.concatenate([weight_ref[k, c], partner(k, c)], axis=0))
                for c in range(codes)
            ],
            axis=0,
        )
        if k == 0:
            kept_ref[...] = block
        else:
            sends[k - 1][pl.ds(0, rows), :] = block.astype(jnp.bfloat16)
            sends[k - 1][pl.ds(rows, STAT_ROWS), :] = stat_block


def head_parts(first, place, gain, total, arrived, weight, early, late):
    codes, streams, span = total.shape
    count, _, depth, part = weight.shape
    rows = codes * streams
    return pl.pallas_call(
        functools.partial(head_kernel, first),
        in_specs=[SMEM] + [VMEM] * 6,
        out_specs=[VMEM] * (count + 1),
        out_shape=[vmem((rows, part), jnp.float32), vmem((1, rows), jnp.float32)]
        + [vmem((rows + STAT_ROWS, part), jnp.bfloat16)] * (count - 1),
        compiler_params=params(16),
        name="head",
    )(place, gain, total, arrived, weight, early, late)


def logits_kernel(width, *refs):
    out_ref = refs[-1]
    streams, codes, part = out_ref.shape
    each = codes // CHUNKS
    rows = each * streams
    count = (len(refs) - 1) // CHUNKS
    for n in range(CHUNKS):
        kept_ref, stat_ref, *arrived = refs[n * count : (n + 1) * count]
        total = kept_ref[...]
        stat = stat_ref[...]
        for block in arrived:
            wide = block[...].astype(jnp.float32)
            total = total + wide[:rows]
            stat = stat + wide[rows : rows + 1, :rows] + wide[rows + 1 : rows + 2, :rows]
        total = total * column_of(lax.rsqrt(stat / width + EPSILON))
        for c in range(each):
            out_ref[:, n * each + c, :] = total[c * streams : (c + 1) * streams]


def finished_logits(chunks, streams, codes, width):
    part = chunks[0][0].shape[1]
    arrays = [array for chunk in chunks for array in chunk]
    return pl.pallas_call(
        functools.partial(logits_kernel, width),
        in_specs=[VMEM] * len(arrays),
        out_specs=VMEM,
        out_shape=shape((streams, codes, part), jnp.float32),
        compiler_params=params(16),
        name="logits",
    )(*arrays)


def paired_device(
    hidden_in,
    temporal_gain,
    temporal_qkv,
    temporal_out_weight,
    cache_keys,
    cache_values,
    lengths,
    depth_in,
    depth_embed,
    depth_gain,
    depth_qkv,
    depth_out_weight,
    head_gain,
    head_weight,
    tokens,
):
    tp = lax.axis_size("tp")
    tp_place = lax.axis_index("tp")
    place = jnp.stack([tp_place, lax.axis_index("section"), lax.axis_index("grp") % 2])
    far = tp // 2 - 1

    def to_pairs(blocks):
        arrived = [None] * len(blocks)
        for k in reversed(range(len(blocks))):
            arrived[k] = lax.ppermute(blocks[k], "tp", [(i, i ^ 2 * (k + 1)) for i in range(tp)])
        return arrived

    order = nearest_last(far)

    def in_order(blocks, order):
        return [blocks[k] for k in order]

    def to_neighbour(block):
        return lax.ppermute(block, "tp", [(i, i ^ 1) for i in range(tp)])

    def summed(kept, last, sent, order):
        folded = kept[1:] + to_neighbour(sent).astype(jnp.float32)
        arrived = to_pairs([folded[k].astype(jnp.bfloat16) for k in range(far)])
        return [kept[0]] + [arrived[k] for k in order] + [to_neighbour(last)]

    def added(terms):
        return sum(term.astype(jnp.float32) for term in terms)

    kept, last, sent, neighbour_columns = temporal_parts(
        place,
        hidden_in,
        temporal_gain,
        lengths,
        temporal_qkv,
        temporal_out_weight,
        cache_keys,
        cache_values,
        head_weight,
        tp,
    )
    sent, depth_in = lax.optimization_barrier((sent, depth_in))
    early = to_neighbour(neighbour_columns)
    resid_in, embedded, near_in = prepared_entry(place, tokens, hidden_in, depth_embed, depth_in, tp)
    temporal = (resid_in.astype(jnp.float32) + added(summed(kept, last, sent, order))).astype(jnp.bfloat16)
    other_rows = lax.ppermute(temporal, "section", [(0, 1), (1, 0)])
    codes = depth_in.shape[0]
    width = depth_in.shape[2]
    hidden_rows = head_weight.shape[1]
    kept, last, sent, token = entry_parts(place, temporal, other_rows, embedded, near_in, tp)
    sent, early = lax.optimization_barrier((sent, early))
    late = lax.ppermute(early, "grp", [(i, i ^ 1) for i in range(lax.axis_size("grp"))])
    own_gain, near_qkv, near_out, *own_columns = brought_near(
        place, token, depth_gain, depth_qkv, depth_out_weight, head_weight, tp
    )
    entry_terms = summed(kept, last, sent, list(range(far)))
    scaled = (added(entry_terms) * own_gain[None]).astype(jnp.bfloat16)
    near = [scaled] + in_order(to_pairs([scaled] * far), order)
    last = to_neighbour(scaled)
    queries, own_pair = depth_projections(
        place, near, last, to_neighbour(jnp.stack(near[1:])), depth_gain, near_qkv
    )
    prior_pair = passed_along(own_pair, "section", 1)
    chunks = mixed_parts(place, queries, own_pair, prior_pair, near_out, entry_terms, far)
    pair_gain = lax.dynamic_slice_in_dim(head_gain, tp_place // 2 * 2 * hidden_rows, 2 * hidden_rows, 0)
    each = codes // CHUNKS
    arrived = [in_order(to_pairs(blocks), order) for _, *blocks in chunks]
    totals = [
        kept + added(blocks) for (kept, *_), blocks in zip(chunks, arrived)
    ]
    others = [to_neighbour(total.astype(jnp.bfloat16)) for total in totals]
    heads = [
        head_parts(n * each, place, pair_gain.reshape(1, 1, -1), total, other, own, early, late)
        for n, (total, other, own) in enumerate(zip(totals, others, own_columns))
    ]
    finished = [[kept, stat, *in_order(to_pairs(blocks), order)] for kept, stat, *blocks in heads]
    logits = finished_logits(finished, sent.shape[2], codes, width)
    return (temporal, logits)


def per_device(*arrays):
    hidden_in, temporal_qkv, depth_qkv, head_weight = arrays[0], arrays[2], arrays[10], arrays[13]
    depth_in, tokens = arrays[7], arrays[14]
    tp = lax.axis_size("tp")
    pairs = hidden_in.shape[0] * (temporal_qkv.shape[2] // HEAD_DIM)
    whole_tiles = (
        pairs % 128 == 0
        and temporal_qkv.shape[2] % HEAD_DIM == 0
        and head_weight.shape[1] % 128 == 0
        and head_weight.shape[2] // tp % 128 == 0
        and depth_qkv.shape[3] % 128 == 0
        and tp >= 4
        and depth_in.shape[0] % (2 * CHUNKS) == 0
        and lax.axis_size("grp") % 2 == 0
        and depth_in.shape[0] // CHUNKS * tokens.shape[0] <= head_weight.shape[2] // tp
        and tp & (tp - 1) == 0
    )
    return (paired_device if whole_tiles else general_device)(*arrays)


def solution(mesh):
    return jax.shard_map(
        per_device,
        mesh=mesh,
        in_specs=(
            P(("grp", "section"), None),
            P(),
            P(None, None, "tp"),
            P("tp", None),
            P(("grp", "section"), None, "tp"),
            P(("grp", "section"), None, "tp"),
            P(("grp", "section")),
            P("section", "tp", None),
            P("section", "tp", None),
            P(),
            P("section", None, None, "tp"),
            P("section", "tp", None),
            P(),
            P("section", "tp", None),
            P("grp", "section"),
        ),
        out_specs=(P(("grp", "section"), "tp"), P("grp", "section", "tp")),
        check_vma=False,
    )
```
